32 devices in a mesh: dp: 4 (over y, x), seq: 8 (over z, core).
Axes of the slice: x: 2, y: 2, z: 4, core: 2. Of those that a mesh axis runs over, the one named last changes fastest.
Arguments:
- tokens: bfloat16 [4096, 1600], P(('dp', 'seq')), may hold values from -6 to 6
- w_qkv: bfloat16 [1600, 4800], P('dp', 'seq'), may hold values from -0.15625 to 0.15625
- w_out: bfloat16 [1600, 1600], P('dp', 'seq'), may hold values from -0.625 to 0.625
- vectors: bfloat16 [8, 1600], P('dp', 'seq'), may hold values from -1.2 to 1.4, as said below
- w_fc: bfloat16 [1600, 6400], P('dp', 'seq'), may hold values from -0.15625 to 0.15625
- b_fc: bfloat16 [6400], P(('dp', 'seq')), may hold values from -2 to 2
- w_proj: bfloat16 [6400, 1600], P('dp', 'seq'), may hold values from -0.078125 to 0.078125
- cotangent: bfloat16 [4096, 1600], P(('dp', 'seq')), may hold values from -6 to 6
Outputs:
- activations: bfloat16 [4096, 1600], P(('dp', 'seq'))
- input_grad: bfloat16 [4096, 1600], P(('dp', 'seq'))
- grad_w_qkv: float32 [1600, 4800], P('dp', 'seq')
- grad_w_out: float32 [1600, 1600], P('dp', 'seq')
- grad_vectors: float32 [8, 1600], P('dp', 'seq')
- grad_w_fc: float32 [1600, 6400], P('dp', 'seq')
- grad_b_fc: float32 [6400], P(('dp', 'seq'))
- grad_w_proj: float32 [6400, 1600], P('dp', 'seq')
The draws below stay inside these ranges and needn't reach their ends.
Inputs may be any that keep to these rules, and one draw needn't show every extreme that they name: `vectors`: rows 0 and 5 (the gains) lie in 0.6 to 1.4; the other rows in -1.2 to 1.2.
All inputs are finite; a program needn't handle non-finite values.
Results may differ from the reference program's by a relative error of at most 0.013.
Values may be sent and summed in bfloat16 or wider, within the bound.
No kernel may reach another device: no remote copies, remote signals or barrier semaphores. Data moves between devices by JAX's collectives and lax.ppermute only.
A program may use at most 512 MiB of HBM per device.

```python
import math
import jax
import jax.numpy as jnp
from jax import lax

D = 1600
HD = 64
FF = 6400
SEQ_LEN = 1024
SEQS = 4
TOKENS = 4096


def draw_vectors(key, part):
    key = jax.random.fold_in(key, 7)
    key_base, key_gain = jax.random.split(key)
    base_rows = jnp.clip(0.3 * jax.random.normal(key_base, (8, D), jnp.float32), -1.2, 1.2)
    gain_rows = jax.random.uniform(key_gain, (8, D), jnp.float32, 0.6, 1.4)
    row_index = jnp.arange(8)[:, None]
    is_gain = (row_index == 0) | (row_index == 5)
    return jnp.where(is_gain, gain_rows, base_rows).astype(jnp.bfloat16)


def shard_levels(own_key, extent, cuts, low, high):
    def one(dim, blocks):
        heights = jax.random.uniform(jax.random.fold_in(jax.random.fold_in(own_key, 6), dim), (blocks,), jnp.float32, low / len(cuts), high / len(cuts))
        return jnp.repeat(jnp.exp(heights), extent[dim] // blocks).reshape((-1,) + (1,) * (len(extent) - dim - 1))

    level = one(*cuts[0])
    for cut in cuts[1:]:
        level = level * one(*cut)
    return level


def bell_draw(rng, extent, spread, most, cuts=(), kind=jnp.bfloat16):
    entries = jax.random.normal(rng, extent, jnp.float32) * spread
    if len(cuts) > 0:
        entries = shard_levels(rng, extent, cuts, -0.22, 0.18) * entries
    return jnp.clip(entries, min=-most, max=most).astype(kind)


def setup_inputs(seed: int = 0) -> dict:
    key_list = jax.random.split(jax.random.key(seed), 9)
    return {
        "tokens": bell_draw(key_list[0], (TOKENS, D), 1.0, 6.0, ((0, 32),)),
        "w_qkv": bell_draw(key_list[1], (D, 3 * D), D ** -0.5, 0.15625, ((0, 4), (1, 8))),
        "w_out": bell_draw(key_list[2], (D, D), (D // 16) ** -0.5, 0.625, ((0, 4), (1, 8))),
        "vectors": draw_vectors(jax.random.fold_in(key_list[8], 71), 0),
        "w_fc": bell_draw(key_list[4], (D, FF), D ** -0.5, 0.15625, ((0, 4), (1, 8))),
        "b_fc": bell_draw(key_list[5], (FF,), 0.3, 2.0, ((0, 32),)),
        "w_proj": bell_draw(key_list[6], (FF, D), FF ** -0.5, 0.078125, ((0, 4), (1, 8))),
        "cotangent": bell_draw(key_list[7], (TOKENS, D), 1.0, 6.0, ((0, 32),)),
    }


@jax.custom_vjp
def low(v):
    return lax.optimization_barrier(v.astype(jnp.bfloat16)).astype(jnp.float32)

@jax.custom_vjp
def low_back(v):
    return v

def low_keep(v):
    return (low(v), None)

def low_pass(kept, grad):
    return (grad,)

def back_keep(v):
    return (v, None)

def back_low(kept, grad):
    return (low(grad),)
low.defvjp(low_keep, low_pass)
low_back.defvjp(back_keep, back_low)
EPSILON = 1e-05
GELU_C = 0.7978845608028654
NEG_FILL = -1e+30

def layer_norm(features, scale_row, shift_row):
    row_mean = lax.optimization_barrier(jnp.mean(features, axis=-1, keepdims=True))
    centred = features - row_mean
    variance = lax.optimization_barrier(jnp.mean(centred * centred, axis=-1, keepdims=True))
    return centred * lax.rsqrt(variance + EPSILON) * scale_row + shift_row

def gelu_tanh(pre_act):
    return 0.5 * pre_act * (1.0 + jnp.tanh(GELU_C * (pre_act + 0.044715 * pre_act * pre_act * pre_act)))

def matmul(operand, weights):
    return jnp.dot(operand, weights, preferred_element_type=jnp.float32, precision=lax.Precision.HIGHEST)

def attend(queries, key_rows, value_rows):
    seq_length = queries.shape[0]
    block_rows = math.gcd(seq_length, 512)
    head_count = queries.shape[1] // HD
    query_blocks = queries.reshape(seq_length // block_rows, block_rows, head_count, HD)
    key_heads = key_rows.reshape(seq_length, head_count, HD)
    value_heads = value_rows.reshape(seq_length, head_count, HD)
    block_starts = jnp.arange(seq_length // block_rows, dtype=jnp.int32) * block_rows
    positions = jnp.arange(seq_length, dtype=jnp.int32)
    score_scale = 1.0 / math.sqrt(HD)

    def one_block(operands):
        query_block, block_start = operands
        raw_scores = jnp.einsum('qhd,khd->hqk', query_block, key_heads, precision=lax.Precision.HIGHEST)
        scores = low_back(raw_scores * score_scale)
        query_pos = block_start + jnp.arange(block_rows, dtype=jnp.int32)
        allowed = positions[None, :] <= query_pos[:, None]
        scores = jnp.where(allowed[None], scores, NEG_FILL)
        row_max = lax.optimization_barrier(jnp.max(scores, axis=-1, keepdims=True))
        unnormed = jnp.exp(scores - row_max)
        weights = unnormed / lax.optimization_barrier(jnp.sum(unnormed, axis=-1, keepdims=True))
        return jnp.einsum('hqk,khd->qhd', low(weights), value_heads, precision=lax.Precision.HIGHEST)
    blocks_out = lax.map(jax.checkpoint(one_block), (query_blocks, block_starts))
    return blocks_out.reshape(seq_length, head_count * HD)

def forward(features, w_qkv, w_out, vectors, w_fc, b_fc, w_proj):
    model_width = features.shape[1]
    normed = low(layer_norm(features, vectors[0], vectors[1]))
    projected = matmul(normed, w_qkv)
    queries = low(low_back(projected[:, :model_width] + vectors[2]))
    key_rows = low(low_back(projected[:, model_width:2 * model_width]))
    value_rows = low(low_back(projected[:, 2 * model_width:] + vectors[3]))
    attended = low(low_back(attend(queries, key_rows, value_rows)))
    middle = features + low_back(matmul(attended, w_out) + vectors[4])
    normed_two = low(layer_norm(middle, vectors[5], vectors[6]))
    pre_act = low_back(matmul(normed_two, w_fc) + b_fc)
    hidden = low(gelu_tanh(pre_act))
    return middle + low_back(matmul(hidden, w_proj) + vectors[7])

def reference(tokens, w_qkv, w_out, vectors, w_fc, b_fc, w_proj, cotangent):
    params = (w_qkv.astype(jnp.float32), w_out.astype(jnp.float32), vectors.astype(jnp.float32), w_fc.astype(jnp.float32), b_fc.astype(jnp.float32), w_proj.astype(jnp.float32))
    inputs = tokens.astype(jnp.float32).reshape(SEQS, SEQ_LEN, D)
    cot_rows = cotangent.astype(jnp.float32).reshape(SEQS, SEQ_LEN, D)

    def one_sequence(totals, operands):
        seq_rows, seq_cot = operands
        result, pullback = jax.vjp(forward, seq_rows, *params)
        grads = pullback(seq_cot)
        totals = tuple((summed + fresh for summed, fresh in zip(totals, grads[1:])))
        return (totals, (result, grads[0]))
    initial = tuple((jnp.zeros_like(param) for param in params))
    totals, (results, in_grads) = lax.scan(one_sequence, initial, (inputs, cot_rows))
    return (results.reshape(TOKENS, D).astype(jnp.bfloat16), in_grads.reshape(TOKENS, D).astype(jnp.bfloat16), totals[0], totals[1], totals[2], totals[3], totals[4], totals[5])
```

```python
import functools
import math

import jax
import jax.numpy as jnp
import numpy as np
from jax import lax
from jax.experimental import pallas as pl
from jax.experimental.pallas import tpu as pltpu
from jax.sharding import PartitionSpec as P

HD = 64
PAIR = 2 * HD
EPSILON = 1e-05
GELU_C = 0.7978845608028654
NEG_FILL = -1e30
BF = jnp.bfloat16
F32 = jnp.float32


def head_plan(head_count, seq_count, width):
    slots = -(-head_count // seq_count)
    slots += slots % 2
    model = head_count * HD

    def tables(turn):
        owner = np.full((seq_count, slots), -1, np.int32)
        for head in range(head_count):
            row = head // seq_count
            owner[(head + turn * row) % seq_count, row] = head
        place = {}
        for dev in range(seq_count):
            for slot in range(slots):
                if owner[dev, slot] >= 0:
                    place[int(owner[dev, slot])] = (dev, slot)
        lists = [[[] for _ in range(seq_count)] for _ in range(seq_count)]
        for col in range(3 * model):
            kind, rest = divmod(col, model)
            head, lane = divmod(rest, HD)
            dev, slot = place[head]
            src, local = divmod(col, width)
            lists[src][dev].append((local, (kind * slots + slot) * HD + lane))
        most = max(len(cell) for row in lists for cell in row)
        return most, owner, lists

    best = min((tables(turn) for turn in range(seq_count)), key=lambda t: t[0])
    most, owner, lists = best
    wide = -(-most // 128) * 128
    send = np.full((seq_count, seq_count, wide), -1, np.int32)
    recv = np.full((seq_count, seq_count, wide), -1, np.int32)
    for src in range(seq_count):
        for dev in range(seq_count):
            for i, (local, target) in enumerate(lists[src][dev]):
                send[src, dev, i] = local
                recv[src, dev, i] = target
    return slots, owner, wide, send, recv


def xor_perm(count, k):
    return [(i, i ^ k) for i in range(count)]


def gather_rel(block, axis):
    count = lax.axis_size(axis)
    return [block] + [lax.ppermute(block, axis, xor_perm(count, k)) for k in range(1, count)]


def scatter_rel(chunks, axis):
    count = lax.axis_size(axis)
    total = chunks[0].astype(F32)
    for k in range(1, count):
        total = total + lax.ppermute(chunks[k], axis, xor_perm(count, k)).astype(F32)
    return total


def gather_small(block, axis):
    count = lax.axis_size(axis)
    me = lax.axis_index(axis)
    stack = block[None]
    step = 1
    while step < count:
        other = lax.ppermute(stack, axis, xor_perm(count, step))
        low = (me & step) == 0
        stack = jnp.where(
            low, jnp.concatenate([stack, other]), jnp.concatenate([other, stack])
        )
        step *= 2
    return stack


def swap_blocks(matrix, count, me):
    size = matrix.shape[1] // count
    return jnp.concatenate(
        [lax.dynamic_slice_in_dim(matrix, (me ^ k) * size, size, axis=1) for k in range(count)],
        axis=1,
    )


def normalise(rows):
    mean = jnp.mean(rows, axis=-1, keepdims=True)
    centred = rows - mean
    inverse = lax.rsqrt(jnp.mean(centred * centred, axis=-1, keepdims=True) + EPSILON)
    return centred * inverse, inverse


def norm_back(grad, unit, inverse, gain):
    scaled = grad * gain
    return (
        scaled
        - jnp.mean(scaled, axis=-1, keepdims=True)
        - unit * jnp.mean(scaled * unit, axis=-1, keepdims=True)
    ) * inverse


def gelu_parts(u):
    cube = u * u * u
    t = jnp.tanh(GELU_C * (u + 0.044715 * cube))
    value = 0.5 * u * (1.0 + t)
    slope = 0.5 * (1.0 + t) + 0.5 * u * (1.0 - t * t) * GELU_C * (1.0 + 3 * 0.044715 * u * u)
    return value, slope


def mm(a, b):
    return jnp.dot(a, b, preferred_element_type=F32)


def mm_nt(a, b):
    return lax.dot_general(a, b, (((1,), (1,)), ((), ())), preferred_element_type=F32)


def mm_tn(a, b):
    return lax.dot_general(a, b, (((0,), (0,)), ((), ())), preferred_element_type=F32)


def block_rows(length):
    return math.gcd(length, 256)


def attend_kernel(q_ref, k_ref, v_ref, o_ref, lse_ref):
    length = q_ref.shape[0]
    rows = block_rows(length)
    first = lax.broadcasted_iota(jnp.int32, (rows, PAIR), 1) < HD
    causal = lax.broadcasted_iota(jnp.int32, (rows, rows), 0) >= lax.broadcasted_iota(
        jnp.int32, (rows, rows), 1
    )
    for i in range(length // rows):
        here = pl.ds(i * rows, rows)
        seen = (i + 1) * rows
        q = q_ref[here, :] * BF(1.0 / math.sqrt(HD))
        keys = k_ref[0:seen, :]
        values = v_ref[0:seen, :]
        outs, logs = [], []
        for mine in (first, ~first):
            s = mm_nt(jnp.where(mine, q, BF(0)), keys)
            tail = jnp.where(causal, s[:, seen - rows :], NEG_FILL)
            s = tail if i == 0 else jnp.concatenate([s[:, : seen - rows], tail], axis=1)
            top = jnp.max(s, axis=-1, keepdims=True)
            e = jnp.exp(s - top)
            total = jnp.sum(e, axis=-1, keepdims=True)
            outs.append(mm(e.astype(BF), values) / total)
            logs.append(top + jnp.log(total))
        o_ref[here, :] = jnp.where(first, outs[0], outs[1]).astype(BF)
        lse_ref[here, :] = jnp.where(first, logs[0], logs[1])


def attend(qkv, slots):
    length = qkv.shape[0]
    pairs = slots * HD // PAIR
    spec = lambda shift: pl.BlockSpec((length, PAIR), lambda g: (0, g + shift))
    return pl.pallas_call(
        attend_kernel,
        grid=(pairs,),
        in_specs=[spec(0), spec(pairs), spec(2 * pairs)],
        out_specs=[spec(0), spec(0)],
        out_shape=[
            jax.ShapeDtypeStruct((length, slots * HD), BF),
            jax.ShapeDtypeStruct((length, slots * HD), F32),
        ],
        compiler_params=pltpu.CompilerParams(vmem_limit_bytes=48 * 1024 * 1024),
    )(qkv, qkv, qkv)


def attend_back_kernel(q_ref, k_ref, v_ref, ga_ref, lse_ref, gq_ref, gk_ref, gv_ref, ak, av):
    length = q_ref.shape[0]
    rows = block_rows(length)
    first = lax.broadcasted_iota(jnp.int32, (rows, PAIR), 1) < HD
    causal = lax.broadcasted_iota(jnp.int32, (rows, rows), 0) >= lax.broadcasted_iota(
        jnp.int32, (rows, rows), 1
    )
    ak[...] = jnp.zeros_like(ak)
    av[...] = jnp.zeros_like(av)
    for i in range(length // rows):
        here = pl.ds(i * rows, rows)
        seen = (i + 1) * rows
        q = q_ref[here, :] * BF(1.0 / math.sqrt(HD))
        ga = ga_ref[here, :]
        keys = k_ref[0:seen, :]
        values = v_ref[0:seen, :]
        grads = []
        for h, mine in enumerate((first, ~first)):
            q_h = jnp.where(mine, q, BF(0))
            ga_h = jnp.where(mine, ga, BF(0))
            s = mm_nt(q_h, keys)
            tail = jnp.where(causal, s[:, seen - rows :], NEG_FILL)
            s = tail if i == 0 else jnp.concatenate([s[:, : seen - rows], tail], axis=1)
            p = jnp.exp(s - lse_ref[here, h * HD : h * HD + 1])
            gp = mm_nt(ga_h, values)
            centre = jnp.sum(p * gp, axis=-1, keepdims=True)
            gs = (p * (gp - centre)).astype(BF)
            av[0:seen, :] += mm_tn(p.astype(BF), ga_h)
            ak[0:seen, :] += mm_tn(gs, q_h)
            grads.append(mm(gs, keys))
        gq_ref[here, :] = (jnp.where(first, grads[0], grads[1]) * (1.0 / math.sqrt(HD))).astype(BF)
    gk_ref[...] = ak[...].astype(BF)
    gv_ref[...] = av[...].astype(BF)


def attend_back(qkv, grad, lse, slots):
    length = qkv.shape[0]
    pairs = slots * HD // PAIR
    spec = lambda shift: pl.BlockSpec((length, PAIR), lambda g: (0, g + shift))
    shape = jax.ShapeDtypeStruct((length, slots * HD), BF)
    return pl.pallas_call(
        attend_back_kernel,
        grid=(pairs,),
        in_specs=[spec(0), spec(pairs), spec(2 * pairs), spec(0), spec(0)],
        out_specs=[spec(0), spec(0), spec(0)],
        out_shape=[shape, shape, shape],
        scratch_shapes=[pltpu.VMEM((length, PAIR), F32), pltpu.VMEM((length, PAIR), F32)],
        compiler_params=pltpu.CompilerParams(vmem_limit_bytes=48 * 1024 * 1024),
    )(qkv, qkv, qkv, grad, lse)


def body(tokens, w_qkv, w_out, vectors, w_fc, b_fc, w_proj, cotangent):
    dps = lax.axis_size("dp")
    seqs = lax.axis_size("seq")
    dp = lax.axis_index("dp")
    sq = lax.axis_index("seq")
    rows, model = tokens.shape
    head_count = model // HD
    slots, owner, wide, send, recv = head_plan(head_count, seqs, w_qkv.shape[1])
    mine = slots * HD
    ff_mine = w_fc.shape[1]
    ff_part = ff_mine // dps
    ratio = seqs // dps
    col = w_proj.shape[1]
    order = np.concatenate([owner[d] for d in range(seqs)])

    per, wide_vec = vectors.shape
    small = gather_small(jnp.concatenate([vectors.reshape(-1), b_fc])[None], "dp")
    small = gather_small(small, "seq").astype(F32)[:, :, 0]
    table = small[:, :, : per * wide_vec].reshape(seqs, dps, per, wide_vec)
    table = table.transpose(1, 2, 0, 3).reshape(dps * per, model)
    gain1, shift1, bias_q, bias_v, bias_o, gain2, shift2, bias_p = [table[i] for i in range(8)]
    bias_fc = small[:, :, per * wide_vec :].transpose(1, 0, 2).reshape(-1)
    bias_fc = lax.dynamic_slice_in_dim(bias_fc, sq * ff_mine, ff_mine)
    own_heads = jnp.asarray(owner)[sq]
    pick = (own_heads[:, None] == jnp.arange(head_count)[None, :]).astype(F32)

    def head_rows(vector):
        return jnp.sum(pick[:, :, None] * vector.reshape(1, head_count, HD), axis=1).reshape(-1)

    def head_spread(vector):
        return jnp.sum(pick[:, :, None] * vector.reshape(slots, 1, HD), axis=0).reshape(-1)

    bias_qkv = jnp.concatenate([head_rows(bias_q), jnp.zeros((mine,), F32), head_rows(bias_v)])

    to_send = (jnp.arange(w_qkv.shape[1])[:, None, None] == jnp.asarray(send)[sq][None]).astype(BF)
    to_recv = (
        lax.dynamic_index_in_dim(jnp.asarray(recv), sq, 1, keepdims=False)[:, :, None]
        == jnp.arange(3 * mine)[None, None]
    ).astype(BF)
    parts = jnp.einsum("ac,cnw->naw", w_qkv, to_send, preferred_element_type=F32).astype(BF)
    parts = lax.all_to_all(parts, "seq", 0, 0, tiled=True)
    own_qkv = jnp.einsum("naw,nwd->ad", parts, to_recv, preferred_element_type=F32).astype(BF)
    wq = jnp.concatenate(gather_rel(own_qkv, "dp"), axis=0)
    wf = jnp.concatenate(gather_rel(w_fc, "dp"), axis=0)

    pieces = w_proj.reshape(ratio, dps, ff_part, col)
    pieces = lax.all_to_all(pieces.transpose(1, 0, 2, 3), "dp", 0, 0, tiled=True)
    pieces = lax.all_to_all(pieces.reshape(seqs, ff_part, col), "seq", 0, 0, tiled=True)
    own_proj = pieces.transpose(1, 0, 2).reshape(ff_part, model)
    wp_rel = jnp.stack(gather_rel(own_proj, "dp"))
    wp = jnp.concatenate(
        [lax.dynamic_index_in_dim(wp_rel, dp ^ k, 0, keepdims=False) for k in range(dps)], axis=0
    )

    wo = lax.all_gather(w_out, ("dp", "seq"), axis=0, tiled=True)
    wo = wo.reshape(dps, seqs, w_out.shape[0], w_out.shape[1]).transpose(0, 2, 1, 3)
    wo = wo.reshape(head_count, HD, model)
    empty = jnp.zeros((HD, model), BF)
    wo = jnp.concatenate([wo[h] if h >= 0 else empty for h in order], axis=0)

    x = tokens.astype(F32)
    z1, inv1 = normalise(x)
    n1 = swap_blocks((z1 * gain1 + shift1).astype(BF), dps, dp)
    n1_all = lax.all_gather(n1, "seq", axis=0, tiled=True)
    gm_all = lax.all_gather(cotangent, "seq", axis=0, tiled=True)
    qkv = (mm(n1_all, wq) + bias_qkv).astype(BF)
    att, lse = attend(qkv, slots)
    att = lax.all_to_all(att.reshape(seqs, rows, mine), "seq", 0, 0, tiled=True)
    att = att.transpose(1, 0, 2).reshape(rows, seqs * mine)
    r = x + (mm(att, wo) + bias_o)
    z2, inv2 = normalise(r)
    n2 = swap_blocks((z2 * gain2 + shift2).astype(BF), dps, dp)
    n2_all = lax.all_gather(n2, "seq", axis=0, tiled=True)
    u = mm(n2_all, wf) + bias_fc
    value, slope = gelu_parts(u)
    e = value.astype(BF)
    mlp = lax.psum_scatter(mm(e, wp).astype(BF), "seq", scatter_dimension=0, tiled=True)
    activations = (r + (mlp.astype(F32) + bias_p)).astype(BF)

    g = cotangent.astype(F32)
    gu = (mm_nt(gm_all, wp) * slope).astype(BF)
    gn2_part = mm_nt(gu, wf).astype(BF)
    gn2 = lax.psum_scatter(gn2_part, "seq", scatter_dimension=0, tiled=True)
    gn2 = swap_blocks(gn2, dps, dp).astype(F32)
    d_proj = mm_tn(e, gm_all)
    d_fc = mm_tn(n2_all, gu)
    sum_fc = jnp.sum(gu.astype(F32), axis=0)
    gr = g + norm_back(gn2, z2, inv2, gain2)
    go = gr.astype(BF)

    ga = mm_nt(go, wo).astype(BF)
    ga = lax.all_to_all(ga.reshape(rows, seqs, mine).transpose(1, 0, 2), "seq", 0, 0, tiled=True)
    ga = ga.reshape(seqs * rows, mine)
    d_out = mm_tn(att, go)
    gq, gk, gv = attend_back(qkv, ga, lse, slots)
    gqkv = jnp.concatenate([gq, gk, gv], axis=1)
    gn1_part = mm_nt(gqkv, wq).astype(BF)
    gn1 = lax.psum_scatter(gn1_part, "seq", scatter_dimension=0, tiled=True)
    gn1 = swap_blocks(gn1, dps, dp).astype(F32)
    d_qkv = mm_tn(n1_all, gqkv)
    input_grad = (gr + norm_back(gn1, z1, inv1, gain1)).astype(BF)

    def row_chunks(matrix):
        size = matrix.shape[0] // dps
        return [matrix[k * size : (k + 1) * size].astype(BF) for k in range(dps)]

    g_fc = scatter_rel(row_chunks(d_fc), "dp")
    g_qkv = scatter_rel(row_chunks(d_qkv), "dp").astype(BF)
    parts = jnp.einsum("ad,nwd->naw", g_qkv, to_recv, preferred_element_type=F32).astype(BF)
    parts = lax.all_to_all(parts, "seq", 0, 0, tiled=True)
    g_qkv = jnp.einsum("naw,cnw->ac", parts, to_send, preferred_element_type=F32)

    chunks = [
        lax.dynamic_slice_in_dim(d_proj, (dp ^ k) * ff_part, ff_part, axis=0).astype(BF)
        for k in range(dps)
    ]
    g_proj = scatter_rel(chunks, "dp").astype(BF)
    g_proj = g_proj.reshape(ff_part, seqs, col).transpose(1, 0, 2)
    g_proj = lax.all_to_all(g_proj, "seq", 0, 0, tiled=True)
    g_proj = g_proj.reshape(dps, ratio, ff_part, col)
    g_proj = lax.all_to_all(g_proj, "dp", 0, 0, tiled=True)
    g_proj = g_proj.transpose(1, 0, 2, 3).reshape(w_proj.shape).astype(F32)

    d_out = d_out.reshape(seqs * slots, HD, model)
    places = [int(np.where(order == h)[0][0]) for h in range(head_count)]
    d_out = jnp.concatenate([d_out[i] for i in places], axis=0).astype(BF)
    d_out = d_out.reshape(dps, w_out.shape[0], seqs, w_out.shape[1]).transpose(0, 2, 1, 3)
    d_out = d_out.reshape(-1, w_out.shape[1])
    g_out = lax.psum_scatter(d_out, ("dp", "seq"), scatter_dimension=0, tiled=True).astype(F32)

    gqkv_sums = jnp.sum(gqkv.astype(F32), axis=0)
    vector_grads = jnp.stack(
        [
            jnp.sum(gn1 * z1, axis=0),
            jnp.sum(gn1, axis=0),
            head_spread(gqkv_sums[:mine]),
            head_spread(gqkv_sums[2 * mine :]),
            jnp.sum(go.astype(F32), axis=0),
            jnp.sum(gn2 * z2, axis=0),
            jnp.sum(gn2, axis=0),
            jnp.sum(g, axis=0),
        ]
    )
    vector_grads = vector_grads.reshape(dps, per, seqs, wide_vec).transpose(0, 2, 1, 3)
    vector_grads = vector_grads.reshape(dps * seqs, per * wide_vec)
    fc_sums = lax.dynamic_update_slice_in_dim(
        jnp.zeros((dps * seqs * b_fc.shape[0],), F32), sum_fc, sq * ff_mine, axis=0
    ).reshape(dps * seqs, -1)
    sums = jnp.concatenate([vector_grads, fc_sums], axis=1)
    sums = lax.psum_scatter(sums, ("dp", "seq"), scatter_dimension=0, tiled=True)[0]
    return (
        activations,
        input_grad,
        g_qkv,
        g_out,
        sums[: per * wide_vec].reshape(per, wide_vec),
        g_fc,
        sums[per * wide_vec :],
        g_proj,
    )


def solution(mesh):
    rows = P(("dp", "seq"), None)
    grid = P("dp", "seq")
    line = P(("dp", "seq"))
    return jax.shard_map(
        body,
        mesh=mesh,
        in_specs=(rows, grid, grid, grid, grid, line, grid, rows),
        out_specs=(rows, rows, grid, grid, grid, grid, line, grid),
        check_vma=False,
    )
```

```python
import functools
import math

import jax
import jax.numpy as jnp
import numpy as np
from jax import lax
from jax.experimental import pallas as pl
from jax.experimental.pallas import tpu as pltpu
from jax.sharding import PartitionSpec as P

HD = 64
PAIR = 2 * HD
EPSILON = 1e-05
GELU_C = 0.7978845608028654
NEG_FILL = -1e30
BF = jnp.bfloat16
F32 = jnp.float32


def head_plan(head_count, seq_count, width):
    slots = -(-head_count // seq_count)
    slots += slots % 2
    model = head_count * HD

    def tables(turn):
        owner = np.full((seq_count, slots), -1, np.int32)
        for head in range(head_count):
            row = head // seq_count
            owner[(head + turn * row) % seq_count, row] = head
        place = {}
        for dev in range(seq_count):
            for slot in range(slots):
                if owner[dev, slot] >= 0:
                    place[int(owner[dev, slot])] = (dev, slot)
        lists = [[[] for _ in range(seq_count)] for _ in range(seq_count)]
        for col in range(3 * model):
            kind, rest = divmod(col, model)
            head, lane = divmod(rest, HD)
            dev, slot = place[head]
            src, local = divmod(col, width)
            lists[src][dev].append((local, (kind * slots + slot) * HD + lane))
        most = max(len(cell) for row in lists for cell in row)
        return most, owner, lists

    best = min((tables(turn) for turn in range(seq_count)), key=lambda t: t[0])
    most, owner, lists = best
    wide = -(-most // 128) * 128
    send = np.full((seq_count, seq_count, wide), -1, np.int32)
    recv = np.full((seq_count, seq_count, wide), -1, np.int32)
    for src in range(seq_count):
        for dev in range(seq_count):
            for i, (local, target) in enumerate(lists[src][dev]):
                send[src, dev, i] = local
                recv[src, dev, i] = target
    return slots, owner, wide, send, recv


def xor_perm(count, k):
    return [(i, i ^ k) for i in range(count)]


def gather_rel(block, axis):
    count = lax.axis_size(axis)
    return [block] + [lax.ppermute(block, axis, xor_perm(count, k)) for k in range(1, count)]


def scatter_rel(chunks, axis):
    count = lax.axis_size(axis)
    total = chunks[0].astype(F32)
    for k in range(1, count):
        total = total + lax.ppermute(chunks[k], axis, xor_perm(count, k)).astype(F32)
    return total


def gather_small(block, axis):
    count = lax.axis_size(axis)
    me = lax.axis_index(axis)
    stack = block[None]
    step = 1
    while step < count:
        other = lax.ppermute(stack, axis, xor_perm(count, step))
        low = (me & step) == 0
        stack = jnp.where(
            low, jnp.concatenate([stack, other]), jnp.concatenate([other, stack])
        )
        step *= 2
    return stack


def swap_blocks(matrix, count, me):
    size = matrix.shape[1] // count
    return jnp.concatenate(
        [lax.dynamic_slice_in_dim(matrix, (me ^ k) * size, size, axis=1) for k in range(count)],
        axis=1,
    )


def normalise(rows):
    mean = jnp.mean(rows, axis=-1, keepdims=True)
    centred = rows - mean
    inverse = lax.rsqrt(jnp.mean(centred * centred, axis=-1, keepdims=True) + EPSILON)
    return centred * inverse, inverse


def norm_back(grad, unit, inverse, gain):
    scaled = grad * gain
    return (
        scaled
        - jnp.mean(scaled, axis=-1, keepdims=True)
        - unit * jnp.mean(scaled * unit, axis=-1, keepdims=True)
    ) * inverse


def gelu_parts(u):
    cube = u * u * u
    t = jnp.tanh(GELU_C * (u + 0.044715 * cube))
    value = 0.5 * u * (1.0 + t)
    slope = 0.5 * (1.0 + t) + 0.5 * u * (1.0 - t * t) * GELU_C * (1.0 + 3 * 0.044715 * u * u)
    return value, slope


def mm(a, b):
    return jnp.dot(a, b, preferred_element_type=F32)


def mm_nt(a, b):
    return lax.dot_general(a, b, (((1,), (1,)), ((), ())), preferred_element_type=F32)


def mm_tn(a, b):
    return lax.dot_general(a, b, (((0,), (0,)), ((), ())), preferred_element_type=F32)


def block_rows(length):
    return math.gcd(length, 256)


def attend_kernel(q_ref, k_ref, v_ref, o_ref, lse_ref):
    length = q_ref.shape[0]
    rows = block_rows(length)
    first = lax.broadcasted_iota(jnp.int32, (rows, PAIR), 1) < HD
    causal = lax.broadcasted_iota(jnp.int32, (rows, rows), 0) >= lax.broadcasted_iota(
        jnp.int32, (rows, rows), 1
    )
    for i in range(length // rows):
        here = pl.ds(i * rows, rows)
        seen = (i + 1) * rows
        q = q_ref[here, :] * BF(1.0 / math.sqrt(HD))
        keys = k_ref[0:seen, :]
        values = v_ref[0:seen, :]
        outs, logs = [], []
        for mine in (first, ~first):
            s = mm_nt(jnp.where(mine, q, BF(0)), keys)
            tail = jnp.where(causal, s[:, seen - rows :], NEG_FILL)
            s = tail if i == 0 else jnp.concatenate([s[:, : seen - rows], tail], axis=1)
            top = jnp.max(s, axis=-1, keepdims=True)
            e = jnp.exp(s - top)
            total = jnp.sum(e, axis=-1, keepdims=True)
            outs.append(mm(e.astype(BF), values) / total)
            logs.append(top + jnp.log(total))
        o_ref[here, :] = jnp.where(first, outs[0], outs[1]).astype(BF)
        lse_ref[here, :] = jnp.where(first, logs[0], logs[1])


def attend(qkv, slots):
    length = qkv.shape[0]
    pairs = slots * HD // PAIR
    spec = lambda shift: pl.BlockSpec((length, PAIR), lambda g: (0, g + shift))
    return pl.pallas_call(
        attend_kernel,
        grid=(pairs,),
        in_specs=[spec(0), spec(pairs), spec(2 * pairs)],
        out_specs=[spec(0), spec(0)],
        out_shape=[
            jax.ShapeDtypeStruct((length, slots * HD), BF),
            jax.ShapeDtypeStruct((length, slots * HD), F32),
        ],
        compiler_params=pltpu.CompilerParams(vmem_limit_bytes=48 * 1024 * 1024),
    )(qkv, qkv, qkv)


def attend_back_kernel(q_ref, k_ref, v_ref, ga_ref, lse_ref, gq_ref, gk_ref, gv_ref, ak, av):
    length = q_ref.shape[0]
    rows = block_rows(length)
    first = lax.broadcasted_iota(jnp.int32, (rows, PAIR), 1) < HD
    causal = lax.broadcasted_iota(jnp.int32, (rows, rows), 0) >= lax.broadcasted_iota(
        jnp.int32, (rows, rows), 1
    )
    ak[...] = jnp.zeros_like(ak)
    av[...] = jnp.zeros_like(av)
    for i in range(length // rows):
        here = pl.ds(i * rows, rows)
        seen = (i + 1) * rows
        q = q_ref[here, :] * BF(1.0 / math.sqrt(HD))
        ga = ga_ref[here, :]
        keys = k_ref[0:seen, :]
        values = v_ref[0:seen, :]
        grads = []
        for h, mine in enumerate((first, ~first)):
            q_h = jnp.where(mine, q, BF(0))
            ga_h = jnp.where(mine, ga, BF(0))
            s = mm_nt(q_h, keys)
            tail = jnp.where(causal, s[:, seen - rows :], NEG_FILL)
            s = tail if i == 0 else jnp.concatenate([s[:, : seen - rows], tail], axis=1)
            p = jnp.exp(s - lse_ref[here, h * HD : h * HD + 1])
            gp = mm_nt(ga_h, values)
            centre = jnp.sum(p * gp, axis=-1, keepdims=True)
            gs = (p * (gp - centre)).astype(BF)
            av[0:seen, :] += mm_tn(p.astype(BF), ga_h)
            ak[0:seen, :] += mm_tn(gs, q_h)
            grads.append(mm(gs, keys))
        gq_ref[here, :] = (jnp.where(first, grads[0], grads[1]) * (1.0 / math.sqrt(HD))).astype(BF)
    gk_ref[...] = ak[...].astype(BF)
    gv_ref[...] = av[...].astype(BF)


def attend_back(qkv, grad, lse, slots):
    length = qkv.shape[0]
    pairs = slots * HD // PAIR
    spec = lambda shift: pl.BlockSpec((length, PAIR), lambda g: (0, g + shift))
    shape = jax.ShapeDtypeStruct((length, slots * HD), BF)
    return pl.pallas_call(
        attend_back_kernel,
        grid=(pairs,),
        in_specs=[spec(0), spec(pairs), spec(2 * pairs), spec(0), spec(0)],
        out_specs=[spec(0), spec(0), spec(0)],
        out_shape=[shape, shape, shape],
        scratch_shapes=[pltpu.VMEM((length, PAIR), F32), pltpu.VMEM((length, PAIR), F32)],
        compiler_params=pltpu.CompilerParams(vmem_limit_bytes=48 * 1024 * 1024),
    )(qkv, qkv, qkv, grad, lse)


ANY = pl.BlockSpec(memory_space=pl.ANY)
WHOLE = pl.BlockSpec(memory_space=pltpu.VMEM)
SCALAR = pl.BlockSpec(memory_space=pltpu.SMEM)
ROOM = pltpu.CompilerParams(vmem_limit_bytes=48 * 1024 * 1024)


def out_blocks(w_out):
    seqs = lax.axis_size("seq")
    line = [w_out] + [
        lax.ppermute(w_out, "seq", xor_perm(seqs, 2 * dz)) for dz in range(1, seqs // 2)
    ]
    near = gather_rel(jnp.stack(line), "dp")
    return [[b, lax.ppermute(b, "seq", xor_perm(seqs, 1))] for b in near]


def block_copies(where, blocks, store, sems, outward):
    copies = []
    for dk, pair in enumerate(blocks):
        for dc, ref in enumerate(pair):
            for dz in range(ref.shape[0]):
                near, far = ref.at[dz], store.at[where[0] ^ dk, where[1] ^ (2 * dz + dc)]
                src, dst = (far, near) if outward else (near, far)
                copies.append(pltpu.make_async_copy(src, dst, sems.at[len(copies)]))
    return copies


def head_columns(att_ref, owner):
    count = int(owner.max()) + 1
    parts = []
    for h in range(count):
        dev, slot = [int(i[0]) for i in np.where(owner == h)]
        parts.append(att_ref[dev, :, slot * HD : (slot + 1) * HD])
    return jnp.concatenate(parts, axis=1)


def out_kernel(dps, seqs, owner, where, att_ref, x_ref, vec_ref, *rest):
    flat = rest[: 2 * dps]
    r_ref, n2_ref, store, sems = rest[2 * dps :]
    blocks = [flat[2 * k : 2 * k + 2] for k in range(dps)]
    copies = block_copies(where, blocks, store, sems, False)
    for c in copies:
        c.start()
    att = head_columns(att_ref, owner)
    depth, width = store.shape[2:]
    for c in copies:
        c.wait()
    for n in range(seqs):
        here = slice(n * width, (n + 1) * width)
        total = x_ref[:, here].astype(F32) + vec_ref[4:5, here]
        for p in range(dps):
            total = total + mm(att[:, p * depth : (p + 1) * depth], store[p, n])
        r_ref[:, here] = total
    unit, _ = normalise(r_ref[...])
    n2 = (unit * vec_ref[5:6, :] + vec_ref[6:7, :]).astype(BF)
    me = where[0]
    for k in range(dps):
        piece = n2[:, k * depth : (k + 1) * depth]
        for i in range(1, dps):
            piece = jnp.where(me == i, n2[:, (i ^ k) * depth : ((i ^ k) + 1) * depth], piece)
        n2_ref[:, k * depth : (k + 1) * depth] = piece


def out_project(where, att, x, table, blocks, owner):
    flat = [b for pair in blocks for b in pair]
    dps, seqs = len(blocks), att.shape[0]
    depth, width = flat[0].shape[1:]
    return pl.pallas_call(
        functools.partial(out_kernel, dps, seqs, owner),
        in_specs=[SCALAR, WHOLE, WHOLE, WHOLE] + [ANY] * len(flat),
        out_specs=[WHOLE, WHOLE],
        out_shape=[jax.ShapeDtypeStruct(x.shape, F32), jax.ShapeDtypeStruct(x.shape, BF)],
        scratch_shapes=[
            pltpu.VMEM((dps, seqs, depth, width), BF),
            pltpu.SemaphoreType.DMA((dps * seqs,)),
        ],
        compiler_params=ROOM,
    )(where, att, x, table, *flat)


def back_kernel(dps, seqs, owner, where, gn2_ref, r_ref, g_ref, vec_ref, *rest):
    flat = rest[: 2 * dps]
    gr_ref, go_ref, ga_ref, sums_ref, store, sems = rest[2 * dps :]
    blocks = [flat[2 * k : 2 * k + 2] for k in range(dps)]
    copies = block_copies(where, blocks, store, sems, False)
    for c in copies:
        c.start()
    depth, width = store.shape[2:]
    me = where[0]
    for k in range(dps):
        piece = gn2_ref[:, k * depth : (k + 1) * depth]
        for i in range(1, dps):
            piece = jnp.where(me == i, gn2_ref[:, (i ^ k) * depth : ((i ^ k) + 1) * depth], piece)
        gr_ref[:, k * depth : (k + 1) * depth] = piece.astype(F32)
    gn2 = gr_ref[...]
    unit, inverse = normalise(r_ref[...])
    gr = g_ref[...].astype(F32) + norm_back(gn2, unit, inverse, vec_ref[5:6, :])
    go = gr.astype(BF)
    gr_ref[...] = gr
    go_ref[...] = go
    sums_ref[0:1, :] = jnp.sum(go.astype(F32), axis=0, keepdims=True)
    sums_ref[1:2, :] = jnp.sum(gn2 * unit, axis=0, keepdims=True)
    sums_ref[2:3, :] = jnp.sum(gn2, axis=0, keepdims=True)
    sums_ref[3:4, :] = jnp.sum(g_ref[...].astype(F32), axis=0, keepdims=True)
    for c in copies:
        c.wait()
    parts = []
    for p in range(dps):
        total = mm_nt(go[:, 0:width], store[p, 0])
        for n in range(1, seqs):
            total = total + mm_nt(go[:, n * width : (n + 1) * width], store[p, n])
        parts.append(total)
    ga = jnp.concatenate(parts, axis=1).astype(BF)
    ga_ref[...] = jnp.zeros_like(ga_ref)
    for h in range(int(owner.max()) + 1):
        dev, slot = [int(i[0]) for i in np.where(owner == h)]
        ga_ref[dev, :, slot * HD : (slot + 1) * HD] = ga[:, h * HD : (h + 1) * HD]


def out_back(where, gn2, r, g, table, blocks, owner):
    flat = [b for pair in blocks for b in pair]
    dps, seqs = len(blocks), owner.shape[0]
    depth, width = flat[0].shape[1:]
    return pl.pallas_call(
        functools.partial(back_kernel, dps, seqs, owner),
        in_specs=[SCALAR, WHOLE, WHOLE, WHOLE, WHOLE] + [ANY] * len(flat),
        out_specs=[WHOLE] * 4,
        out_shape=[
            jax.ShapeDtypeStruct(r.shape, F32),
            jax.ShapeDtypeStruct(r.shape, BF),
            jax.ShapeDtypeStruct((seqs, r.shape[0], owner.shape[1] * HD), BF),
            jax.ShapeDtypeStruct((4, r.shape[1]), F32),
        ],
        scratch_shapes=[
            pltpu.VMEM((dps, seqs, depth, width), BF),
            pltpu.SemaphoreType.DMA((dps * seqs,)),
        ],
        compiler_params=ROOM,
    )(where, gn2, r, g, table, *flat)


def grad_out_kernel(dps, seqs, owner, where, att_ref, go_ref, *rest):
    flat = rest[: 2 * dps]
    store, sems = rest[2 * dps :]
    blocks = [flat[2 * k : 2 * k + 2] for k in range(dps)]
    att = head_columns(att_ref, owner)
    depth, width = store.shape[2:]
    for p in range(dps):
        rows = att[:, p * depth : (p + 1) * depth]
        for n in range(seqs):
            store[p, n] = mm_tn(rows, go_ref[:, n * width : (n + 1) * width]).astype(BF)
    copies = block_copies(where, blocks, store, sems, True)
    for c in copies:
        c.start()
    for c in copies:
        c.wait()


def grad_out(where, att, go, dps, owner):
    seqs = att.shape[0]
    depth, width = go.shape[1] // dps, go.shape[1] // seqs
    shape = jax.ShapeDtypeStruct((seqs // 2, depth, width), BF)
    flat = pl.pallas_call(
        functools.partial(grad_out_kernel, dps, seqs, owner),
        in_specs=[SCALAR, WHOLE, WHOLE],
        out_specs=[ANY] * (2 * dps),
        out_shape=[shape] * (2 * dps),
        scratch_shapes=[
            pltpu.VMEM((dps, seqs, depth, width), BF),
            pltpu.SemaphoreType.DMA((dps * seqs,)),
        ],
        compiler_params=ROOM,
    )(where, att, go)
    return [flat[2 * k : 2 * k + 2] for k in range(dps)]


def sum_out_blocks(blocks):
    seqs = lax.axis_size("seq")
    chip = [
        (mine.astype(F32) + lax.ppermute(other, "seq", xor_perm(seqs, 1)).astype(F32)).astype(BF)
        for mine, other in blocks
    ]
    line = scatter_rel(chip, "dp").astype(BF)
    total = line[0].astype(F32)
    for dz in range(1, seqs // 2):
        total = total + lax.ppermute(line[dz], "seq", xor_perm(seqs, 2 * dz)).astype(F32)
    return total


def sum_all(block):
    for axis in ("dp", "seq"):
        step = 1
        while step < lax.axis_size(axis):
            block = block + lax.ppermute(block, axis, xor_perm(lax.axis_size(axis), step))
            step *= 2
    return block


def body(tokens, w_qkv, w_out, vectors, w_fc, b_fc, w_proj, cotangent):
    dps = lax.axis_size("dp")
    seqs = lax.axis_size("seq")
    dp = lax.axis_index("dp")
    sq = lax.axis_index("seq")
    rows, model = tokens.shape
    head_count = model // HD
    slots, owner, wide, send, recv = head_plan(head_count, seqs, w_qkv.shape[1])
    mine = slots * HD
    ff_mine = w_fc.shape[1]
    ff_part = ff_mine // dps
    ratio = seqs // dps
    col = w_proj.shape[1]

    per, wide_vec = vectors.shape
    small = gather_small(jnp.concatenate([vectors.reshape(-1), b_fc])[None], "dp")
    small = gather_small(small, "seq").astype(F32)[:, :, 0]
    table = small[:, :, : per * wide_vec].reshape(seqs, dps, per, wide_vec)
    table = table.transpose(1, 2, 0, 3).reshape(dps * per, model)
    gain1, shift1, bias_q, bias_v, bias_o, gain2, shift2, bias_p = [table[i] for i in range(8)]
    bias_fc = small[:, :, per * wide_vec :].transpose(1, 0, 2).reshape(-1)
    bias_fc = lax.dynamic_slice_in_dim(bias_fc, sq * ff_mine, ff_mine)
    own_heads = jnp.asarray(owner)[sq]
    pick = (own_heads[:, None] == jnp.arange(head_count)[None, :]).astype(F32)

    def head_rows(vector):
        return jnp.sum(pick[:, :, None] * vector.reshape(1, head_count, HD), axis=1).reshape(-1)

    def head_spread(vector):
        return jnp.sum(pick[:, :, None] * vector.reshape(slots, 1, HD), axis=0).reshape(-1)

    bias_qkv = jnp.concatenate([head_rows(bias_q), jnp.zeros((mine,), F32), head_rows(bias_v)])

    to_send = (jnp.arange(w_qkv.shape[1])[:, None, None] == jnp.asarray(send)[sq][None]).astype(BF)
    to_recv = (
        lax.dynamic_index_in_dim(jnp.asarray(recv), sq, 1, keepdims=False)[:, :, None]
        == jnp.arange(3 * mine)[None, None]
    ).astype(BF)
    parts = jnp.einsum("ac,cnw->naw", w_qkv, to_send, preferred_element_type=F32).astype(BF)
    parts = lax.all_to_all(parts, "seq", 0, 0, tiled=True)
    own_qkv = jnp.einsum("naw,nwd->ad", parts, to_recv, preferred_element_type=F32).astype(BF)
    wf = jnp.concatenate(gather_rel(w_fc, "dp"), axis=0)

    pieces = w_proj.reshape(ratio, dps, ff_part, col)
    pieces = lax.all_to_all(pieces.transpose(1, 0, 2, 3), "dp", 0, 0, tiled=True)
    pieces = lax.all_to_all(pieces.reshape(seqs, ff_part, col), "seq", 0, 0, tiled=True)
    own_proj = pieces.transpose(1, 0, 2).reshape(ff_part, model)
    wp_rel = jnp.stack(gather_rel(own_proj, "dp"))
    wp = jnp.concatenate(
        [lax.dynamic_index_in_dim(wp_rel, dp ^ k, 0, keepdims=False) for k in range(dps)], axis=0
    )

    where = jnp.stack([dp, sq]).astype(jnp.int32)
    wo = out_blocks(w_out)

    x = tokens.astype(F32)
    z1, inv1 = normalise(x)
    n1 = swap_blocks((z1 * gain1 + shift1).astype(BF), dps, dp)
    n1, own_qkv = lax.optimization_barrier((n1, own_qkv))
    n1_all = lax.all_gather(n1, "seq", axis=0, tiled=True)
    wq = jnp.concatenate(gather_rel(own_qkv, "dp"), axis=0)
    cot, n1_all = lax.optimization_barrier((cotangent, n1_all))
    gm_all = lax.all_gather(cot, "seq", axis=0, tiled=True)
    qkv = (mm(n1_all, wq) + bias_qkv).astype(BF)
    att, lse = attend(qkv, slots)
    att = lax.all_to_all(att.reshape(seqs, rows, mine), "seq", 0, 0, tiled=True)
    r, n2 = out_project(where, att, tokens, table, wo, owner)
    n2_all = lax.all_gather(n2, "seq", axis=0, tiled=True)
    u = mm(n2_all, wf) + bias_fc
    value, slope = gelu_parts(u)
    e = value.astype(BF)

    gu = (mm_nt(gm_all, wp) * slope).astype(BF)
    gn2_part = mm_nt(gu, wf).astype(BF)
    gn2 = lax.psum_scatter(gn2_part, "seq", scatter_dimension=0, tiled=True)
    e, gn2 = lax.optimization_barrier((e, gn2))
    mlp = lax.psum_scatter(mm(e, wp).astype(BF), "seq", scatter_dimension=0, tiled=True)
    activations = (r + (mlp.astype(F32) + bias_p)).astype(BF)
    d_proj = mm_tn(e, gm_all)
    d_fc = mm_tn(n2_all, gu)
    sum_fc = jnp.sum(gu.astype(F32), axis=0)

    gr, go, ga, sums_two = out_back(where, gn2, r, cotangent, table, wo, owner)
    ga = lax.all_to_all(ga, "seq", 0, 0, tiled=True)
    ga = ga.reshape(seqs * rows, mine)
    d_out = grad_out(where, att, go, dps, owner)
    gq, gk, gv = attend_back(qkv, ga, lse, slots)
    gqkv = jnp.concatenate([gq, gk, gv], axis=1)
    gn1_full = mm_nt(gqkv, wq)
    gn1 = lax.psum_scatter(gn1_full.astype(BF), "seq", scatter_dimension=0, tiled=True)
    gn1 = swap_blocks(gn1, dps, dp).astype(F32)
    d_qkv = mm_tn(n1_all, gqkv)
    input_grad = (gr + norm_back(gn1, z1, inv1, gain1)).astype(BF)

    def row_chunks(matrix):
        size = matrix.shape[0] // dps
        return [matrix[k * size : (k + 1) * size].astype(BF) for k in range(dps)]

    g_fc = scatter_rel(row_chunks(d_fc), "dp")
    g_qkv = scatter_rel(row_chunks(d_qkv), "dp").astype(BF)
    parts = jnp.einsum("ad,nwd->naw", g_qkv, to_recv, preferred_element_type=F32).astype(BF)
    parts = lax.all_to_all(parts, "seq", 0, 0, tiled=True)
    g_qkv = jnp.einsum("naw,cnw->ac", parts, to_send, preferred_element_type=F32)

    chunks = [
        lax.dynamic_slice_in_dim(d_proj, (dp ^ k) * ff_part, ff_part, axis=0).astype(BF)
        for k in range(dps)
    ]
    g_proj = scatter_rel(chunks, "dp").astype(BF)
    g_proj = g_proj.reshape(ff_part, seqs, col).transpose(1, 0, 2)
    g_proj = lax.all_to_all(g_proj, "seq", 0, 0, tiled=True)
    g_proj = g_proj.reshape(dps, ratio, ff_part, col)
    g_proj = lax.all_to_all(g_proj, "dp", 0, 0, tiled=True)
    g_proj = g_proj.transpose(1, 0, 2, 3).reshape(w_proj.shape).astype(F32)

    g_out = sum_out_blocks(d_out)

    gqkv_sums = jnp.sum(gqkv.astype(F32), axis=0)
    both = jnp.stack([jnp.sum(gn1_full * n1_all.astype(F32), axis=0), jnp.sum(gn1_full, axis=0)])
    both = swap_blocks(both, dps, dp)
    vector_grads = jnp.concatenate(
        [
            ((both[0] - shift1 * both[1]) / gain1)[None],
            both[1:],
            head_spread(gqkv_sums[:mine])[None],
            head_spread(gqkv_sums[2 * mine :])[None],
            sums_two,
        ]
    )
    fc_sums = lax.dynamic_update_slice_in_dim(
        jnp.zeros((dps * seqs * b_fc.shape[0],), F32), sum_fc, sq * ff_mine, axis=0
    ).reshape(-1, model)
    sums = sum_all(jnp.concatenate([vector_grads, fc_sums]))
    own_vec = lax.dynamic_slice(sums, (dp * per, sq * wide_vec), (per, wide_vec))
    own_fc = lax.dynamic_slice_in_dim(
        sums[8:].reshape(-1), (dp * seqs + sq) * b_fc.shape[0], b_fc.shape[0]
    )
    return (
        activations,
        input_grad,
        g_qkv,
        g_out,
        own_vec,
        g_fc,
        own_fc,
        g_proj,
    )


def solution(mesh):
    rows = P(("dp", "seq"), None)
    grid = P("dp", "seq")
    line = P(("dp", "seq"))
    return jax.shard_map(
        body,
        mesh=mesh,
        in_specs=(rows, grid, grid, grid, grid, line, grid, rows),
        out_specs=(rows, rows, grid, grid, grid, grid, line, grid),
        check_vma=False,
    )
```

```python
import functools
import math

import jax
import jax.numpy as jnp
import numpy as np
from jax import lax
from jax.experimental import pallas as pl
from jax.experimental.pallas import tpu as pltpu
from jax.sharding import PartitionSpec as P

HD = 64
PAIR = 2 * HD
EPSILON = 1e-05
GELU_C = 0.7978845608028654
NEG_FILL = -1e30
BF = jnp.bfloat16
F32 = jnp.float32


def head_plan(head_count, seq_count, width):
    slots = -(-head_count // seq_count)
    slots += slots % 2
    model = head_count * HD

    def tables(turn):
        owner = np.full((seq_count, slots), -1, np.int32)
        for head in range(head_count):
            row = head // seq_count
            owner[(head + turn * row) % seq_count, row] = head
        place = {}
        for dev in range(seq_count):
            for slot in range(slots):
                if owner[dev, slot] >= 0:
                    place[int(owner[dev, slot])] = (dev, slot)
        lists = [[[] for _ in range(seq_count)] for _ in range(seq_count)]
        for col in range(3 * model):
            kind, rest = divmod(col, model)
            head, lane = divmod(rest, HD)
            dev, slot = place[head]
            src, local = divmod(col, width)
            lists[src][dev].append((local, (kind * slots + slot) * HD + lane))
        most = max(len(cell) for row in lists for cell in row)
        return most, owner, lists

    best = min((tables(turn) for turn in range(seq_count)), key=lambda t: t[0])
    most, owner, lists = best
    wide = -(-most // 128) * 128
    send = np.full((seq_count, seq_count, wide), -1, np.int32)
    recv = np.full((seq_count, seq_count, wide), -1, np.int32)
    for src in range(seq_count):
        for dev in range(seq_count):
            for i, (local, target) in enumerate(lists[src][dev]):
                send[src, dev, i] = local
                recv[src, dev, i] = target
    return slots, owner, wide, send, recv


def xor_perm(count, k):
    return [(i, i ^ k) for i in range(count)]


def gather_rel(block, axis):
    count = lax.axis_size(axis)
    return [block] + [lax.ppermute(block, axis, xor_perm(count, k)) for k in range(1, count)]


def scatter_rel(chunks, axis):
    count = lax.axis_size(axis)
    total = chunks[0].astype(F32)
    for k in range(1, count):
        total = total + lax.ppermute(chunks[k], axis, xor_perm(count, k)).astype(F32)
    return total


def gather_small(block, axis):
    count = lax.axis_size(axis)
    me = lax.axis_index(axis)
    stack = block[None]
    step = 1
    while step < count:
        other = lax.ppermute(stack, axis, xor_perm(count, step))
        low = (me & step) == 0
        stack = jnp.where(
            low, jnp.concatenate([stack, other]), jnp.concatenate([other, stack])
        )
        step *= 2
    return stack


ANY = pl.BlockSpec(memory_space=pl.ANY)
WHOLE = pl.BlockSpec(memory_space=pltpu.VMEM)
SCALAR = pl.BlockSpec(memory_space=pltpu.SMEM)
ROOM = pltpu.CompilerParams(vmem_limit_bytes=56 * 1024 * 1024)


def normalise(rows):
    mean = jnp.mean(rows, axis=-1, keepdims=True)
    centred = rows - mean
    inverse = lax.rsqrt(jnp.mean(centred * centred, axis=-1, keepdims=True) + EPSILON)
    return centred * inverse, inverse


def norm_back(grad, unit, inverse, gain):
    scaled = grad * gain
    return (
        scaled
        - jnp.mean(scaled, axis=-1, keepdims=True)
        - unit * jnp.mean(scaled * unit, axis=-1, keepdims=True)
    ) * inverse


def gelu_parts(u):
    cube = u * u * u
    t = jnp.tanh(GELU_C * (u + 0.044715 * cube))
    value = 0.5 * u * (1.0 + t)
    slope = 0.5 * (1.0 + t) + 0.5 * u * (1.0 - t * t) * GELU_C * (1.0 + 3 * 0.044715 * u * u)
    return value, slope


def mm(a, b):
    return jnp.dot(a, b, preferred_element_type=F32)


def mm_nt(a, b):
    return lax.dot_general(a, b, (((1,), (1,)), ((), ())), preferred_element_type=F32)


def mm_tn(a, b):
    return lax.dot_general(a, b, (((0,), (0,)), ((), ())), preferred_element_type=F32)


def block_rows(length):
    return math.gcd(length, 256)


def head_masks(rows):
    first = lax.broadcasted_iota(jnp.int32, (rows, PAIR), 1) < HD
    causal = lax.broadcasted_iota(jnp.int32, (rows, rows), 0) >= lax.broadcasted_iota(
        jnp.int32, (rows, rows), 1
    )
    return first, causal


def masked_scores(q, keys, causal):
    rows, seen = q.shape[0], keys.shape[0]
    s = mm_nt(q, keys)
    tail = jnp.where(causal, s[:, seen - rows :], NEG_FILL)
    return tail if seen == rows else jnp.concatenate([s[:, : seen - rows], tail], axis=1)


def attend_rows(q, keys, values, first, causal):
    q = q * BF(1.0 / math.sqrt(HD))
    outs, logs = [], []
    for mine in (first, ~first):
        s = masked_scores(jnp.where(mine, q, BF(0)), keys, causal)
        top = jnp.max(s, axis=-1, keepdims=True)
        e = jnp.exp(s - top)
        total = jnp.sum(e, axis=-1, keepdims=True)
        outs.append(mm(e.astype(BF), values) / total)
        logs.append(top + jnp.log(total))
    return jnp.where(first, outs[0], outs[1]).astype(BF), jnp.where(first, logs[0], logs[1])


def row_blocks_in(where, refs, store, sems):
    copies = [
        pltpu.make_async_copy(ref, store.at[where[0] ^ k], sems.at[k])
        for k, ref in enumerate(refs)
    ]
    for c in copies:
        c.start()
    return copies


def right_blocks(rows, store):
    count, depth = store.shape[:2]
    total = mm(rows[:, :depth], store[0])
    for p in range(1, count):
        total = total + mm(rows[:, p * depth : (p + 1) * depth], store[p])
    return total


def attend_kernel(dps, pairs, where, x_ref, vec_ref, bias_ref, *rest):
    w_refs = rest[:dps]
    n1_ref, qkv_ref, att_ref, lse_ref, w, qkv, sems = rest[dps:]
    i = pl.program_id(0)
    rows = x_ref.shape[0]
    steps = qkv.shape[0] // rows

    @pl.when(i == 0)
    def _():
        for c in row_blocks_in(where, w_refs, w, sems):
            c.wait()

    unit, _ = normalise(x_ref[...].astype(F32))
    n1 = (unit * vec_ref[0:1, :] + vec_ref[1:2, :]).astype(BF)
    n1_ref[...] = n1
    tile = (right_blocks(n1, w) + bias_ref[...]).astype(BF)
    qkv_ref[...] = tile
    qkv[pl.ds(pl.multiple_of(i * rows, rows), rows), :] = tile
    first, causal = head_masks(rows)
    part = att_ref.shape[1]
    for j in range(steps):

        @pl.when(i == j)
        def _(j=j):
            seen = (j + 1) * rows
            for g in range(pairs):
                lanes = slice(g * PAIR, (g + 1) * PAIR)
                keys = qkv[0:seen, (pairs + g) * PAIR : (pairs + g + 1) * PAIR]
                values = qkv[0:seen, (2 * pairs + g) * PAIR : (2 * pairs + g + 1) * PAIR]
                out, log = attend_rows(
                    qkv[j * rows : seen, lanes], keys, values, first, causal
                )
                for b in range(rows // part):
                    att_ref[b, :, lanes] = out[b * part : (b + 1) * part]
                lse_ref[:, lanes] = log


def attend(where, x_all, table, bias, weights, slots, part):
    length, model = x_all.shape
    dps = len(weights)
    depth, width = weights[0].shape
    mine = slots * HD
    rows = block_rows(length)
    whole = lambda shape: pl.BlockSpec(shape, lambda i: (0,) * len(shape))
    tile = lambda cols: pl.BlockSpec((rows, cols), lambda i: (i, 0))
    return pl.pallas_call(
        functools.partial(attend_kernel, dps, mine // PAIR),
        grid=(length // rows,),
        in_specs=[SCALAR, tile(model), whole(table.shape), whole(bias.shape)] + [ANY] * dps,
        out_specs=[
            tile(model),
            tile(width),
            pl.BlockSpec((rows // part, part, mine), lambda i: (i, 0, 0)),
            tile(mine),
        ],
        out_shape=[
            jax.ShapeDtypeStruct((length, model), BF),
            jax.ShapeDtypeStruct((length, width), BF),
            jax.ShapeDtypeStruct((length // part, part, mine), BF),
            jax.ShapeDtypeStruct((length, mine), F32),
        ],
        scratch_shapes=[
            pltpu.VMEM((dps, depth, width), BF),
            pltpu.VMEM((length, width), BF),
            pltpu.SemaphoreType.DMA((dps,)),
        ],
        compiler_params=ROOM,
    )(where, x_all, table, bias, *weights)


def attend_back_kernel(dps, pairs, where, qkv_ref, ga_ref, lse_ref, *rest):
    w_refs = rest[:dps]
    gqkv_ref, gn1_ref, w, ak, av, sems = rest[dps:]
    length = qkv_ref.shape[0]
    rows = block_rows(length)
    copies = row_blocks_in(where, w_refs, w, sems)
    first, causal = head_masks(rows)
    part = ga_ref.shape[1]
    for g in range(pairs):
        lanes = slice(g * PAIR, (g + 1) * PAIR)
        k_lanes = slice((pairs + g) * PAIR, (pairs + g + 1) * PAIR)
        v_lanes = slice((2 * pairs + g) * PAIR, (2 * pairs + g + 1) * PAIR)
        ak[...] = jnp.zeros_like(ak)
        av[...] = jnp.zeros_like(av)
        for i in range(length // rows):
            here = slice(i * rows, (i + 1) * rows)
            seen = (i + 1) * rows
            q = qkv_ref[here, lanes] * BF(1.0 / math.sqrt(HD))
            ga = jnp.concatenate(
                [ga_ref[b, :, lanes] for b in range(i * rows // part, seen // part)], axis=0
            )
            keys = qkv_ref[0:seen, k_lanes]
            values = qkv_ref[0:seen, v_lanes]
            grads = []
            for h, mine in enumerate((first, ~first)):
                q_h = jnp.where(mine, q, BF(0))
                ga_h = jnp.where(mine, ga, BF(0))
                s = masked_scores(q_h, keys, causal)
                lane = g * PAIR + h * HD
                p = jnp.exp(s - lse_ref[here, lane : lane + 1])
                gp = mm_nt(ga_h, values)
                centre = jnp.sum(p * gp, axis=-1, keepdims=True)
                gs = (p * (gp - centre)).astype(BF)
                av[0:seen, :] += mm_tn(p.astype(BF), ga_h)
                ak[0:seen, :] += mm_tn(gs, q_h)
                grads.append(mm(gs, keys))
            gqkv_ref[here, lanes] = (
                jnp.where(first, grads[0], grads[1]) * (1.0 / math.sqrt(HD))
            ).astype(BF)
        gqkv_ref[:, k_lanes] = ak[...].astype(BF)
        gqkv_ref[:, v_lanes] = av[...].astype(BF)
    for c in copies:
        c.wait()
    depth = w.shape[1]
    for i in range(length // rows):
        here = slice(i * rows, (i + 1) * rows)
        for p in range(dps):
            gn1_ref[here, p * depth : (p + 1) * depth] = mm_nt(gqkv_ref[here, :], w[p]).astype(BF)


def attend_back(where, qkv, grad, lse, weights):
    length, width = qkv.shape
    dps = len(weights)
    depth = weights[0].shape[0]
    return pl.pallas_call(
        functools.partial(attend_back_kernel, dps, grad.shape[2] // PAIR),
        in_specs=[SCALAR, WHOLE, WHOLE, WHOLE] + [ANY] * dps,
        out_specs=[WHOLE, WHOLE],
        out_shape=[
            jax.ShapeDtypeStruct((length, width), BF),
            jax.ShapeDtypeStruct((length, dps * depth), BF),
        ],
        scratch_shapes=[
            pltpu.VMEM((dps, depth, width), BF),
            pltpu.VMEM((length, PAIR), F32),
            pltpu.VMEM((length, PAIR), F32),
            pltpu.SemaphoreType.DMA((dps,)),
        ],
        compiler_params=ROOM,
    )(where, qkv, grad, lse, *weights)


def grad_qkv_kernel(dps, where, n1_ref, gqkv_ref, gn1_ref, *rest):
    outs = rest[:dps]
    sums_ref, norm_ref, store, sems = rest[dps:]
    depth = store.shape[1]
    gqkv = gqkv_ref[...]
    for p in range(dps):
        store[p] = mm_tn(n1_ref[:, p * depth : (p + 1) * depth], gqkv).astype(BF)
    copies = [
        pltpu.make_async_copy(store.at[where[0] ^ k], ref, sems.at[k])
        for k, ref in enumerate(outs)
    ]
    for c in copies:
        c.start()
    sums_ref[...] = jnp.sum(gqkv.astype(F32), axis=0, keepdims=True)
    gn1 = gn1_ref[...].astype(F32)
    norm_ref[0:1, :] = jnp.sum(gn1 * n1_ref[...].astype(F32), axis=0, keepdims=True)
    norm_ref[1:2, :] = jnp.sum(gn1, axis=0, keepdims=True)
    for c in copies:
        c.wait()


def grad_qkv(where, n1, gqkv, gn1, dps):
    model, width = n1.shape[1], gqkv.shape[1]
    depth = model // dps
    *chunks, sums, norm = pl.pallas_call(
        functools.partial(grad_qkv_kernel, dps),
        in_specs=[SCALAR, WHOLE, WHOLE, WHOLE],
        out_specs=[ANY] * dps + [WHOLE, WHOLE],
        out_shape=[jax.ShapeDtypeStruct((depth, width), BF)] * dps
        + [jax.ShapeDtypeStruct((1, width), F32), jax.ShapeDtypeStruct((2, model), F32)],
        scratch_shapes=[pltpu.VMEM((dps, depth, width), BF), pltpu.SemaphoreType.DMA((dps,))],
        compiler_params=ROOM,
    )(where, n1, gqkv, gn1)
    return chunks, sums, norm


def piece_rows(total, count):
    tiles = total // 16
    return 16 * -(-tiles // count), lambda q: 16 * ((q * tiles) // count)


def feed_kernel(dps, where, n2_ref, gm_ref, bias_ref, *rest):
    f_refs, p_refs = rest[:dps], rest[dps : 2 * dps]
    e_ref, gu_ref, gn2_ref, sum_ref, wf, wp, sems, sems2 = rest[2 * dps :]
    i = pl.program_id(0)
    size, start = piece_rows(wp.shape[0], dps)

    @pl.when(i == 0)
    def _():
        copies = row_blocks_in(where, f_refs, wf, sems)
        for k, ref in enumerate(p_refs):
            here = pl.ds(pl.multiple_of(start(where[0] ^ k), 16), size)
            one = pltpu.make_async_copy(ref, wp.at[here, :], sems2)
            one.start()
            one.wait()
        for c in copies:
            c.wait()
        sum_ref[...] = jnp.zeros_like(sum_ref)

    u = right_blocks(n2_ref[...], wf) + bias_ref[...]
    ge = mm_nt(gm_ref[...], wp[...])
    value, slope = gelu_parts(u)
    e_ref[...] = value.astype(BF)
    gu = (ge * slope).astype(BF)
    gu_ref[...] = gu
    sum_ref[...] += jnp.sum(gu.astype(F32), axis=0, keepdims=True)
    depth = wf.shape[1]
    for p in range(dps):
        gn2_ref[:, p * depth : (p + 1) * depth] = mm_nt(gu, wf[p]).astype(BF)


def feed(where, n2, gm, bias, fc, proj):
    length, model = n2.shape
    dps = len(fc)
    depth, width = fc[0].shape
    rows = block_rows(length)
    whole = lambda shape: pl.BlockSpec(shape, lambda i: (0,) * len(shape))
    tile = lambda cols: pl.BlockSpec((rows, cols), lambda i: (i, 0))
    return pl.pallas_call(
        functools.partial(feed_kernel, dps),
        grid=(length // rows,),
        in_specs=[SCALAR, tile(model), tile(model), whole(bias.shape)] + [ANY] * (2 * dps),
        out_specs=[tile(width), tile(width), tile(model), whole((1, width))],
        out_shape=[
            jax.ShapeDtypeStruct((length, width), BF),
            jax.ShapeDtypeStruct((length, width), BF),
            jax.ShapeDtypeStruct((length, model), BF),
            jax.ShapeDtypeStruct((1, width), F32),
        ],
        scratch_shapes=[
            pltpu.VMEM((dps, depth, width), BF),
            pltpu.VMEM((width, model), BF),
            pltpu.SemaphoreType.DMA((dps,)),
            pltpu.SemaphoreType.DMA,
        ],
        compiler_params=ROOM,
    )(where, n2, gm, bias, *fc, *proj)


def feed_grad_kernel(dps, where, n2_ref, gm_ref, e_ref, gu_ref, *rest):
    p_refs = rest[:dps]
    mlp_ref = rest[dps]
    f_outs, p_outs = rest[dps + 1 : 2 * dps + 1], rest[2 * dps + 1 : 3 * dps + 1]
    wp, df, dp_, sems, sems2 = rest[3 * dps + 1 :]
    width = wp.shape[0]
    size, start = piece_rows(width, dps)
    spots = [pl.ds(pl.multiple_of(start(where[0] ^ k), 16), size) for k in range(dps)]
    depth = df.shape[1]
    for p in range(dps):
        df[p] = mm_tn(n2_ref[:, p * depth : (p + 1) * depth], gu_ref[...]).astype(BF)
    copies = [
        pltpu.make_async_copy(df.at[where[0] ^ k], ref, sems.at[k]) for k, ref in enumerate(f_outs)
    ]
    for c in copies:
        c.start()
    for a in range(0, width, 256):
        b = min(width, a + 256)
        dp_[a:b, :] = mm_tn(e_ref[:, a:b], gm_ref[...]).astype(BF)
    more = [
        pltpu.make_async_copy(dp_.at[spots[k], :], ref, sems2.at[k])
        for k, ref in enumerate(p_outs)
    ]
    for c in more:
        c.start()
    for c in copies:
        c.wait()
    for k, ref in enumerate(p_refs):
        one = pltpu.make_async_copy(ref, wp.at[spots[k], :], sems.at[k])
        one.start()
        one.wait()
    rows = block_rows(e_ref.shape[0])
    for a in range(0, e_ref.shape[0], rows):
        mlp_ref[a : a + rows, :] = mm(e_ref[a : a + rows, :], wp[...]).astype(BF)
    for c in more:
        c.wait()


def feed_grad(where, n2, gm, e, gu, proj):
    length, model = n2.shape
    dps = len(proj)
    width = e.shape[1]
    depth = model // dps
    size, _ = piece_rows(width, dps)
    mlp, *chunks = pl.pallas_call(
        functools.partial(feed_grad_kernel, dps),
        in_specs=[SCALAR, WHOLE, WHOLE, WHOLE, WHOLE] + [ANY] * dps,
        out_specs=[WHOLE] + [ANY] * (2 * dps),
        out_shape=[jax.ShapeDtypeStruct((length, model), BF)]
        + [jax.ShapeDtypeStruct((depth, width), BF)] * dps
        + [jax.ShapeDtypeStruct((size, model), BF)] * dps,
        scratch_shapes=[
            pltpu.VMEM((width, model), BF),
            pltpu.VMEM((dps, depth, width), BF),
            pltpu.VMEM((width, model), BF),
            pltpu.SemaphoreType.DMA((dps,)),
            pltpu.SemaphoreType.DMA((dps,)),
        ],
        compiler_params=ROOM,
    )(where, n2, gm, e, gu, *proj)
    return mlp, chunks[:dps], chunks[dps:]


def last_kernel(gn1_ref, x_ref, gr_ref, vec_ref, out_ref):
    unit, inverse = normalise(x_ref[...].astype(F32))
    grad = norm_back(gn1_ref[...].astype(F32), unit, inverse, vec_ref[0:1, :])
    out_ref[...] = (gr_ref[...] + grad).astype(BF)


def last_norm(gn1, x, gr, table):
    return pl.pallas_call(
        last_kernel,
        in_specs=[WHOLE] * 4,
        out_specs=WHOLE,
        out_shape=jax.ShapeDtypeStruct(x.shape, BF),
        compiler_params=ROOM,
    )(gn1, x, gr, table)


def out_blocks(w_out):
    seqs = lax.axis_size("seq")
    line = [w_out] + [
        lax.ppermute(w_out, "seq", xor_perm(seqs, 2 * dz)) for dz in range(1, seqs // 2)
    ]
    near = gather_rel(jnp.stack(line), "dp")
    return [[b, lax.ppermute(b, "seq", xor_perm(seqs, 1))] for b in near]


def block_copies(where, blocks, store, sems, outward):
    copies = []
    for dk, pair in enumerate(blocks):
        for dc, ref in enumerate(pair):
            for dz in range(ref.shape[0]):
                near, far = ref.at[dz], store.at[where[0] ^ dk, where[1] ^ (2 * dz + dc)]
                src, dst = (far, near) if outward else (near, far)
                copies.append(pltpu.make_async_copy(src, dst, sems.at[len(copies)]))
    return copies


def head_columns(att_ref, owner):
    count = int(owner.max()) + 1
    parts = []
    for h in range(count):
        dev, slot = [int(i[0]) for i in np.where(owner == h)]
        parts.append(att_ref[dev, :, slot * HD : (slot + 1) * HD])
    return jnp.concatenate(parts, axis=1)


def out_kernel(dps, seqs, owner, where, att_ref, x_ref, vec_ref, *rest):
    flat = rest[: 2 * dps]
    r_ref, n2_ref, store, sems = rest[2 * dps :]
    blocks = [flat[2 * k : 2 * k + 2] for k in range(dps)]
    copies = block_copies(where, blocks, store, sems, False)
    for c in copies:
        c.start()
    att = head_columns(att_ref, owner)
    depth, width = store.shape[2:]
    for c in copies:
        c.wait()
    for n in range(seqs):
        here = slice(n * width, (n + 1) * width)
        total = x_ref[:, here].astype(F32) + vec_ref[4:5, here]
        for p in range(dps):
            total = total + mm(att[:, p * depth : (p + 1) * depth], store[p, n])
        r_ref[:, here] = total
    unit, _ = normalise(r_ref[...])
    n2_ref[...] = (unit * vec_ref[5:6, :] + vec_ref[6:7, :]).astype(BF)


def out_project(where, att, x, table, blocks, owner):
    flat = [b for pair in blocks for b in pair]
    dps, seqs = len(blocks), att.shape[0]
    depth, width = flat[0].shape[1:]
    return pl.pallas_call(
        functools.partial(out_kernel, dps, seqs, owner),
        in_specs=[SCALAR, WHOLE, WHOLE, WHOLE] + [ANY] * len(flat),
        out_specs=[WHOLE, WHOLE],
        out_shape=[jax.ShapeDtypeStruct(x.shape, F32), jax.ShapeDtypeStruct(x.shape, BF)],
        scratch_shapes=[
            pltpu.VMEM((dps, seqs, depth, width), BF),
            pltpu.SemaphoreType.DMA((dps * seqs,)),
        ],
        compiler_params=ROOM,
    )(where, att, x, table, *flat)


def back_kernel(dps, seqs, owner, where, gn2_ref, r_ref, g_ref, vec_ref, *rest):
    flat = rest[: 2 * dps]
    gr_ref, go_ref, ga_ref, sums_ref, store, sems = rest[2 * dps :]
    blocks = [flat[2 * k : 2 * k + 2] for k in range(dps)]
    copies = block_copies(where, blocks, store, sems, False)
    for c in copies:
        c.start()
    depth, width = store.shape[2:]
    gn2 = gn2_ref[...].astype(F32)
    unit, inverse = normalise(r_ref[...])
    gr = g_ref[...].astype(F32) + norm_back(gn2, unit, inverse, vec_ref[5:6, :])
    go = gr.astype(BF)
    gr_ref[...] = gr
    go_ref[...] = go
    sums_ref[0:1, :] = jnp.sum(go.astype(F32), axis=0, keepdims=True)
    sums_ref[1:2, :] = jnp.sum(gn2 * unit, axis=0, keepdims=True)
    sums_ref[2:3, :] = jnp.sum(gn2, axis=0, keepdims=True)
    sums_ref[3:4, :] = jnp.sum(g_ref[...].astype(F32), axis=0, keepdims=True)
    for c in copies:
        c.wait()
    parts = []
    for p in range(dps):
        total = mm_nt(go[:, 0:width], store[p, 0])
        for n in range(1, seqs):
            total = total + mm_nt(go[:, n * width : (n + 1) * width], store[p, n])
        parts.append(total)
    ga = jnp.concatenate(parts, axis=1).astype(BF)
    ga_ref[...] = jnp.zeros_like(ga_ref)
    for h in range(int(owner.max()) + 1):
        dev, slot = [int(i[0]) for i in np.where(owner == h)]
        ga_ref[dev, :, slot * HD : (slot + 1) * HD] = ga[:, h * HD : (h + 1) * HD]


def out_back(where, gn2, r, g, table, blocks, owner):
    flat = [b for pair in blocks for b in pair]
    dps, seqs = len(blocks), owner.shape[0]
    depth, width = flat[0].shape[1:]
    return pl.pallas_call(
        functools.partial(back_kernel, dps, seqs, owner),
        in_specs=[SCALAR, WHOLE, WHOLE, WHOLE, WHOLE] + [ANY] * len(flat),
        out_specs=[WHOLE] * 4,
        out_shape=[
            jax.ShapeDtypeStruct(r.shape, F32),
            jax.ShapeDtypeStruct(r.shape, BF),
            jax.ShapeDtypeStruct((seqs, r.shape[0], owner.shape[1] * HD), BF),
            jax.ShapeDtypeStruct((4, r.shape[1]), F32),
        ],
        scratch_shapes=[
            pltpu.VMEM((dps, seqs, depth, width), BF),
            pltpu.SemaphoreType.DMA((dps * seqs,)),
        ],
        compiler_params=ROOM,
    )(where, gn2, r, g, table, *flat)


def grad_out_kernel(dps, seqs, owner, where, att_ref, go_ref, *rest):
    flat = rest[: 2 * dps]
    store, sems = rest[2 * dps :]
    blocks = [flat[2 * k : 2 * k + 2] for k in range(dps)]
    att = head_columns(att_ref, owner)
    depth, width = store.shape[2:]
    for p in range(dps):
        rows = att[:, p * depth : (p + 1) * depth]
        for n in range(seqs):
            store[p, n] = mm_tn(rows, go_ref[:, n * width : (n + 1) * width]).astype(BF)
    copies = block_copies(where, blocks, store, sems, True)
    for c in copies:
        c.start()
    for c in copies:
        c.wait()


def grad_out(where, att, go, dps, owner):
    seqs = att.shape[0]
    depth, width = go.shape[1] // dps, go.shape[1] // seqs
    shape = jax.ShapeDtypeStruct((seqs // 2, depth, width), BF)
    flat = pl.pallas_call(
        functools.partial(grad_out_kernel, dps, seqs, owner),
        in_specs=[SCALAR, WHOLE, WHOLE],
        out_specs=[ANY] * (2 * dps),
        out_shape=[shape] * (2 * dps),
        scratch_shapes=[
            pltpu.VMEM((dps, seqs, depth, width), BF),
            pltpu.SemaphoreType.DMA((dps * seqs,)),
        ],
        compiler_params=ROOM,
    )(where, att, go)
    return [flat[2 * k : 2 * k + 2] for k in range(dps)]


def sum_out_blocks(blocks):
    seqs = lax.axis_size("seq")
    chip = [
        (mine.astype(F32) + lax.ppermute(other, "seq", xor_perm(seqs, 1)).astype(F32)).astype(BF)
        for mine, other in blocks
    ]
    line = scatter_rel(chip, "dp").astype(BF)
    total = line[0].astype(F32)
    for dz in range(1, seqs // 2):
        total = total + lax.ppermute(line[dz], "seq", xor_perm(seqs, 2 * dz)).astype(F32)
    return total


def sum_all(block):
    for axis in ("dp", "seq"):
        step = 1
        while step < lax.axis_size(axis):
            block = block + lax.ppermute(block, axis, xor_perm(lax.axis_size(axis), step))
            step *= 2
    return block


def body(tokens, w_qkv, w_out, vectors, w_fc, b_fc, w_proj, cotangent):
    dps = lax.axis_size("dp")
    seqs = lax.axis_size("seq")
    dp = lax.axis_index("dp")
    sq = lax.axis_index("seq")
    rows, model = tokens.shape
    head_count = model // HD
    slots, owner, wide, send, recv = head_plan(head_count, seqs, w_qkv.shape[1])
    mine = slots * HD
    ff_mine = w_fc.shape[1]
    ratio = seqs // dps
    col = w_proj.shape[1]

    per, wide_vec = vectors.shape
    small = gather_small(jnp.concatenate([vectors.reshape(-1), b_fc])[None], "dp")
    small = gather_small(small, "seq").astype(F32)[:, :, 0]
    table = small[:, :, : per * wide_vec].reshape(seqs, dps, per, wide_vec)
    table = table.transpose(1, 2, 0, 3).reshape(dps * per, model)
    gain1, shift1, bias_q, bias_v, bias_o, gain2, shift2, bias_p = [table[i] for i in range(8)]
    bias_fc = small[:, :, per * wide_vec :].transpose(1, 0, 2).reshape(-1)
    bias_fc = lax.dynamic_slice_in_dim(bias_fc, sq * ff_mine, ff_mine)
    own_heads = jnp.asarray(owner)[sq]
    pick = (own_heads[:, None] == jnp.arange(head_count)[None, :]).astype(F32)

    def head_rows(vector):
        return jnp.sum(pick[:, :, None] * vector.reshape(1, head_count, HD), axis=1).reshape(-1)

    def head_spread(vector):
        return jnp.sum(pick[:, :, None] * vector.reshape(slots, 1, HD), axis=0).reshape(-1)

    bias_qkv = jnp.concatenate([head_rows(bias_q), jnp.zeros((mine,), F32), head_rows(bias_v)])

    to_send = (jnp.arange(w_qkv.shape[1])[:, None, None] == jnp.asarray(send)[sq][None]).astype(BF)
    to_recv = (
        lax.dynamic_index_in_dim(jnp.asarray(recv), sq, 1, keepdims=False)[:, :, None]
        == jnp.arange(3 * mine)[None, None]
    ).astype(BF)
    parts = jnp.einsum("ac,cnw->naw", w_qkv, to_send, preferred_element_type=F32).astype(BF)
    parts = lax.all_to_all(parts, "seq", 0, 0, tiled=True)
    own_qkv = jnp.einsum("naw,nwd->ad", parts, to_recv, preferred_element_type=F32).astype(BF)
    wf = gather_rel(w_fc, "dp")

    size, start = piece_rows(ff_mine, dps)
    pieces = w_proj.reshape(ratio, ff_mine, col)
    pieces = jnp.stack([pieces[:, start(q) : start(q) + size] for q in range(dps)])
    pieces = lax.all_to_all(pieces, "dp", 0, 0, tiled=True)
    pieces = lax.all_to_all(pieces.reshape(seqs, size, col), "seq", 0, 0, tiled=True)
    wp = gather_rel(pieces.transpose(1, 0, 2).reshape(size, model), "dp")

    where = jnp.stack([dp, sq]).astype(jnp.int32)
    wo = out_blocks(w_out)

    x_all = lax.all_gather(tokens, "seq", axis=0, tiled=True)
    cot, own_qkv = lax.optimization_barrier((cotangent, own_qkv))
    gm_all = lax.all_gather(cot, "seq", axis=0, tiled=True)
    wq = gather_rel(own_qkv, "dp")
    n1_all, qkv, att, lse = attend(where, x_all, table, bias_qkv[None], wq, slots, rows)
    att = lax.all_to_all(att, "seq", 0, 0, tiled=True)
    r, n2 = out_project(where, att, tokens, table, wo, owner)
    n2_all = lax.all_gather(n2, "seq", axis=0, tiled=True)

    e, gu, gn2_part, sum_fc = feed(where, n2_all, gm_all, bias_fc[None], wf, wp)
    gn2 = lax.psum_scatter(gn2_part, "seq", scatter_dimension=0, tiled=True)
    mlp, d_fc, d_proj = feed_grad(where, n2_all, gm_all, e, gu, wp)
    gn2, mlp = lax.optimization_barrier((gn2, mlp))
    mlp = lax.psum_scatter(mlp, "seq", scatter_dimension=0, tiled=True)
    activations = (r + (mlp.astype(F32) + bias_p)).astype(BF)

    gr, go, ga, sums_two = out_back(where, gn2, r, cotangent, table, wo, owner)
    ga = lax.all_to_all(ga, "seq", 0, 0, tiled=True)
    d_out = grad_out(where, att, go, dps, owner)
    gqkv, gn1_part = attend_back(where, qkv, ga, lse, wq)
    gn1 = lax.psum_scatter(gn1_part, "seq", scatter_dimension=0, tiled=True)
    d_qkv, gqkv_sums, norm_sums = grad_qkv(where, n1_all, gqkv, gn1_part, dps)
    input_grad = last_norm(gn1, tokens, gr, table)

    g_fc = scatter_rel(d_fc, "dp")
    g_qkv = scatter_rel(d_qkv, "dp").astype(BF)
    parts = jnp.einsum("ad,nwd->naw", g_qkv, to_recv, preferred_element_type=F32).astype(BF)
    parts = lax.all_to_all(parts, "seq", 0, 0, tiled=True)
    g_qkv = jnp.einsum("naw,cnw->ac", parts, to_send, preferred_element_type=F32)

    g_proj = scatter_rel(d_proj, "dp").astype(BF)
    g_proj = g_proj.reshape(size, seqs, col).transpose(1, 0, 2)
    g_proj = lax.all_to_all(g_proj, "seq", 0, 0, tiled=True)
    g_proj = g_proj.reshape(dps, ratio, size, col)
    g_proj = lax.all_to_all(g_proj, "dp", 0, 0, tiled=True)
    ends = [start(q) for q in range(dps)] + [ff_mine]
    g_proj = jnp.concatenate(
        [g_proj[q, :, : ends[q + 1] - ends[q]] for q in range(dps)], axis=1
    )
    g_proj = g_proj.reshape(w_proj.shape).astype(F32)

    g_out = sum_out_blocks(d_out)

    vector_grads = jnp.concatenate(
        [
            ((norm_sums[0] - shift1 * norm_sums[1]) / gain1)[None],
            norm_sums[1:],
            head_spread(gqkv_sums[0, :mine])[None],
            head_spread(gqkv_sums[0, 2 * mine :])[None],
            sums_two,
        ]
    )
    fc_sums = lax.dynamic_update_slice_in_dim(
        jnp.zeros((dps * seqs * b_fc.shape[0],), F32), sum_fc[0], sq * ff_mine, axis=0
    ).reshape(-1, model)
    sums = sum_all(jnp.concatenate([vector_grads, fc_sums]))
    own_vec = lax.dynamic_slice(sums, (dp * per, sq * wide_vec), (per, wide_vec))
    own_fc = lax.dynamic_slice_in_dim(
        sums[8:].reshape(-1), (dp * seqs + sq) * b_fc.shape[0], b_fc.shape[0]
    )
    return (
        activations,
        input_grad,
        g_qkv,
        g_out,
        own_vec,
        g_fc,
        own_fc,
        g_proj,
    )


def solution(mesh):
    rows = P(("dp", "seq"), None)
    grid = P("dp", "seq")
    line = P(("dp", "seq"))
    return jax.shard_map(
        body,
        mesh=mesh,
        in_specs=(rows, grid, grid, grid, grid, line, grid, rows),
        out_specs=(rows, rows, grid, grid, grid, grid, line, grid),
        check_vma=False,
    )
```

```python
import functools
import math

import jax
import jax.numpy as jnp
import numpy as np
from jax import lax
from jax.experimental import pallas as pl
from jax.experimental.pallas import tpu as pltpu
from jax.sharding import PartitionSpec as P

HD = 64
PAIR = 2 * HD
EPSILON = 1e-05
GELU_C = 0.7978845608028654
NEG_FILL = -1e30
BF = jnp.bfloat16
F32 = jnp.float32


def head_plan(head_count, seq_count, width):
    slots = -(-head_count // seq_count)
    slots += slots % 2
    model = head_count * HD

    def tables(turn):
        owner = np.full((seq_count, slots), -1, np.int32)
        for head in range(head_count):
            row = head // seq_count
            owner[(head + turn * row) % seq_count, row] = head
        place = {}
        for dev in range(seq_count):
            for slot in range(slots):
                if owner[dev, slot] >= 0:
                    place[int(owner[dev, slot])] = (dev, slot)
        lists = [[[] for _ in range(seq_count)] for _ in range(seq_count)]
        for col in range(3 * model):
            kind, rest = divmod(col, model)
            head, lane = divmod(rest, HD)
            dev, slot = place[head]
            src, local = divmod(col, width)
            lists[src][dev].append((local, (kind * slots + slot) * HD + lane))
        most = max(len(cell) for row in lists for cell in row)
        return most, owner, lists

    best = min((tables(turn) for turn in range(seq_count)), key=lambda t: t[0])
    most, owner, lists = best
    wide = -(-most // 128) * 128
    send = np.full((seq_count, seq_count, wide), -1, np.int32)
    recv = np.full((seq_count, seq_count, wide), -1, np.int32)
    for src in range(seq_count):
        for dev in range(seq_count):
            for i, (local, target) in enumerate(lists[src][dev]):
                send[src, dev, i] = local
                recv[src, dev, i] = target
    return slots, owner, wide, send, recv


def xor_perm(count, k):
    return [(i, i ^ k) for i in range(count)]


def after(value, *others):
    return lax.optimization_barrier((value, *others))[0]


def gather_rel(block, axis):
    count = lax.axis_size(axis)
    return [block] + [lax.ppermute(block, axis, xor_perm(count, k)) for k in range(1, count)]


def scatter_rel(chunks, axis):
    count = lax.axis_size(axis)
    total = chunks[0].astype(F32)
    for k in range(1, count):
        total = total + lax.ppermute(chunks[k], axis, xor_perm(count, k)).astype(F32)
    return total


def gather_small(block, axis):
    count = lax.axis_size(axis)
    me = lax.axis_index(axis)
    stack = block[None]
    step = 1
    while step < count:
        other = lax.ppermute(stack, axis, xor_perm(count, step))
        low = (me & step) == 0
        stack = jnp.where(
            low, jnp.concatenate([stack, other]), jnp.concatenate([other, stack])
        )
        step *= 2
    return stack


ANY = pl.BlockSpec(memory_space=pl.ANY)
WHOLE = pl.BlockSpec(memory_space=pltpu.VMEM)
SCALAR = pl.BlockSpec(memory_space=pltpu.SMEM)
ROOM = pltpu.CompilerParams(vmem_limit_bytes=56 * 1024 * 1024)


def normalise(rows):
    mean = jnp.mean(rows, axis=-1, keepdims=True)
    centred = rows - mean
    inverse = lax.rsqrt(jnp.mean(centred * centred, axis=-1, keepdims=True) + EPSILON)
    return centred * inverse, inverse


def norm_back(grad, unit, inverse, gain):
    scaled = grad * gain
    return (
        scaled
        - jnp.mean(scaled, axis=-1, keepdims=True)
        - unit * jnp.mean(scaled * unit, axis=-1, keepdims=True)
    ) * inverse


def gelu_parts(u):
    cube = u * u * u
    t = jnp.tanh(GELU_C * (u + 0.044715 * cube))
    value = 0.5 * u * (1.0 + t)
    slope = 0.5 * (1.0 + t) + 0.5 * u * (1.0 - t * t) * GELU_C * (1.0 + 3 * 0.044715 * u * u)
    return value, slope


def mm(a, b):
    return jnp.dot(a, b, preferred_element_type=F32)


def mm_nt(a, b):
    return lax.dot_general(a, b, (((1,), (1,)), ((), ())), preferred_element_type=F32)


def mm_tn(a, b):
    return lax.dot_general(a, b, (((0,), (0,)), ((), ())), preferred_element_type=F32)


def block_rows(length):
    return math.gcd(length, 256)


def head_masks(rows):
    first = lax.broadcasted_iota(jnp.int32, (rows, PAIR), 1) < HD
    causal = lax.broadcasted_iota(jnp.int32, (rows, rows), 0) >= lax.broadcasted_iota(
        jnp.int32, (rows, rows), 1
    )
    return first, causal


def masked_scores(q, keys, causal):
    rows, seen = q.shape[0], keys.shape[0]
    s = mm_nt(q, keys)
    tail = jnp.where(causal, s[:, seen - rows :], NEG_FILL)
    return tail if seen == rows else jnp.concatenate([s[:, : seen - rows], tail], axis=1)


def attend_rows(q, keys, values, first, causal):
    q = q * BF(1.0 / math.sqrt(HD))
    outs, logs = [], []
    for mine in (first, ~first):
        s = masked_scores(jnp.where(mine, q, BF(0)), keys, causal)
        top = jnp.max(s, axis=-1, keepdims=True)
        e = jnp.exp(s - top)
        total = jnp.sum(e, axis=-1, keepdims=True)
        outs.append(mm(e.astype(BF), values) / total)
        logs.append(top + jnp.log(total))
    return jnp.where(first, outs[0], outs[1]).astype(BF), jnp.where(first, logs[0], logs[1])


def row_blocks_in(where, refs, store, sems):
    copies = [
        pltpu.make_async_copy(ref, store.at[where[0] ^ k], sems.at[k])
        for k, ref in enumerate(refs)
    ]
    for c in copies:
        c.start()
    return copies


def right_blocks(rows, store):
    count, depth = store.shape[:2]
    total = mm(rows[:, :depth], store[0])
    for p in range(1, count):
        total = total + mm(rows[:, p * depth : (p + 1) * depth], store[p])
    return total


def attend_kernel(dps, pairs, where, x_ref, vec_ref, bias_ref, *rest):
    w_refs = rest[:dps]
    n1_ref, qkv_ref, att_ref, lse_ref, w, qkv, sems = rest[dps:]
    i = pl.program_id(0)
    rows = x_ref.shape[0]
    steps = qkv.shape[0] // rows

    @pl.when(i == 0)
    def _():
        for c in row_blocks_in(where, w_refs, w, sems):
            c.wait()

    unit, _ = normalise(x_ref[...].astype(F32))
    n1 = (unit * vec_ref[0:1, :] + vec_ref[1:2, :]).astype(BF)
    n1_ref[...] = n1
    tile = (right_blocks(n1, w) + bias_ref[...]).astype(BF)
    qkv_ref[...] = tile
    qkv[pl.ds(pl.multiple_of(i * rows, rows), rows), :] = tile
    first, causal = head_masks(rows)
    part = att_ref.shape[1]
    for j in range(steps):

        @pl.when(i == j)
        def _(j=j):
            seen = (j + 1) * rows
            for g in range(pairs):
                lanes = slice(g * PAIR, (g + 1) * PAIR)
                keys = qkv[0:seen, (pairs + g) * PAIR : (pairs + g + 1) * PAIR]
                values = qkv[0:seen, (2 * pairs + g) * PAIR : (2 * pairs + g + 1) * PAIR]
                out, log = attend_rows(
                    qkv[j * rows : seen, lanes], keys, values, first, causal
                )
                for b in range(rows // part):
                    att_ref[b, :, lanes] = out[b * part : (b + 1) * part]
                lse_ref[:, lanes] = log


def attend(where, x_all, table, bias, weights, slots, part):
    length, model = x_all.shape
    dps = len(weights)
    depth, width = weights[0].shape
    mine = slots * HD
    rows = block_rows(length)
    whole = lambda shape: pl.BlockSpec(shape, lambda i: (0,) * len(shape))
    tile = lambda cols: pl.BlockSpec((rows, cols), lambda i: (i, 0))
    return pl.pallas_call(
        functools.partial(attend_kernel, dps, mine // PAIR),
        grid=(length // rows,),
        in_specs=[SCALAR, tile(model), whole(table.shape), whole(bias.shape)] + [ANY] * dps,
        out_specs=[
            tile(model),
            tile(width),
            pl.BlockSpec((rows // part, part, mine), lambda i: (i, 0, 0)),
            tile(mine),
        ],
        out_shape=[
            jax.ShapeDtypeStruct((length, model), BF),
            jax.ShapeDtypeStruct((length, width), BF),
            jax.ShapeDtypeStruct((length // part, part, mine), BF),
            jax.ShapeDtypeStruct((length, mine), F32),
        ],
        scratch_shapes=[
            pltpu.VMEM((dps, depth, width), BF),
            pltpu.VMEM((length, width), BF),
            pltpu.SemaphoreType.DMA((dps,)),
        ],
        compiler_params=ROOM,
    )(where, x_all, table, bias, *weights)


def attend_back_kernel(dps, pairs, where, qkv_ref, ga_ref, lse_ref, *rest):
    w_refs = rest[:dps]
    gqkv_ref, gn1_ref, w, ak, av, sems = rest[dps:]
    length = qkv_ref.shape[0]
    rows = block_rows(length)
    copies = row_blocks_in(where, w_refs, w, sems)
    first, causal = head_masks(rows)
    part = ga_ref.shape[1]
    for g in range(pairs):
        lanes = slice(g * PAIR, (g + 1) * PAIR)
        k_lanes = slice((pairs + g) * PAIR, (pairs + g + 1) * PAIR)
        v_lanes = slice((2 * pairs + g) * PAIR, (2 * pairs + g + 1) * PAIR)
        ak[...] = jnp.zeros_like(ak)
        av[...] = jnp.zeros_like(av)
        for i in range(length // rows):
            here = slice(i * rows, (i + 1) * rows)
            seen = (i + 1) * rows
            q = qkv_ref[here, lanes] * BF(1.0 / math.sqrt(HD))
            ga = jnp.concatenate(
                [ga_ref[b, :, lanes] for b in range(i * rows // part, seen // part)], axis=0
            )
            keys = qkv_ref[0:seen, k_lanes]
            values = qkv_ref[0:seen, v_lanes]
            grads = []
            for h, mine in enumerate((first, ~first)):
                q_h = jnp.where(mine, q, BF(0))
                ga_h = jnp.where(mine, ga, BF(0))
                s = masked_scores(q_h, keys, causal)
                lane = g * PAIR + h * HD
                p = jnp.exp(s - lse_ref[here, lane : lane + 1])
                gp = mm_nt(ga_h, values)
                centre = jnp.sum(p * gp, axis=-1, keepdims=True)
                gs = (p * (gp - centre)).astype(BF)
                av[0:seen, :] += mm_tn(p.astype(BF), ga_h)
                ak[0:seen, :] += mm_tn(gs, q_h)
                grads.append(mm(gs, keys))
            gqkv_ref[here, lanes] = (
                jnp.where(first, grads[0], grads[1]) * (1.0 / math.sqrt(HD))
            ).astype(BF)
        gqkv_ref[:, k_lanes] = ak[...].astype(BF)
        gqkv_ref[:, v_lanes] = av[...].astype(BF)
    for c in copies:
        c.wait()
    depth = w.shape[1]
    for i in range(length // rows):
        here = slice(i * rows, (i + 1) * rows)
        for p in range(dps):
            gn1_ref[here, p * depth : (p + 1) * depth] = mm_nt(gqkv_ref[here, :], w[p]).astype(BF)


def attend_back(where, qkv, grad, lse, weights):
    length, width = qkv.shape
    dps = len(weights)
    depth = weights[0].shape[0]
    return pl.pallas_call(
        functools.partial(attend_back_kernel, dps, grad.shape[2] // PAIR),
        in_specs=[SCALAR, WHOLE, WHOLE, WHOLE] + [ANY] * dps,
        out_specs=[WHOLE, WHOLE],
        out_shape=[
            jax.ShapeDtypeStruct((length, width), BF),
            jax.ShapeDtypeStruct((length, dps * depth), BF),
        ],
        scratch_shapes=[
            pltpu.VMEM((dps, depth, width), BF),
            pltpu.VMEM((length, PAIR), F32),
            pltpu.VMEM((length, PAIR), F32),
            pltpu.SemaphoreType.DMA((dps,)),
        ],
        compiler_params=ROOM,
    )(where, qkv, grad, lse, *weights)


def grad_qkv_kernel(dps, where, n1_ref, gqkv_ref, gn1_ref, *rest):
    outs = rest[:dps]
    sums_ref, norm_ref, store, sems = rest[dps:]
    depth = store.shape[1]
    gqkv = gqkv_ref[...]
    for p in range(dps):
        store[p] = mm_tn(n1_ref[:, p * depth : (p + 1) * depth], gqkv).astype(BF)
    copies = [
        pltpu.make_async_copy(store.at[where[0] ^ k], ref, sems.at[k])
        for k, ref in enumerate(outs)
    ]
    for c in copies:
        c.start()
    sums_ref[...] = jnp.sum(gqkv.astype(F32), axis=0, keepdims=True)
    gn1 = gn1_ref[...].astype(F32)
    norm_ref[0:1, :] = jnp.sum(gn1 * n1_ref[...].astype(F32), axis=0, keepdims=True)
    norm_ref[1:2, :] = jnp.sum(gn1, axis=0, keepdims=True)
    for c in copies:
        c.wait()


def grad_qkv(where, n1, gqkv, gn1, dps):
    model, width = n1.shape[1], gqkv.shape[1]
    depth = model // dps
    *chunks, sums, norm = pl.pallas_call(
        functools.partial(grad_qkv_kernel, dps),
        in_specs=[SCALAR, WHOLE, WHOLE, WHOLE],
        out_specs=[ANY] * dps + [WHOLE, WHOLE],
        out_shape=[jax.ShapeDtypeStruct((depth, width), BF)] * dps
        + [jax.ShapeDtypeStruct((1, width), F32), jax.ShapeDtypeStruct((2, model), F32)],
        scratch_shapes=[pltpu.VMEM((dps, depth, width), BF), pltpu.SemaphoreType.DMA((dps,))],
        compiler_params=ROOM,
    )(where, n1, gqkv, gn1)
    return chunks, sums, norm


def piece_rows(total, count):
    tiles = total // 16
    return 16 * -(-tiles // count), lambda q: 16 * ((q * tiles) // count)


def feed_kernel(dps, where, n2_ref, gm_ref, bias_ref, *rest):
    f_refs, p_refs = rest[:dps], rest[dps : 2 * dps]
    e_ref, gu_ref, gn2_ref, sum_ref, wf, wp, sems, sems2 = rest[2 * dps :]
    i = pl.program_id(0)
    size, start = piece_rows(wp.shape[0], dps)

    @pl.when(i == 0)
    def _():
        copies = row_blocks_in(where, f_refs, wf, sems)
        for k, ref in enumerate(p_refs):
            here = pl.ds(pl.multiple_of(start(where[0] ^ k), 16), size)
            one = pltpu.make_async_copy(ref, wp.at[here, :], sems2)
            one.start()
            one.wait()
        for c in copies:
            c.wait()
        sum_ref[...] = jnp.zeros_like(sum_ref)

    u = right_blocks(n2_ref[...], wf) + bias_ref[...]
    ge = mm_nt(gm_ref[...], wp[...])
    value, slope = gelu_parts(u)
    e_ref[...] = value.astype(BF)
    gu = (ge * slope).astype(BF)
    gu_ref[...] = gu
    sum_ref[...] += jnp.sum(gu.astype(F32), axis=0, keepdims=True)
    depth = wf.shape[1]
    for p in range(dps):
        gn2_ref[:, p * depth : (p + 1) * depth] = mm_nt(gu, wf[p]).astype(BF)


def feed(where, n2, gm, bias, fc, proj):
    length, model = n2.shape
    dps = len(fc)
    depth, width = fc[0].shape
    rows = block_rows(length)
    whole = lambda shape: pl.BlockSpec(shape, lambda i: (0,) * len(shape))
    tile = lambda cols: pl.BlockSpec((rows, cols), lambda i: (i, 0))
    return pl.pallas_call(
        functools.partial(feed_kernel, dps),
        grid=(length // rows,),
        in_specs=[SCALAR, tile(model), tile(model), whole(bias.shape)] + [ANY] * (2 * dps),
        out_specs=[tile(width), tile(width), tile(model), whole((1, width))],
        out_shape=[
            jax.ShapeDtypeStruct((length, width), BF),
            jax.ShapeDtypeStruct((length, width), BF),
            jax.ShapeDtypeStruct((length, model), BF),
            jax.ShapeDtypeStruct((1, width), F32),
        ],
        scratch_shapes=[
            pltpu.VMEM((dps, depth, width), BF),
            pltpu.VMEM((width, model), BF),
            pltpu.SemaphoreType.DMA((dps,)),
            pltpu.SemaphoreType.DMA,
        ],
        compiler_params=ROOM,
    )(where, n2, gm, bias, *fc, *proj)


def feed_grad_kernel(dps, where, n2_ref, gm_ref, e_ref, gu_ref, *rest):
    p_refs = rest[:dps]
    mlp_ref = rest[dps]
    f_outs, p_outs = rest[dps + 1 : 2 * dps + 1], rest[2 * dps + 1 : 3 * dps + 1]
    wp, df, dp_, sems, sems2 = rest[3 * dps + 1 :]
    width = wp.shape[0]
    size, start = piece_rows(width, dps)
    spots = [pl.ds(pl.multiple_of(start(where[0] ^ k), 16), size) for k in range(dps)]
    depth = df.shape[1]
    for p in range(dps):
        df[p] = mm_tn(n2_ref[:, p * depth : (p + 1) * depth], gu_ref[...]).astype(BF)
    copies = [
        pltpu.make_async_copy(df.at[where[0] ^ k], ref, sems.at[k]) for k, ref in enumerate(f_outs)
    ]
    for c in copies:
        c.start()
    for a in range(0, width, 256):
        b = min(width, a + 256)
        dp_[a:b, :] = mm_tn(e_ref[:, a:b], gm_ref[...]).astype(BF)
    more = [
        pltpu.make_async_copy(dp_.at[spots[k], :], ref, sems2.at[k])
        for k, ref in enumerate(p_outs)
    ]
    for c in more:
        c.start()
    for c in copies:
        c.wait()
    for k, ref in enumerate(p_refs):
        one = pltpu.make_async_copy(ref, wp.at[spots[k], :], sems.at[k])
        one.start()
        one.wait()
    rows = block_rows(e_ref.shape[0])
    for a in range(0, e_ref.shape[0], rows):
        mlp_ref[a : a + rows, :] = mm(e_ref[a : a + rows, :], wp[...]).astype(BF)
    for c in more:
        c.wait()


def feed_grad(where, n2, gm, e, gu, proj):
    length, model = n2.shape
    dps = len(proj)
    width = e.shape[1]
    depth = model // dps
    size, _ = piece_rows(width, dps)
    mlp, *chunks = pl.pallas_call(
        functools.partial(feed_grad_kernel, dps),
        in_specs=[SCALAR, WHOLE, WHOLE, WHOLE, WHOLE] + [ANY] * dps,
        out_specs=[WHOLE] + [ANY] * (2 * dps),
        out_shape=[jax.ShapeDtypeStruct((length, model), BF)]
        + [jax.ShapeDtypeStruct((depth, width), BF)] * dps
        + [jax.ShapeDtypeStruct((size, model), BF)] * dps,
        scratch_shapes=[
            pltpu.VMEM((width, model), BF),
            pltpu.VMEM((dps, depth, width), BF),
            pltpu.VMEM((width, model), BF),
            pltpu.SemaphoreType.DMA((dps,)),
            pltpu.SemaphoreType.DMA((dps,)),
        ],
        compiler_params=ROOM,
    )(where, n2, gm, e, gu, *proj)
    return mlp, chunks[:dps], chunks[dps:]


def last_kernel(gn1_ref, x_ref, gr_ref, vec_ref, out_ref):
    unit, inverse = normalise(x_ref[...].astype(F32))
    grad = norm_back(gn1_ref[...].astype(F32), unit, inverse, vec_ref[0:1, :])
    out_ref[...] = (gr_ref[...] + grad).astype(BF)


def last_norm(gn1, x, gr, table):
    return pl.pallas_call(
        last_kernel,
        in_specs=[WHOLE] * 4,
        out_specs=WHOLE,
        out_shape=jax.ShapeDtypeStruct(x.shape, BF),
        compiler_params=ROOM,
    )(gn1, x, gr, table)


def line_blocks(block):
    seqs = lax.axis_size("seq")
    return jnp.stack(
        [block]
        + [lax.ppermute(block, "seq", xor_perm(seqs, 2 * dz)) for dz in range(1, seqs // 2)]
    )


def out_blocks(line):
    seqs = lax.axis_size("seq")
    return [[b, lax.ppermute(b, "seq", xor_perm(seqs, 1))] for b in gather_rel(line, "dp")]


def block_copies(where, blocks, store, sems, outward):
    copies = []
    for dk, pair in enumerate(blocks):
        for dc, ref in enumerate(pair):
            for dz in range(ref.shape[0]):
                near, far = ref.at[dz], store.at[where[0] ^ dk, where[1] ^ (2 * dz + dc)]
                src, dst = (far, near) if outward else (near, far)
                copies.append(pltpu.make_async_copy(src, dst, sems.at[len(copies)]))
    return copies


def head_columns(att_ref, owner):
    count = int(owner.max()) + 1
    parts = []
    for h in range(count):
        dev, slot = [int(i[0]) for i in np.where(owner == h)]
        parts.append(att_ref[dev, :, slot * HD : (slot + 1) * HD])
    return jnp.concatenate(parts, axis=1)


def out_kernel(dps, seqs, owner, where, att_ref, x_ref, vec_ref, *rest):
    flat = rest[: 2 * dps]
    r_ref, n2_ref, store, sems = rest[2 * dps :]
    blocks = [flat[2 * k : 2 * k + 2] for k in range(dps)]
    copies = block_copies(where, blocks, store, sems, False)
    for c in copies:
        c.start()
    att = head_columns(att_ref, owner)
    depth, width = store.shape[2:]
    for c in copies:
        c.wait()
    for n in range(seqs):
        here = slice(n * width, (n + 1) * width)
        total = x_ref[:, here].astype(F32) + vec_ref[4:5, here]
        for p in range(dps):
            total = total + mm(att[:, p * depth : (p + 1) * depth], store[p, n])
        r_ref[:, here] = total
    unit, _ = normalise(r_ref[...])
    n2_ref[...] = (unit * vec_ref[5:6, :] + vec_ref[6:7, :]).astype(BF)


def out_project(where, att, x, table, blocks, owner):
    flat = [b for pair in blocks for b in pair]
    dps, seqs = len(blocks), att.shape[0]
    depth, width = flat[0].shape[1:]
    return pl.pallas_call(
        functools.partial(out_kernel, dps, seqs, owner),
        in_specs=[SCALAR, WHOLE, WHOLE, WHOLE] + [ANY] * len(flat),
        out_specs=[WHOLE, WHOLE],
        out_shape=[jax.ShapeDtypeStruct(x.shape, F32), jax.ShapeDtypeStruct(x.shape, BF)],
        scratch_shapes=[
            pltpu.VMEM((dps, seqs, depth, width), BF),
            pltpu.SemaphoreType.DMA((dps * seqs,)),
        ],
        compiler_params=ROOM,
    )(where, att, x, table, *flat)


def back_kernel(dps, seqs, owner, where, gn2_ref, r_ref, g_ref, vec_ref, *rest):
    flat = rest[: 2 * dps]
    gr_ref, go_ref, ga_ref, sums_ref, store, sems = rest[2 * dps :]
    blocks = [flat[2 * k : 2 * k + 2] for k in range(dps)]
    copies = block_copies(where, blocks, store, sems, False)
    for c in copies:
        c.start()
    depth, width = store.shape[2:]
    gn2 = gn2_ref[...].astype(F32)
    unit, inverse = normalise(r_ref[...])
    gr = g_ref[...].astype(F32) + norm_back(gn2, unit, inverse, vec_ref[5:6, :])
    go = gr.astype(BF)
    gr_ref[...] = gr
    go_ref[...] = go
    sums_ref[0:1, :] = jnp.sum(go.astype(F32), axis=0, keepdims=True)
    sums_ref[1:2, :] = jnp.sum(gn2 * unit, axis=0, keepdims=True)
    sums_ref[2:3, :] = jnp.sum(gn2, axis=0, keepdims=True)
    sums_ref[3:4, :] = jnp.sum(g_ref[...].astype(F32), axis=0, keepdims=True)
    for c in copies:
        c.wait()
    parts = []
    for p in range(dps):
        total = mm_nt(go[:, 0:width], store[p, 0])
        for n in range(1, seqs):
            total = total + mm_nt(go[:, n * width : (n + 1) * width], store[p, n])
        parts.append(total)
    ga = jnp.concatenate(parts, axis=1).astype(BF)
    ga_ref[...] = jnp.zeros_like(ga_ref)
    for h in range(int(owner.max()) + 1):
        dev, slot = [int(i[0]) for i in np.where(owner == h)]
        ga_ref[dev, :, slot * HD : (slot + 1) * HD] = ga[:, h * HD : (h + 1) * HD]


def out_back(where, gn2, r, g, table, blocks, owner):
    flat = [b for pair in blocks for b in pair]
    dps, seqs = len(blocks), owner.shape[0]
    depth, width = flat[0].shape[1:]
    return pl.pallas_call(
        functools.partial(back_kernel, dps, seqs, owner),
        in_specs=[SCALAR, WHOLE, WHOLE, WHOLE, WHOLE] + [ANY] * len(flat),
        out_specs=[WHOLE] * 4,
        out_shape=[
            jax.ShapeDtypeStruct(r.shape, F32),
            jax.ShapeDtypeStruct(r.shape, BF),
            jax.ShapeDtypeStruct((seqs, r.shape[0], owner.shape[1] * HD), BF),
            jax.ShapeDtypeStruct((4, r.shape[1]), F32),
        ],
        scratch_shapes=[
            pltpu.VMEM((dps, seqs, depth, width), BF),
            pltpu.SemaphoreType.DMA((dps * seqs,)),
        ],
        compiler_params=ROOM,
    )(where, gn2, r, g, table, *flat)


def grad_out_kernel(dps, seqs, owner, where, att_ref, go_ref, *rest):
    flat = rest[: 2 * dps]
    store, sems = rest[2 * dps :]
    blocks = [flat[2 * k : 2 * k + 2] for k in range(dps)]
    att = head_columns(att_ref, owner)
    depth, width = store.shape[2:]
    for p in range(dps):
        rows = att[:, p * depth : (p + 1) * depth]
        for n in range(seqs):
            store[p, n] = mm_tn(rows, go_ref[:, n * width : (n + 1) * width]).astype(BF)
    copies = block_copies(where, blocks, store, sems, True)
    for c in copies:
        c.start()
    for c in copies:
        c.wait()


def grad_out(where, att, go, dps, owner):
    seqs = att.shape[0]
    depth, width = go.shape[1] // dps, go.shape[1] // seqs
    shape = jax.ShapeDtypeStruct((seqs // 2, depth, width), BF)
    flat = pl.pallas_call(
        functools.partial(grad_out_kernel, dps, seqs, owner),
        in_specs=[SCALAR, WHOLE, WHOLE],
        out_specs=[ANY] * (2 * dps),
        out_shape=[shape] * (2 * dps),
        scratch_shapes=[
            pltpu.VMEM((dps, seqs, depth, width), BF),
            pltpu.SemaphoreType.DMA((dps * seqs,)),
        ],
        compiler_params=ROOM,
    )(where, att, go)
    return [flat[2 * k : 2 * k + 2] for k in range(dps)]


def sum_out_blocks(blocks):
    seqs = lax.axis_size("seq")
    chip = [
        (mine.astype(F32) + lax.ppermute(other, "seq", xor_perm(seqs, 1)).astype(F32)).astype(BF)
        for mine, other in blocks
    ]
    line = scatter_rel(chip, "dp").astype(BF)
    total = line[0].astype(F32)
    for dz in range(1, seqs // 2):
        total = total + lax.ppermute(line[dz], "seq", xor_perm(seqs, 2 * dz)).astype(F32)
    return total


def sum_all(block):
    for axis in ("dp", "seq"):
        step = 1
        while step < lax.axis_size(axis):
            block = block + lax.ppermute(block, axis, xor_perm(lax.axis_size(axis), step))
            step *= 2
    return block


def body(tokens, w_qkv, w_out, vectors, w_fc, b_fc, w_proj, cotangent):
    dps = lax.axis_size("dp")
    seqs = lax.axis_size("seq")
    dp = lax.axis_index("dp")
    sq = lax.axis_index("seq")
    rows, model = tokens.shape
    head_count = model // HD
    slots, owner, wide, send, recv = head_plan(head_count, seqs, w_qkv.shape[1])
    mine = slots * HD
    ff_mine = w_fc.shape[1]
    ratio = seqs // dps
    col = w_proj.shape[1]

    per, wide_vec = vectors.shape
    small = gather_small(jnp.concatenate([vectors.reshape(-1), b_fc])[None], "dp")
    small = gather_small(small, "seq").astype(F32)[:, :, 0]
    table = small[:, :, : per * wide_vec].reshape(seqs, dps, per, wide_vec)
    table = table.transpose(1, 2, 0, 3).reshape(dps * per, model)
    gain1, shift1, bias_q, bias_v, bias_o, gain2, shift2, bias_p = [table[i] for i in range(8)]
    bias_fc = small[:, :, per * wide_vec :].transpose(1, 0, 2).reshape(-1)
    bias_fc = lax.dynamic_slice_in_dim(bias_fc, sq * ff_mine, ff_mine)
    own_heads = jnp.asarray(owner)[sq]
    pick = (own_heads[:, None] == jnp.arange(head_count)[None, :]).astype(F32)

    def head_rows(vector):
        return jnp.sum(pick[:, :, None] * vector.reshape(1, head_count, HD), axis=1).reshape(-1)

    def head_spread(vector):
        return jnp.sum(pick[:, :, None] * vector.reshape(slots, 1, HD), axis=0).reshape(-1)

    bias_qkv = jnp.concatenate([head_rows(bias_q), jnp.zeros((mine,), F32), head_rows(bias_v)])

    to_send = (jnp.arange(w_qkv.shape[1])[:, None, None] == jnp.asarray(send)[sq][None]).astype(BF)
    to_recv = (
        lax.dynamic_index_in_dim(jnp.asarray(recv), sq, 1, keepdims=False)[:, :, None]
        == jnp.arange(3 * mine)[None, None]
    ).astype(BF)
    parts = jnp.einsum("ac,cnw->naw", w_qkv, to_send, preferred_element_type=F32).astype(BF)
    parts = lax.all_to_all(parts, "seq", 0, 0, tiled=True)
    own_qkv = jnp.einsum("naw,nwd->ad", parts, to_recv, preferred_element_type=F32).astype(BF)
    wf = gather_rel(w_fc, "dp")

    size, start = piece_rows(ff_mine, dps)
    pieces = w_proj.reshape(ratio, ff_mine, col)
    pieces = jnp.stack([pieces[:, start(q) : start(q) + size] for q in range(dps)])
    pieces = lax.all_to_all(pieces, "dp", 0, 0, tiled=True)
    own_qkv = after(own_qkv, pieces, *wf)

    where = jnp.stack([dp, sq]).astype(jnp.int32)
    x_all = lax.all_gather(after(tokens, parts), "seq", axis=0, tiled=True)
    gm_all = lax.all_gather(after(cotangent, x_all), "seq", axis=0, tiled=True)
    wq = gather_rel(own_qkv, "dp")
    line = line_blocks(w_out)
    wo = out_blocks(line)
    pieces = lax.all_to_all(
        after(pieces.reshape(seqs, size, col), x_all), "seq", 0, 0, tiled=True
    )
    x_all = after(x_all, line)
    n1_all, qkv, att, lse = attend(where, x_all, table, bias_qkv[None], wq, slots, rows)
    att = lax.all_to_all(after(att, pieces), "seq", 0, 0, tiled=True)
    wp = gather_rel(pieces.transpose(1, 0, 2).reshape(size, model), "dp")
    r, n2 = out_project(where, att, tokens, table, wo, owner)
    n2_all = lax.all_gather(after(n2, *wp), "seq", axis=0, tiled=True)

    e, gu, gn2_part, sum_fc = feed(where, n2_all, gm_all, bias_fc[None], wf, wp)
    gn2 = lax.psum_scatter(gn2_part, "seq", scatter_dimension=0, tiled=True)
    mlp, d_fc, d_proj = feed_grad(where, n2_all, gm_all, e, gu, wp)
    gn2, mlp = lax.optimization_barrier((gn2, mlp))
    mlp = lax.psum_scatter(mlp, "seq", scatter_dimension=0, tiled=True)
    activations = (r + (mlp.astype(F32) + bias_p)).astype(BF)

    gr, go, ga, sums_two = out_back(where, gn2, r, cotangent, table, wo, owner)
    ga = lax.all_to_all(ga, "seq", 0, 0, tiled=True)
    d_out = grad_out(where, att, go, dps, owner)
    g_proj = scatter_rel(d_proj, "dp").astype(BF)
    g_fc = scatter_rel([after(d, g_proj) for d in d_fc], "dp")
    gqkv, gn1_part = attend_back(where, qkv, after(ga, g_proj, *d_out[0]), lse, wq)
    gn1 = lax.psum_scatter(gn1_part, "seq", scatter_dimension=0, tiled=True)
    d_qkv, gqkv_sums, norm_sums = grad_qkv(where, n1_all, gqkv, gn1_part, dps)
    input_grad = last_norm(gn1, tokens, gr, table)

    g_qkv = scatter_rel(d_qkv, "dp").astype(BF)
    parts = jnp.einsum("ad,nwd->naw", g_qkv, to_recv, preferred_element_type=F32).astype(BF)
    parts = lax.all_to_all(parts, "seq", 0, 0, tiled=True)
    g_qkv = jnp.einsum("naw,cnw->ac", parts, to_send, preferred_element_type=F32)

    g_proj = g_proj.reshape(size, seqs, col).transpose(1, 0, 2)
    g_proj = lax.all_to_all(g_proj, "seq", 0, 0, tiled=True)
    g_proj = g_proj.reshape(dps, ratio, size, col)
    g_proj = lax.all_to_all(g_proj, "dp", 0, 0, tiled=True)
    ends = [start(q) for q in range(dps)] + [ff_mine]
    g_proj = jnp.concatenate(
        [g_proj[q, :, : ends[q + 1] - ends[q]] for q in range(dps)], axis=1
    )
    g_proj = g_proj.reshape(w_proj.shape).astype(F32)

    g_out = sum_out_blocks(d_out)

    vector_grads = jnp.concatenate(
        [
            ((norm_sums[0] - shift1 * norm_sums[1]) / gain1)[None],
            norm_sums[1:],
            head_spread(gqkv_sums[0, :mine])[None],
            head_spread(gqkv_sums[0, 2 * mine :])[None],
            sums_two,
        ]
    )
    fc_sums = lax.dynamic_update_slice_in_dim(
        jnp.zeros((dps * seqs * b_fc.shape[0],), F32), sum_fc[0], sq * ff_mine, axis=0
    ).reshape(-1, model)
    sums = sum_all(jnp.concatenate([vector_grads, fc_sums]))
    own_vec = lax.dynamic_slice(sums, (dp * per, sq * wide_vec), (per, wide_vec))
    own_fc = lax.dynamic_slice_in_dim(
        sums[8:].reshape(-1), (dp * seqs + sq) * b_fc.shape[0], b_fc.shape[0]
    )
    return (
        activations,
        input_grad,
        g_qkv,
        g_out,
        own_vec,
        g_fc,
        own_fc,
        g_proj,
    )


def solution(mesh):
    rows = P(("dp", "seq"), None)
    grid = P("dp", "seq")
    line = P(("dp", "seq"))
    return jax.shard_map(
        body,
        mesh=mesh,
        in_specs=(rows, grid, grid, grid, grid, line, grid, rows),
        out_specs=(rows, rows, grid, grid, grid, grid, line, grid),
        check_vma=False,
    )
```

```python
import functools
import math

import jax
import jax.numpy as jnp
import numpy as np
from jax import lax
from jax.experimental import pallas as pl
from jax.experimental.pallas import tpu as pltpu
from jax.sharding import PartitionSpec as P

HD = 64
PAIR = 2 * HD
EPSILON = 1e-05
GELU_C = 0.7978845608028654
NEG_FILL = -1e30
BF = jnp.bfloat16
F32 = jnp.float32


def head_plan(head_count, seq_count, width):
    slots = -(-head_count // seq_count)
    slots += slots % 2
    model = head_count * HD

    def tables(turn):
        owner = np.full((seq_count, slots), -1, np.int32)
        for head in range(head_count):
            row = head // seq_count
            owner[(head + turn * row) % seq_count, row] = head
        place = {}
        for dev in range(seq_count):
            for slot in range(slots):
                if owner[dev, slot] >= 0:
                    place[int(owner[dev, slot])] = (dev, slot)
        lists = [[[] for _ in range(seq_count)] for _ in range(seq_count)]
        for col in range(3 * model):
            kind, rest = divmod(col, model)
            head, lane = divmod(rest, HD)
            dev, slot = place[head]
            src, local = divmod(col, width)
            lists[src][dev].append((local, (kind * slots + slot) * HD + lane))
        most = max(len(cell) for row in lists for cell in row)
        return most, owner, lists

    best = min((tables(turn) for turn in range(seq_count)), key=lambda t: t[0])
    most, owner, lists = best
    wide = -(-most // 128) * 128
    send = np.full((seq_count, seq_count, wide), -1, np.int32)
    recv = np.full((seq_count, seq_count, wide), -1, np.int32)
    for src in range(seq_count):
        for dev in range(seq_count):
            for i, (local, target) in enumerate(lists[src][dev]):
                send[src, dev, i] = local
                recv[src, dev, i] = target
    return slots, owner, wide, send, recv


ANY = pl.BlockSpec(memory_space=pl.ANY)
WHOLE = pl.BlockSpec(memory_space=pltpu.VMEM)
SCALAR = pl.BlockSpec(memory_space=pltpu.SMEM)


def blocks_of(*shapes):
    return [pl.BlockSpec(s.shape, lambda n=len(s.shape): (0,) * n) for s in shapes]


ROOM = pltpu.CompilerParams(vmem_limit_bytes=56 * 1024 * 1024)


def like(shape, kind=BF):
    return jax.ShapeDtypeStruct(shape, kind)


def phase(*values):
    return lax.optimization_barrier(values)


def xor_perm(count, k):
    return [(i, i ^ k) for i in range(count)]


def near_far(count):
    every = range(1, count)
    return [k for k in every if not k & (k - 1)], [k for k in every if k & (k - 1)]


def send_rel(blocks, axis, ks):
    count = lax.axis_size(axis)
    return {k: lax.ppermute(blocks[k], axis, xor_perm(count, k)) for k in ks}


def in_order(mine, *found):
    every = {0: mine}
    for part in found:
        every.update(part)
    return [every[k] for k in range(len(every))]


def can_halve(count, rows):
    return count == 4 and rows % 16 == 0


def cut(rows):
    return 16 * (rows // 16 - rows // 32)


def split_far(chunks):
    if len(chunks) != 4:
        return chunks
    far = chunks[3]
    half = far.shape[0] // 2 if far.ndim == 3 else cut(far.shape[0])
    return list(chunks[:3]) + [far[:half], far[half:]]


def reduce_first(chunks):
    if len(chunks) == 5:
        return [
            lax.ppermute(chunks[3], "dp", xor_perm(4, 1)),
            lax.ppermute(chunks[4], "dp", xor_perm(4, 2)),
        ]
    near, far = near_far(len(chunks))
    return list(send_rel(dict(enumerate(chunks)), "dp", far).values())


def reduce_second(chunks, found):
    if len(chunks) == 5:
        half = found[0].shape[0]
        first = jnp.concatenate(
            [chunks[1][:half], total_of([chunks[1][half:], found[1]]).astype(BF)]
        )
        second = jnp.concatenate(
            [total_of([chunks[2][:half], found[0]]).astype(BF), chunks[2][half:]]
        )
        return [
            chunks[0],
            lax.ppermute(first, "dp", xor_perm(4, 1)),
            lax.ppermute(second, "dp", xor_perm(4, 2)),
        ]
    near, far = near_far(len(chunks))
    return [chunks[0]] + found + list(send_rel(dict(enumerate(chunks)), "dp", near).values())


def swap_core(block):
    return lax.ppermute(block, "seq", xor_perm(lax.axis_size("seq"), 1))


def exchange(block):
    return lax.all_to_all(block, "seq", 0, 0, tiled=True)


def total_of(parts):
    total = parts[0].astype(F32)
    for part in parts[1:]:
        total = total + part.astype(F32)
    return total


def as_rows(values, lanes):
    size = -values.shape[1] % (16 * lanes)
    return jnp.pad(values, ((0, 0), (0, size))).reshape(values.shape[0], -1, lanes)


def normalise(rows):
    mean = jnp.mean(rows, axis=-1, keepdims=True)
    centred = rows - mean
    inverse = lax.rsqrt(jnp.mean(centred * centred, axis=-1, keepdims=True) + EPSILON)
    return centred * inverse, inverse


def norm_back(grad, unit, inverse, gain):
    scaled = grad * gain
    return (
        scaled
        - jnp.mean(scaled, axis=-1, keepdims=True)
        - unit * jnp.mean(scaled * unit, axis=-1, keepdims=True)
    ) * inverse


def gelu_parts(u):
    square = u * u
    t = jnp.tanh(u * (GELU_C + GELU_C * 0.044715 * square))
    half = 0.5 + 0.5 * t
    slope = half + u * (0.5 - 0.5 * t * t) * (GELU_C + 3 * 0.044715 * GELU_C * square)
    return u * half, slope


def mm(a, b):
    return jnp.dot(a, b, preferred_element_type=F32)


def mm_nt(a, b):
    return lax.dot_general(a, b, (((1,), (1,)), ((), ())), preferred_element_type=F32)


def mm_tn(a, b):
    return lax.dot_general(a, b, (((0,), (0,)), ((), ())), preferred_element_type=F32)


def run_copies(pairs, sems):
    found = [pltpu.make_async_copy(src, dst, sems.at[i]) for i, (src, dst) in enumerate(pairs)]
    for c in found:
        c.start()
    return found


def wait_for(copies):
    for c in copies:
        c.wait()


def stage_shape(dps, depth, width):
    return (dps, depth, width) if depth % 16 else (1, 16, 128)


def place_rows(where, refs, store, stage, sems, outward=False):
    depth = refs[0].shape[0]
    if outward and len(refs) == 5:
        pairs = []
        for k, ref in zip((0, 1, 2, 3, 3), refs):
            first = (where[0] ^ k) * depth
            if ref is refs[4]:
                first = first + refs[3].shape[0]
            pairs.append((store.at[pl.ds(pl.multiple_of(first, 16), ref.shape[0]), :], ref))
        return run_copies(pairs, sems)
    if depth % 16:
        spots = [stage.at[where[0] ^ k] for k in range(len(refs))]
    else:
        spots = [
            store.at[pl.ds(pl.multiple_of((where[0] ^ k) * depth, 16), depth), :]
            for k in range(len(refs))
        ]
    if outward:
        if depth % 16:
            for p in range(len(refs)):
                stage[p] = store[p * depth : (p + 1) * depth, :]
        return run_copies(list(zip(spots, refs)), sems)
    return run_copies(list(zip(refs, spots)), sems)


def settle_rows(copies, store, stage):
    wait_for(copies)
    depth = stage.shape[1]
    if depth % 16:
        for p in range(stage.shape[0]):
            store[p * depth : (p + 1) * depth, :] = stage[p]


def hot(row, count):
    return (
        lax.broadcasted_iota(jnp.int32, (count, row.shape[1]), 0) == row
    ).astype(BF)


def pack_kernel(where, w_ref, send_ref, more_ref, out_ref):
    depth = w_ref.shape[0]
    for n in range(out_ref.shape[0]):
        out_ref[n, 0:depth] = mm(w_ref[...], hot(send_ref[where[1], n], w_ref.shape[1])).astype(BF)
        out_ref[n, depth:] = more_ref[...]


def pack_columns(where, w_qkv, send, more):
    seqs, _, _, wide = send.shape
    shape = like((seqs, w_qkv.shape[0] + more.shape[0], wide))
    return pl.pallas_call(
        pack_kernel,
        in_specs=[SCALAR, WHOLE, WHOLE, WHOLE],
        out_specs=blocks_of(shape)[0],
        out_shape=shape,
        compiler_params=ROOM,
    )(where, w_qkv, send, more)


def unpack_kernel(where, recv_ref, in_ref, out_ref):
    total = None
    for n in range(in_ref.shape[0]):
        part = mm_nt(in_ref[n, 0 : out_ref.shape[0]], hot(recv_ref[n, where[1]], out_ref.shape[1]))
        total = part if total is None else total + part
    out_ref[...] = total.astype(BF)


def unpack_columns(where, parts, recv, depth, width):
    return pl.pallas_call(
        unpack_kernel,
        in_specs=[SCALAR, WHOLE, WHOLE],
        out_specs=blocks_of(like((depth, width)))[0],
        out_shape=like((depth, width)),
        compiler_params=ROOM,
    )(where, recv, parts)


def repack_kernel(where, recv_ref, more_ref, *rest):
    parts, out_ref = rest[:-1], rest[-1]
    grad = total_of([p[...] for p in parts]).astype(BF)
    depth = grad.shape[0]
    for n in range(out_ref.shape[0]):
        out_ref[n, 0:depth] = mm(grad, hot(recv_ref[n, where[1]], grad.shape[1])).astype(BF)
        out_ref[n, depth:] = more_ref[n]


def repack_columns(where, parts, recv, more):
    seqs, _, _, wide = recv.shape
    shape = like((seqs, parts[0].shape[0] + more.shape[1], wide))
    return pl.pallas_call(
        repack_kernel,
        in_specs=[SCALAR] + [WHOLE] * (2 + len(parts)),
        out_specs=blocks_of(shape)[0],
        out_shape=shape,
        compiler_params=ROOM,
    )(where, recv, more, *parts)


def restore_kernel(where, send_ref, in_ref, out_ref):
    depth = out_ref.shape[0]
    total = None
    for n in range(in_ref.shape[0]):
        part = mm_nt(in_ref[n, 0:depth], hot(send_ref[where[1], n], out_ref.shape[1]))
        total = part if total is None else total + part
    out_ref[...] = total


def restore_columns(where, parts, send, depth, width):
    return pl.pallas_call(
        restore_kernel,
        in_specs=[SCALAR, WHOLE, WHOLE],
        out_specs=blocks_of(like((depth, width)))[0],
        out_shape=like((depth, width), F32),
        compiler_params=ROOM,
    )(where, send, parts)


def piece_rows(total, count):
    tiles = total // 16
    return 16 * -(-tiles // count), lambda q: 16 * ((q * tiles) // count)


def pieces_kernel(where, w_ref, *outs):
    size, start = piece_rows(w_ref.shape[1], len(outs))
    for k, ref in enumerate(outs):
        first = pl.multiple_of(start(where[0] ^ k), 16)
        ref[...] = w_ref[:, pl.ds(first, size), :]


def proj_pieces(where, w_proj, dps):
    ratio, ff_mine, col = w_proj.shape
    size, _ = piece_rows(ff_mine, dps)
    return pl.pallas_call(
        pieces_kernel,
        in_specs=[SCALAR, WHOLE],
        out_specs=blocks_of(*[like((ratio, size, col))] * dps),
        out_shape=[like((ratio, size, col))] * dps,
        compiler_params=ROOM,
    )(where, w_proj)


def turn_kernel(where, *rest):
    ins, (out_ref, sems) = rest[:-2], rest[-2:]
    ratio = ins[0].shape[0]
    spots = [out_ref.at[pl.ds((where[0] ^ k) * ratio, ratio)] for k in range(len(ins))]
    wait_for(run_copies(list(zip(ins, spots)), sems))


def turn_pieces(where, parts):
    ratio, size, col = parts[0].shape
    return pl.pallas_call(
        turn_kernel,
        in_specs=[SCALAR] + [WHOLE] * len(parts),
        out_specs=blocks_of(like((ratio * len(parts), size, col)))[0],
        out_shape=like((ratio * len(parts), size, col)),
        scratch_shapes=[pltpu.SemaphoreType.DMA((len(parts),))],
        compiler_params=ROOM,
    )(where, *parts)


def join_kernel(in_ref, out_ref):
    width = in_ref.shape[2]
    for n in range(in_ref.shape[0]):
        out_ref[:, n * width : (n + 1) * width] = in_ref[n]


def join_columns(parts):
    seqs, size, col = parts.shape
    return pl.pallas_call(
        join_kernel,
        in_specs=[WHOLE],
        out_specs=blocks_of(like((size, col * seqs)))[0],
        out_shape=like((size, col * seqs)),
        compiler_params=ROOM,
    )(parts)


def split_kernel(*refs):
    out_ref = refs[-1]
    total = total_of([r[...] for r in refs[:-1]]).astype(BF)
    width = out_ref.shape[2]
    for n in range(out_ref.shape[0]):
        out_ref[n] = total[:, n * width : (n + 1) * width]


def split_columns(parts, seqs):
    size, model = parts[0].shape
    return pl.pallas_call(
        split_kernel,
        in_specs=[WHOLE] * len(parts),
        out_specs=blocks_of(like((seqs, size, model // seqs)))[0],
        out_shape=like((seqs, size, model // seqs)),
        compiler_params=ROOM,
    )(*parts)


def rows_kernel(where, *rest):
    ins, (out_ref, store, sems) = rest[:-3], rest[-3:]
    dps, ratio, size, _ = store.shape
    ff_mine = out_ref.shape[0] // ratio
    _, start = piece_rows(ff_mine, dps)
    wait_for(run_copies([(ref, store.at[where[0] ^ k]) for k, ref in enumerate(ins)], sems))
    for q in range(dps):
        for b in range(ratio):
            first = b * ff_mine + start(q)
            out_ref[first : first + size, :] = store[q, b].astype(F32)


def proj_rows(where, parts, ff_mine):
    ratio, size, col = parts[0].shape
    return pl.pallas_call(
        rows_kernel,
        in_specs=[SCALAR] + [ANY] * len(parts),
        out_specs=blocks_of(like((ratio * ff_mine, col)))[0],
        out_shape=like((ratio * ff_mine, col), F32),
        scratch_shapes=[
            pltpu.VMEM((len(parts), ratio, size, col), BF),
            pltpu.SemaphoreType.DMA((len(parts),)),
        ],
        compiler_params=ROOM,
    )(where, *parts)


def head_masks(rows):
    first = lax.broadcasted_iota(jnp.int32, (rows, PAIR), 1) < HD
    causal = lax.broadcasted_iota(jnp.int32, (rows, rows), 0) >= lax.broadcasted_iota(
        jnp.int32, (rows, rows), 1
    )
    return first, causal


def masked_scores(q, keys, causal):
    rows, seen = q.shape[0], keys.shape[0]
    s = mm_nt(q, keys)
    tail = jnp.where(causal, s[:, seen - rows :], NEG_FILL)
    return tail if seen == rows else jnp.concatenate([s[:, : seen - rows], tail], axis=1)


def attend_rows(q, keys, values, first, causal):
    q = q * BF(1.0 / math.sqrt(HD))
    outs, logs = [], []
    for mine in (first, ~first):
        s = masked_scores(jnp.where(mine, q, BF(0)), keys, causal)
        top = jnp.max(s, axis=-1, keepdims=True)
        e = jnp.exp(s - top)
        total = jnp.sum(e, axis=-1, keepdims=True)
        outs.append(mm(e.astype(BF), values) / total)
        logs.append(top + jnp.log(total))
    return jnp.where(first, outs[0], outs[1]).astype(BF), jnp.where(first, logs[0], logs[1])


def attend_kernel(pairs, dps, where, x_ref, vec_ref, bias_ref, *rest):
    w_refs = rest[:dps]
    n1_ref, qkv_ref, att_ref, lse_ref, w, stage, qkv, sems = rest[dps:]
    i = pl.program_id(0)
    rows = x_ref.shape[0]
    part = rows // 2

    @pl.when(i == 0)
    def _():
        settle_rows(place_rows(where, w_refs, w, stage, sems), w, stage)

    unit, _ = normalise(x_ref[...].astype(F32))
    n1 = (unit * vec_ref[0:1, :] + vec_ref[1:2, :]).astype(BF)
    n1_ref[...] = n1
    tile = (mm(n1, w[...]) + bias_ref[...]).astype(BF)
    qkv_ref[...] = tile
    qkv[pl.ds(pl.multiple_of(i * rows, rows), rows), :] = tile
    first, causal = head_masks(rows)
    for j in range(qkv.shape[0] // rows):

        @pl.when(i == j)
        def _(j=j):
            seen = (j + 1) * rows
            for g in range(pairs):
                lanes = slice(g * PAIR, (g + 1) * PAIR)
                keys = qkv[0:seen, (pairs + g) * PAIR : (pairs + g + 1) * PAIR]
                values = qkv[0:seen, (2 * pairs + g) * PAIR : (2 * pairs + g + 1) * PAIR]
                out, log = attend_rows(qkv[j * rows : seen, lanes], keys, values, first, causal)
                for b in range(2):
                    att_ref[b, :, lanes] = out[b * part : (b + 1) * part]
                lse_ref[:, lanes] = log


def attend(where, x_all, table, bias, weights, part):
    length, model = x_all.shape
    depth, width = weights[0].shape
    dps = len(weights)
    heads = width // 3
    rows = 2 * part
    whole = lambda a: pl.BlockSpec(a.shape, lambda i: (0,) * a.ndim)
    tile = lambda cols: pl.BlockSpec((rows, cols), lambda i: (i, 0))
    return pl.pallas_call(
        functools.partial(attend_kernel, heads // PAIR, dps),
        grid=(length // rows,),
        in_specs=[SCALAR, tile(model), whole(table), whole(bias)] + [ANY] * dps,
        out_specs=[
            tile(model),
            tile(width),
            pl.BlockSpec((2, part, heads), lambda i: (i, 0, 0)),
            tile(heads),
        ],
        out_shape=[
            like((length, model)),
            like((length, width)),
            like((length // part, part, heads)),
            like((length, heads), F32),
        ],
        scratch_shapes=[
            pltpu.VMEM((model, width), BF),
            pltpu.VMEM(stage_shape(dps, depth, width), BF),
            pltpu.VMEM((length, width), BF),
            pltpu.SemaphoreType.DMA((dps,)),
        ],
        compiler_params=ROOM,
    )(where, x_all, table, bias, *weights)


def attend_back_kernel(pairs, qkv_ref, ga_ref, lse_ref, gqkv_ref, sums_ref, ak, av):
    length = qkv_ref.shape[0]
    part = ga_ref.shape[1]
    rows = 2 * part
    first, causal = head_masks(rows)
    for g in range(pairs):
        lanes = slice(g * PAIR, (g + 1) * PAIR)
        k_lanes = slice((pairs + g) * PAIR, (pairs + g + 1) * PAIR)
        v_lanes = slice((2 * pairs + g) * PAIR, (2 * pairs + g + 1) * PAIR)
        ak[...] = jnp.zeros_like(ak)
        av[...] = jnp.zeros_like(av)
        for i in range(length // rows):
            here = slice(i * rows, (i + 1) * rows)
            seen = (i + 1) * rows
            q = qkv_ref[here, lanes] * BF(1.0 / math.sqrt(HD))
            ga = jnp.concatenate([ga_ref[b, :, lanes] for b in (2 * i, 2 * i + 1)], axis=0)
            keys = qkv_ref[0:seen, k_lanes]
            values = qkv_ref[0:seen, v_lanes]
            grads = []
            for h, mine in enumerate((first, ~first)):
                q_h = jnp.where(mine, q, BF(0))
                ga_h = jnp.where(mine, ga, BF(0))
                s = masked_scores(q_h, keys, causal)
                lane = g * PAIR + h * HD
                p = jnp.exp(s - lse_ref[here, lane : lane + 1])
                gp = mm_nt(ga_h, values)
                centre = jnp.sum(p * gp, axis=-1, keepdims=True)
                gs = (p * (gp - centre)).astype(BF)
                av[0:seen, :] += mm_tn(p.astype(BF), ga_h)
                ak[0:seen, :] += mm_tn(gs, q_h)
                grads.append(mm(gs, keys))
            gqkv_ref[here, lanes] = (
                jnp.where(first, grads[0], grads[1]) * (1.0 / math.sqrt(HD))
            ).astype(BF)
        gqkv_ref[:, k_lanes] = ak[...].astype(BF)
        gqkv_ref[:, v_lanes] = av[...].astype(BF)
    sums_ref[...] = jnp.sum(gqkv_ref[...].astype(F32), axis=0, keepdims=True)


def attend_back(qkv, grad, lse):
    length, width = qkv.shape
    return pl.pallas_call(
        functools.partial(attend_back_kernel, grad.shape[2] // PAIR),
        in_specs=[WHOLE] * 3,
        out_specs=[WHOLE, WHOLE],
        out_shape=[like((length, width)), like((1, width), F32)],
        scratch_shapes=[pltpu.VMEM((length, PAIR), F32), pltpu.VMEM((length, PAIR), F32)],
        compiler_params=ROOM,
    )(qkv, grad, lse)


def grad_blocks_kernel(where, a_ref, g_ref, *rest):
    outs, (store, stage, sems) = rest[:-3], rest[-3:]
    g = g_ref[...]
    model = a_ref.shape[1]
    for a in range(0, model, 256):
        b = min(model, a + 256)
        store[a:b, :] = mm_tn(a_ref[:, a:b], g).astype(BF)
    wait_for(place_rows(where, outs, store, stage, sems, True))


def chunk_shapes(count, rows, cols):
    shapes = [like((rows, cols))] * count
    if can_halve(count, rows):
        shapes[3:] = [like((cut(rows), cols)), like((rows - cut(rows), cols))]
    return shapes


def grad_blocks(where, a, g, dps):
    model, width = a.shape[1], g.shape[1]
    depth = model // dps
    shapes = chunk_shapes(dps, depth, width)
    return pl.pallas_call(
        grad_blocks_kernel,
        in_specs=[SCALAR, WHOLE, WHOLE],
        out_specs=[ANY] * len(shapes),
        out_shape=shapes,
        scratch_shapes=[
            pltpu.VMEM((model, width), BF),
            pltpu.VMEM(stage_shape(dps, depth, width), BF),
            pltpu.SemaphoreType.DMA((len(shapes),)),
        ],
        compiler_params=ROOM,
    )(where, a, g)


def grad_rows_kernel(dps, where, g_ref, n1_ref, *rest):
    w_refs = rest[:dps]
    out_ref, sums_ref, w, stage, sems = rest[dps:]

    @pl.when(pl.program_id(0) == 0)
    def _():
        settle_rows(place_rows(where, w_refs, w, stage, sems), w, stage)
        sums_ref[...] = jnp.zeros_like(sums_ref)

    grad = mm_nt(g_ref[...], w[...])
    sums_ref[0:1, :] += jnp.sum(grad * n1_ref[...].astype(F32), axis=0, keepdims=True)
    sums_ref[1:2, :] += jnp.sum(grad, axis=0, keepdims=True)
    out_ref[...] = grad.astype(BF)


def grad_rows(where, gqkv, weights, n1, rows):
    length, model = n1.shape
    depth, width = weights[0].shape
    dps = len(weights)
    tile = lambda cols: pl.BlockSpec((rows, cols), lambda i: (i, 0))
    return pl.pallas_call(
        functools.partial(grad_rows_kernel, dps),
        grid=(length // rows,),
        in_specs=[SCALAR, tile(width), tile(model)] + [ANY] * dps,
        out_specs=[tile(model), pl.BlockSpec((2, model), lambda i: (0, 0))],
        out_shape=[like((length, model)), like((2, model), F32)],
        scratch_shapes=[
            pltpu.VMEM((model, width), BF),
            pltpu.VMEM(stage_shape(dps, depth, width), BF),
            pltpu.SemaphoreType.DMA((dps,)),
        ],
        compiler_params=ROOM,
    )(where, gqkv, n1, *weights)


def place_pieces(where, refs, store, sem):
    size, start = piece_rows(store.shape[0], len(refs))
    for k, ref in enumerate(refs):
        spot = store.at[pl.ds(pl.multiple_of(start(where[0] ^ k), 16), size), :]
        one = pltpu.make_async_copy(ref, spot, sem)
        one.start()
        one.wait()


def feed_kernel(dps, where, n2_ref, gm_ref, bias_ref, *rest):
    f_refs, p_refs = rest[:dps], rest[dps : 2 * dps]
    e_ref, gu_ref, gn2_ref, sum_ref, wf, stage, wp, sems, sem = rest[2 * dps :]

    @pl.when(pl.program_id(0) == 0)
    def _():
        copies = place_rows(where, f_refs, wf, stage, sems)
        place_pieces(where, p_refs, wp, sem)
        settle_rows(copies, wf, stage)
        sum_ref[...] = jnp.zeros_like(sum_ref)

    u = mm(n2_ref[...], wf[...]) + bias_ref[...]
    ge = mm_nt(gm_ref[...], wp[...])
    value, slope = gelu_parts(u)
    e_ref[...] = value.astype(BF)
    gu = (ge * slope).astype(BF)
    gu_ref[...] = gu
    sum_ref[...] += jnp.sum(gu.astype(F32), axis=0, keepdims=True)
    gn2_ref[...] = mm_nt(gu, wf[...]).astype(BF)


def feed(where, n2, gm, bias, fc, proj, rows):
    length, model = n2.shape
    dps = len(fc)
    depth, width = fc[0].shape
    whole = lambda shape: pl.BlockSpec(shape, lambda i: (0,) * len(shape))
    tile = lambda cols: pl.BlockSpec((rows, cols), lambda i: (i, 0))
    return pl.pallas_call(
        functools.partial(feed_kernel, dps),
        grid=(length // rows,),
        in_specs=[SCALAR, tile(model), tile(model), whole(bias.shape)] + [ANY] * (2 * dps),
        out_specs=[tile(width), tile(width), tile(model), whole((1, width))],
        out_shape=[
            like((length, width)),
            like((length, width)),
            like((length, model)),
            like((1, width), F32),
        ],
        scratch_shapes=[
            pltpu.VMEM((model, width), BF),
            pltpu.VMEM(stage_shape(dps, depth, width), BF),
            pltpu.VMEM((width, model), BF),
            pltpu.SemaphoreType.DMA((dps,)),
            pltpu.SemaphoreType.DMA,
        ],
        compiler_params=ROOM,
    )(where, n2, gm, bias, *fc, *proj)


def grad_proj_kernel(dps, where, gm_ref, e_ref, *rest):
    outs, (store, sems) = rest[:-2], rest[-2:]
    width = store.shape[0]
    for a in range(0, width, 256):
        b = min(width, a + 256)
        store[a:b, :] = mm_tn(e_ref[:, a:b], gm_ref[...]).astype(BF)
    _, start = piece_rows(width, dps)
    pairs = []
    for i, ref in enumerate(outs):
        first = start(where[0] ^ min(i, dps - 1))
        if i == dps:
            first = first + outs[i - 1].shape[0]
        pairs.append((store.at[pl.ds(pl.multiple_of(first, 16), ref.shape[0]), :], ref))
    wait_for(run_copies(pairs, sems))


def grad_proj(where, gm, e, dps):
    model, width = gm.shape[1], e.shape[1]
    size, _ = piece_rows(width, dps)
    shapes = chunk_shapes(dps, size, model)
    return pl.pallas_call(
        functools.partial(grad_proj_kernel, dps),
        in_specs=[SCALAR, WHOLE, WHOLE],
        out_specs=[ANY] * len(shapes),
        out_shape=shapes,
        scratch_shapes=[
            pltpu.VMEM((width, model), BF),
            pltpu.SemaphoreType.DMA((len(shapes),)),
        ],
        compiler_params=ROOM,
    )(where, gm, e)


def feed_out_kernel(dps, where, e_ref, *rest):
    p_refs = rest[:dps]
    out_ref, wp, sem = rest[dps:]

    @pl.when(pl.program_id(0) == 0)
    def _():
        place_pieces(where, p_refs, wp, sem)

    out_ref[...] = mm(e_ref[...], wp[...]).astype(BF)


def feed_out(where, e, proj, rows):
    length, width = e.shape
    model = proj[0].shape[1]
    return pl.pallas_call(
        functools.partial(feed_out_kernel, len(proj)),
        grid=(length // rows,),
        in_specs=[SCALAR, pl.BlockSpec((rows, width), lambda i: (i, 0))] + [ANY] * len(proj),
        out_specs=pl.BlockSpec((rows, model), lambda i: (i, 0)),
        out_shape=like((length, model)),
        scratch_shapes=[pltpu.VMEM((width, model), BF), pltpu.SemaphoreType.DMA],
        compiler_params=ROOM,
    )(where, e, *proj)


def last_kernel(gn1_ref, gr_ref, vec_ref, x_hbm, out_ref, x_ref, sem):
    copy = pltpu.make_async_copy(x_hbm, x_ref, sem)
    copy.start()
    copy.wait()
    unit, inverse = normalise(x_ref[...].astype(F32))
    grad = norm_back(gn1_ref[...].astype(F32), unit, inverse, vec_ref[0:1, :])
    out_ref[...] = (gr_ref[...] + grad).T.astype(BF)


def last_norm(gn1, x, gr, table):
    shape = like(x.shape[::-1])
    return pl.pallas_call(
        last_kernel,
        in_specs=[WHOLE] * 3 + [ANY],
        out_specs=blocks_of(shape)[0],
        out_shape=shape,
        scratch_shapes=[pltpu.VMEM(x.shape, BF), pltpu.SemaphoreType.DMA],
        compiler_params=ROOM,
    )(gn1, gr, table, x)


def line_blocks(block):
    seqs = lax.axis_size("seq")
    return jnp.stack(
        [block]
        + [lax.ppermute(block, "seq", xor_perm(seqs, 2 * dz)) for dz in range(1, seqs // 2)]
    )


def block_pairs(where, flat, store):
    return [
        (ref.at[dz], store.at[where[0] ^ (i // 2), where[1] ^ (2 * dz + i % 2)])
        for i, ref in enumerate(flat)
        for dz in range(ref.shape[0])
    ]


def head_columns(att_ref, owner):
    count = int(owner.max()) + 1
    parts = []
    for h in range(count):
        dev, slot = [int(i[0]) for i in np.where(owner == h)]
        parts.append(att_ref[dev, :, slot * HD : (slot + 1) * HD])
    return jnp.concatenate(parts, axis=1)


def block_scratch(flat):
    line, depth, width = flat[0].shape
    dps = len(flat) // 2
    return [
        pltpu.VMEM((dps, 2 * line, depth, width), BF),
        pltpu.SemaphoreType.DMA((dps * 2 * line + 1,)),
    ]


def out_kernel(owner, where, att_ref, vec_ref, x_hbm, *rest):
    flat, (r_ref, n2_ref, store, sems, x_ref) = rest[:-5], rest[-5:]
    copies = run_copies(block_pairs(where, flat, store) + [(x_hbm, x_ref)], sems)
    att = head_columns(att_ref, owner)
    dps, seqs, depth, width = store.shape
    wait_for(copies)
    for n in range(seqs):
        here = slice(n * width, (n + 1) * width)
        total = x_ref[:, here].astype(F32) + vec_ref[4:5, here]
        for p in range(dps):
            total = total + mm(att[:, p * depth : (p + 1) * depth], store[p, n])
        r_ref[:, here] = total
    unit, _ = normalise(r_ref[...])
    n2_ref[...] = (unit * vec_ref[5:6, :] + vec_ref[6:7, :]).astype(BF)


def out_project(where, att, x, table, flat, owner):
    return pl.pallas_call(
        functools.partial(out_kernel, owner),
        in_specs=[SCALAR, WHOLE, WHOLE, ANY] + [ANY] * len(flat),
        out_specs=blocks_of(x, x),
        out_shape=[like(x.shape, F32), like(x.shape)],
        scratch_shapes=block_scratch(flat) + [pltpu.VMEM(x.shape, BF)],
        compiler_params=ROOM,
    )(where, att, table, x, *flat)


def back_kernel(owner, where, gn2_ref, r_ref, vec_ref, g_hbm, *rest):
    flat = rest[:-7]
    gr_ref, go_ref, ga_ref, sums_ref, store, sems, g_ref = rest[-7:]
    copies = run_copies([(g_hbm, g_ref)] + block_pairs(where, flat, store), sems)
    copies[0].wait()
    dps, seqs, depth, width = store.shape
    gn2 = gn2_ref[...].astype(F32)
    unit, inverse = normalise(r_ref[...])
    gr = g_ref[...].astype(F32) + norm_back(gn2, unit, inverse, vec_ref[5:6, :])
    go = gr.astype(BF)
    gr_ref[...] = gr
    go_ref[...] = go
    sums_ref[0:1, :] = jnp.sum(go.astype(F32), axis=0, keepdims=True)
    sums_ref[1:2, :] = jnp.sum(gn2 * unit, axis=0, keepdims=True)
    sums_ref[2:3, :] = jnp.sum(gn2, axis=0, keepdims=True)
    sums_ref[3:4, :] = jnp.sum(g_ref[...].astype(F32), axis=0, keepdims=True)
    wait_for(copies[1:])
    found = []
    for p in range(dps):
        total = mm_nt(go[:, 0:width], store[p, 0])
        for n in range(1, seqs):
            total = total + mm_nt(go[:, n * width : (n + 1) * width], store[p, n])
        found.append(total)
    ga = jnp.concatenate(found, axis=1).astype(BF)
    ga_ref[...] = jnp.zeros_like(ga_ref)
    for h in range(int(owner.max()) + 1):
        dev, slot = [int(i[0]) for i in np.where(owner == h)]
        ga_ref[dev, :, slot * HD : (slot + 1) * HD] = ga[:, h * HD : (h + 1) * HD]


def out_back(where, gn2, r, g, table, flat, owner):
    shapes = [
        like(r.shape, F32),
        like(r.shape),
        like((owner.shape[0], r.shape[0], owner.shape[1] * HD)),
        like((4, r.shape[1]), F32),
    ]
    return pl.pallas_call(
        functools.partial(back_kernel, owner),
        in_specs=[SCALAR, WHOLE, WHOLE, WHOLE, ANY] + [ANY] * len(flat),
        out_specs=blocks_of(*shapes),
        out_shape=shapes,
        scratch_shapes=block_scratch(flat) + [pltpu.VMEM(g.shape, BF)],
        compiler_params=ROOM,
    )(where, gn2, r, table, g, *flat)


def grad_out_kernel(owner, where, att_ref, far_att_ref, go_ref, far_go_ref, *rest):
    outs, (store, sems) = rest[:-2], rest[-2:]
    att = jnp.concatenate([head_columns(r, owner) for r in (att_ref, far_att_ref)], axis=0)
    go = jnp.concatenate([go_ref[...], far_go_ref[...]], axis=0)
    dps, line, depth, width = store.shape
    even = where[1] % 2 == 0
    for z in range(line):
        a, b = 2 * z * width, (2 * z + 1) * width
        cols = jnp.where(even, go[:, a : a + width], go[:, b : b + width])
        for p in range(dps):
            store[p, z] = mm_tn(att[:, p * depth : (p + 1) * depth], cols).astype(BF)
    pairs = [
        (store.at[where[0] ^ k, (where[1] // 2) ^ dz], ref.at[dz])
        for k, ref in enumerate(outs)
        for dz in range(line)
    ]
    wait_for(run_copies(pairs, sems))


def grad_out(where, att, far_att, go, far_go, dps, owner):
    seqs = att.shape[0]
    line, depth, width = seqs // 2, go.shape[1] // dps, go.shape[1] // seqs
    return pl.pallas_call(
        functools.partial(grad_out_kernel, owner),
        in_specs=[SCALAR] + [WHOLE] * 4,
        out_specs=[ANY] * dps,
        out_shape=[like((line, depth, width))] * dps,
        scratch_shapes=[
            pltpu.VMEM((dps, line, depth, width), BF),
            pltpu.SemaphoreType.DMA((dps * line,)),
        ],
        compiler_params=ROOM,
    )(where, att, far_att, go, far_go)


def body(tokens, w_qkv, w_out, vectors, w_fc, b_fc, w_proj, cotangent):
    dps = lax.axis_size("dp")
    seqs = lax.axis_size("seq")
    dp = lax.axis_index("dp")
    sq = lax.axis_index("seq")
    rows, model = tokens.shape
    head_count = model // HD
    slots, owner, wide, send, recv = head_plan(head_count, seqs, w_qkv.shape[1])
    send = jnp.asarray(send)[:, :, None, :]
    recv = jnp.asarray(recv)[:, :, None, :]
    mine = slots * HD
    ff_mine = w_fc.shape[1]
    ratio = seqs // dps
    col = w_proj.shape[1]
    where = jnp.stack([dp, sq]).astype(jnp.int32)
    per, wide_vec = vectors.shape
    own_heads = jnp.asarray(owner)[sq]
    pick = (own_heads[:, None] == jnp.arange(head_count)[None, :]).astype(F32)

    def head_rows(vector):
        return jnp.sum(pick[:, :, None] * vector.reshape(1, head_count, HD), axis=1).reshape(-1)

    def head_spread(vector):
        return jnp.sum(pick[:, :, None] * vector.reshape(slots, 1, HD), axis=0).reshape(-1)

    near, far = near_far(dps)
    copies = lambda block: {k: block for k in range(dps)}
    chunks = lambda blocks: dict(enumerate(blocks))

    lanes = send.shape[3]
    small = jnp.concatenate([vectors.reshape(-1), b_fc])
    count = small.shape[0]
    small = jnp.stack(in_order(small, send_rel(copies(small), "dp", near + far)))
    small = as_rows(small.reshape(1, -1), lanes)[0]
    parts = exchange(pack_columns(where, w_qkv, send, small))
    wf_near = send_rel(copies(w_fc), "dp", near)
    pieces = proj_pieces(where, w_proj.reshape(ratio, ff_mine, col), dps)
    pieces = in_order(pieces[0], send_rel(chunks(pieces), "dp", near + far))
    parts, wf_near, x_own, out_own, pieces, fc_own = phase(
        parts, wf_near, tokens, w_out, pieces, w_fc
    )

    x_all = lax.all_gather(x_own, "seq", axis=0, tiled=True)
    own_qkv = unpack_columns(where, parts, recv, w_qkv.shape[0], 3 * mine)
    wq = in_order(own_qkv, send_rel(copies(own_qkv), "dp", near + far))
    wf_far = send_rel(copies(fc_own), "dp", far)
    line = line_blocks(out_own)
    pieces = exchange(turn_pieces(where, pieces))
    small = parts[:, w_qkv.shape[0] :].reshape(seqs, -1)[:, : dps * count].astype(F32)
    small = jnp.take(small.reshape(seqs, dps, count), dp ^ jnp.arange(dps), axis=1)
    table = small[:, :, : per * wide_vec].reshape(seqs, dps, per, wide_vec)
    table = table.transpose(1, 2, 0, 3).reshape(dps * per, model)
    bias_fc = small[:, :, per * wide_vec :].transpose(1, 0, 2).reshape(-1)
    bias_fc = lax.dynamic_slice_in_dim(bias_fc, sq * ff_mine, ff_mine)[None]
    bias_qkv = jnp.concatenate(
        [head_rows(table[2]), jnp.zeros((mine,), F32), head_rows(table[3])]
    )[None]
    x_all, wq, wf_far, line, pieces, table, bias_qkv, cot = phase(
        x_all, wq, wf_far, line, pieces, table, bias_qkv, cotangent
    )

    gm_all = lax.all_gather(cot, "seq", axis=0, tiled=True)
    wo = {0: line, **send_rel(copies(line), "dp", near)}
    n1_all, qkv, att, lse = attend(where, x_all, table, bias_qkv, wq, rows)
    att, wo, pieces = phase(att, wo, pieces)

    att = exchange(att)
    wo.update(send_rel(copies(wo[0]), "dp", far))
    wo_other = {k: swap_core(wo[k]) for k in [0] + near}
    own_proj = join_columns(pieces)
    att, wo, wo_other, own_proj = phase(att, wo, wo_other, own_proj)
    wo_other.update({k: swap_core(wo[k]) for k in far})
    wp_near = send_rel(copies(own_proj), "dp", near)
    flat = [b for k in range(dps) for b in (wo[k], wo_other[k])]
    r, n2 = out_project(where, att, x_own, table, flat, owner)
    n2, att, own_proj = phase(n2, att, own_proj)

    n2_all = lax.all_gather(n2, "seq", axis=0, tiled=True)
    wp = in_order(own_proj, wp_near, send_rel(copies(own_proj), "dp", far))
    far_att = swap_core(att)
    n2_all, gm_all, wp, far_att = phase(n2_all, gm_all, wp, far_att)
    wf = in_order(fc_own, wf_near, wf_far)
    e, gu, gn2_part, sum_fc = feed(where, n2_all, gm_all, bias_fc, wf, wp, 2 * rows)

    gn2 = lax.psum_scatter(gn2_part, "seq", scatter_dimension=0, tiled=True)
    d_proj = grad_proj(where, gm_all, e, dps)
    proj_first = reduce_first(d_proj)
    d_fc = grad_blocks(where, n2_all, gu, dps)
    d_fc, proj_first, e_late = phase(d_fc, proj_first, e)
    proj_in = reduce_second(d_proj, proj_first)
    mlp = feed_out(where, e_late, wp, 2 * rows)
    gn2, d_fc, mlp, proj_in = phase(gn2, d_fc, mlp, proj_in)

    mlp = lax.psum_scatter(mlp, "seq", scatter_dimension=0, tiled=True)
    activations = (r + (mlp.astype(F32) + table[7])).astype(BF)
    gr, go, ga, sums_two = out_back(where, gn2, r, cot, table, flat, owner)
    fc_first = reduce_first(d_fc)
    ga, go, fc_first = phase(ga, go, fc_first)

    ga = exchange(ga)
    fc_in = reduce_second(d_fc, fc_first)
    d_out = grad_out(where, att, far_att, go, swap_core(go), dps, owner)
    g_proj = split_columns(proj_in, seqs)
    d_out = split_far(d_out)
    ga, d_out, fc_in, g_proj = phase(ga, d_out, fc_in, g_proj)

    out_first = reduce_first(d_out)
    g_proj = exchange(g_proj)
    gqkv, gqkv_sums = attend_back(qkv, ga, lse)
    gqkv, out_first = phase(gqkv, out_first)
    d_qkv = grad_blocks(where, n1_all, gqkv, dps)
    out_in = reduce_second(d_out, out_first)
    d_qkv, gqkv, g_proj = phase(d_qkv, gqkv, g_proj)

    qkv_first = reduce_first(d_qkv)
    gn1_part, norm_sums = grad_rows(where, gqkv, wq, n1_all, 2 * rows)
    gn1_part, qkv_first = phase(gn1_part, qkv_first)
    gn1 = lax.psum_scatter(gn1_part, "seq", scatter_dimension=0, tiled=True)
    qkv_in = reduce_second(d_qkv, qkv_first)
    g_line = total_of(out_in).astype(BF)
    g_fc = total_of(fc_in)
    vector_grads = jnp.concatenate(
        [
            ((norm_sums[0] - table[1] * norm_sums[1]) / table[0])[None],
            norm_sums[1:],
            head_spread(gqkv_sums[0, :mine])[None],
            head_spread(gqkv_sums[0, 2 * mine :])[None],
            sums_two,
        ]
    )
    fc_sums = lax.dynamic_update_slice_in_dim(
        jnp.zeros((dps * seqs * b_fc.shape[0],), F32), sum_fc[0], sq * ff_mine, axis=0
    )
    sums = jnp.concatenate(
        [
            vector_grads.reshape(dps, per, seqs, wide_vec).transpose(0, 2, 1, 3).reshape(
                dps, seqs, per * wide_vec
            ),
            fc_sums.reshape(dps, seqs, -1),
        ],
        axis=2,
    )
    sums = as_rows(sums.transpose(1, 0, 2).reshape(seqs, -1).astype(BF), lanes)
    qkv_in, sums, g_proj, g_fc, g_line = phase(qkv_in, sums, g_proj, g_fc, g_line)

    parts = exchange(repack_columns(where, qkv_in, recv, sums))
    g_proj = {
        k: lax.dynamic_slice_in_dim(g_proj, (dp ^ k) * ratio, ratio, axis=0) for k in range(dps)
    }
    g_proj = in_order(g_proj[0], send_rel(g_proj, "dp", near + far))
    g_proj = proj_rows(where, g_proj, ff_mine)
    g_out = total_of(
        [g_line[0]]
        + [
            lax.ppermute(g_line[dz], "seq", xor_perm(seqs, 2 * dz))
            for dz in range(1, seqs // 2)
        ]
    )
    input_grad = last_norm(gn1, x_own, gr, table)
    parts, g_proj, input_grad, activations = phase(parts, g_proj, input_grad, activations)
    g_qkv = restore_columns(where, parts, send, *w_qkv.shape)
    sums = parts[:, w_qkv.shape[0] :].reshape(seqs, -1)[:, : dps * count].astype(F32)
    sums = sums.sum(axis=0).reshape(dps, count)
    sums = {k: lax.dynamic_index_in_dim(sums, dp ^ k, 0, keepdims=False) for k in range(dps)}
    sums = total_of(in_order(sums[0], send_rel(sums, "dp", near + far)))
    return (
        activations,
        input_grad.T,
        g_qkv,
        g_out,
        sums[: per * wide_vec].reshape(per, wide_vec),
        g_fc,
        sums[per * wide_vec :],
        g_proj,
    )


def solution(mesh):
    rows = P(("dp", "seq"), None)
    grid = P("dp", "seq")
    line = P(("dp", "seq"))
    return jax.shard_map(
        body,
        mesh=mesh,
        in_specs=(rows, grid, grid, grid, grid, line, grid, rows),
        out_specs=(rows, rows, grid, grid, grid, grid, line, grid),
        check_vma=False,
    )
```

```python
import functools
import math

import jax
import jax.numpy as jnp
import numpy as np
from jax import lax
from jax.experimental import pallas as pl
from jax.experimental.pallas import tpu as pltpu
from jax.sharding import PartitionSpec as P

HD = 64
PAIR = 2 * HD
EPSILON = 1e-05
GELU_C = 0.7978845608028654
NEG_FILL = -1e30
BF = jnp.bfloat16
F32 = jnp.float32


def head_plan(head_count, seq_count, width):
    slots = -(-head_count // seq_count)
    slots += slots % 2
    model = head_count * HD

    def tables(turn):
        owner = np.full((seq_count, slots), -1, np.int32)
        for head in range(head_count):
            row = head // seq_count
            owner[(head + turn * row) % seq_count, row] = head
        place = {}
        for dev in range(seq_count):
            for slot in range(slots):
                if owner[dev, slot] >= 0:
                    place[int(owner[dev, slot])] = (dev, slot)
        lists = [[[] for _ in range(seq_count)] for _ in range(seq_count)]
        for col in range(3 * model):
            kind, rest = divmod(col, model)
            head, lane = divmod(rest, HD)
            dev, slot = place[head]
            src, local = divmod(col, width)
            lists[src][dev].append((local, (kind * slots + slot) * HD + lane))
        most = max(len(cell) for row in lists for cell in row)
        return most, owner, lists

    best = min((tables(turn) for turn in range(seq_count)), key=lambda t: t[0])
    most, owner, lists = best
    wide = -(-most // 128) * 128
    send = np.full((seq_count, seq_count, wide), -1, np.int32)
    recv = np.full((seq_count, seq_count, wide), -1, np.int32)
    for src in range(seq_count):
        for dev in range(seq_count):
            for i, (local, target) in enumerate(lists[src][dev]):
                send[src, dev, i] = local
                recv[src, dev, i] = target
    return slots, owner, wide, send, recv


ANY = pl.BlockSpec(memory_space=pl.ANY)
WHOLE = pl.BlockSpec(memory_space=pltpu.VMEM)
SCALAR = pl.BlockSpec(memory_space=pltpu.SMEM)


def blocks_of(*shapes):
    return [pl.BlockSpec(s.shape, lambda n=len(s.shape): (0,) * n) for s in shapes]


ROOM = pltpu.CompilerParams(vmem_limit_bytes=56 * 1024 * 1024)


def like(shape, kind=BF):
    return jax.ShapeDtypeStruct(shape, kind)


def phase(*values):
    return lax.optimization_barrier(values)


def xor_perm(count, k):
    return [(i, i ^ k) for i in range(count)]


def near_far(count):
    every = range(1, count)
    return [k for k in every if not k & (k - 1)], [k for k in every if k & (k - 1)]


def send_rel(blocks, axis, ks):
    count = lax.axis_size(axis)
    return {k: lax.ppermute(blocks[k], axis, xor_perm(count, k)) for k in ks}


def in_order(mine, *found):
    every = {0: mine}
    for part in found:
        every.update(part)
    return [every[k] for k in range(len(every))]


def can_halve(count, rows):
    return count == 4 and rows % 16 == 0


def cut(rows):
    return 16 * (rows // 16 - rows // 32)


def split_far(chunks):
    if len(chunks) != 4:
        return chunks
    far = chunks[3]
    half = far.shape[0] // 2 if far.ndim == 3 else cut(far.shape[0])
    return list(chunks[:3]) + [far[:half], far[half:]]


def reduce_first(chunks):
    if len(chunks) == 5:
        return [
            lax.ppermute(chunks[3], "dp", xor_perm(4, 1)),
            lax.ppermute(chunks[4], "dp", xor_perm(4, 2)),
        ]
    near, far = near_far(len(chunks))
    return list(send_rel(dict(enumerate(chunks)), "dp", far).values())


def reduce_second(chunks, found):
    if len(chunks) == 5:
        first, second = merge_halves(chunks[1], chunks[2], *found)
        return [
            chunks[0],
            lax.ppermute(first, "dp", xor_perm(4, 1)),
            lax.ppermute(second, "dp", xor_perm(4, 2)),
        ]
    near, far = near_far(len(chunks))
    return [chunks[0]] + found + list(send_rel(dict(enumerate(chunks)), "dp", near).values())


def merge_kernel(one_ref, two_ref, top_ref, low_ref, first_ref, second_ref):
    half = top_ref.shape[0]
    first_ref[:half] = one_ref[:half]
    first_ref[half:] = (one_ref[half:].astype(F32) + low_ref[...].astype(F32)).astype(BF)
    second_ref[:half] = (two_ref[:half].astype(F32) + top_ref[...].astype(F32)).astype(BF)
    second_ref[half:] = two_ref[half:]


def merge_halves(one, two, top, low):
    shape = like(one.shape)
    return pl.pallas_call(
        merge_kernel,
        in_specs=[WHOLE] * 4,
        out_specs=blocks_of(shape, shape),
        out_shape=[shape, shape],
        compiler_params=ROOM,
    )(one, two, top, low)


def swap_core(block):
    return lax.ppermute(block, "seq", xor_perm(lax.axis_size("seq"), 1))


def exchange(block):
    return lax.all_to_all(block, "seq", 0, 0, tiled=True)


def total_of(parts):
    total = parts[0].astype(F32)
    for part in parts[1:]:
        total = total + part.astype(F32)
    return total


def as_rows(values, lanes):
    size = -values.shape[1] % (16 * lanes)
    return jnp.pad(values, ((0, 0), (0, size))).reshape(values.shape[0], -1, lanes)


def normalise(rows):
    mean = jnp.mean(rows, axis=-1, keepdims=True)
    centred = rows - mean
    inverse = lax.rsqrt(jnp.mean(centred * centred, axis=-1, keepdims=True) + EPSILON)
    return centred * inverse, inverse


def norm_back(grad, unit, inverse, gain):
    scaled = grad * gain
    return (
        scaled
        - jnp.mean(scaled, axis=-1, keepdims=True)
        - unit * jnp.mean(scaled * unit, axis=-1, keepdims=True)
    ) * inverse


def gelu_parts(u):
    square = u * u
    t = jnp.tanh(u * (GELU_C + GELU_C * 0.044715 * square))
    half = 0.5 + 0.5 * t
    slope = half + u * (0.5 - 0.5 * t * t) * (GELU_C + 3 * 0.044715 * GELU_C * square)
    return u * half, slope


def mm(a, b):
    return jnp.dot(a, b, preferred_element_type=F32)


def mm_nt(a, b):
    return lax.dot_general(a, b, (((1,), (1,)), ((), ())), preferred_element_type=F32)


def mm_tn(a, b):
    return lax.dot_general(a, b, (((0,), (0,)), ((), ())), preferred_element_type=F32)


def run_copies(pairs, sems):
    found = [pltpu.make_async_copy(src, dst, sems.at[i]) for i, (src, dst) in enumerate(pairs)]
    for c in found:
        c.start()
    return found


def wait_for(copies):
    for c in copies:
        c.wait()


def stage_shape(dps, depth, width):
    return (dps, depth, width) if depth % 16 else (1, 16, 128)


def place_rows(where, refs, store, stage, sems, outward=False):
    depth = refs[0].shape[0]
    if outward and len(refs) == 5:
        pairs = []
        for k, ref in zip((0, 1, 2, 3, 3), refs):
            first = (where[0] ^ k) * depth
            if ref is refs[4]:
                first = first + refs[3].shape[0]
            pairs.append((store.at[pl.ds(pl.multiple_of(first, 16), ref.shape[0]), :], ref))
        return run_copies(pairs, sems)
    if depth % 16:
        spots = [stage.at[where[0] ^ k] for k in range(len(refs))]
    else:
        spots = [
            store.at[pl.ds(pl.multiple_of((where[0] ^ k) * depth, 16), depth), :]
            for k in range(len(refs))
        ]
    if outward:
        if depth % 16:
            for p in range(len(refs)):
                stage[p] = store[p * depth : (p + 1) * depth, :]
        return run_copies(list(zip(spots, refs)), sems)
    return run_copies(list(zip(refs, spots)), sems)


def settle_rows(copies, store, stage):
    wait_for(copies)
    depth = stage.shape[1]
    if depth % 16:
        for p in range(stage.shape[0]):
            store[p * depth : (p + 1) * depth, :] = stage[p]


def hot(row, count):
    return (
        lax.broadcasted_iota(jnp.int32, (count, row.shape[1]), 0) == row
    ).astype(BF)


def pack_kernel(where, w_ref, send_ref, more_ref, out_ref):
    depth = w_ref.shape[0]
    for n in range(out_ref.shape[0]):
        out_ref[n, 0:depth] = mm(w_ref[...], hot(send_ref[where[1], n], w_ref.shape[1])).astype(BF)
        out_ref[n, depth:] = more_ref[...]


def pack_columns(where, w_qkv, send, more):
    seqs, _, _, wide = send.shape
    shape = like((seqs, w_qkv.shape[0] + more.shape[0], wide))
    return pl.pallas_call(
        pack_kernel,
        in_specs=[SCALAR, WHOLE, WHOLE, WHOLE],
        out_specs=blocks_of(shape)[0],
        out_shape=shape,
        compiler_params=ROOM,
    )(where, w_qkv, send, more)


def unpack_kernel(where, recv_ref, in_ref, out_ref):
    total = None
    for n in range(in_ref.shape[0]):
        part = mm_nt(in_ref[n, 0 : out_ref.shape[0]], hot(recv_ref[n, where[1]], out_ref.shape[1]))
        total = part if total is None else total + part
    out_ref[...] = total.astype(BF)


def unpack_columns(where, parts, recv, depth, width):
    return pl.pallas_call(
        unpack_kernel,
        in_specs=[SCALAR, WHOLE, WHOLE],
        out_specs=blocks_of(like((depth, width)))[0],
        out_shape=like((depth, width)),
        compiler_params=ROOM,
    )(where, recv, parts)


def repack_kernel(where, recv_ref, more_ref, *rest):
    parts, out_ref = rest[:-1], rest[-1]
    grad = total_of([p[...] for p in parts]).astype(BF)
    depth = grad.shape[0]
    for n in range(out_ref.shape[0]):
        out_ref[n, 0:depth] = mm(grad, hot(recv_ref[n, where[1]], grad.shape[1])).astype(BF)
        out_ref[n, depth:] = more_ref[n]


def repack_columns(where, parts, recv, more):
    seqs, _, _, wide = recv.shape
    shape = like((seqs, parts[0].shape[0] + more.shape[1], wide))
    return pl.pallas_call(
        repack_kernel,
        in_specs=[SCALAR] + [WHOLE] * (2 + len(parts)),
        out_specs=blocks_of(shape)[0],
        out_shape=shape,
        compiler_params=ROOM,
    )(where, recv, more, *parts)


def restore_kernel(where, send_ref, in_ref, out_ref):
    depth = out_ref.shape[0]
    total = None
    for n in range(in_ref.shape[0]):
        part = mm_nt(in_ref[n, 0:depth], hot(send_ref[where[1], n], out_ref.shape[1]))
        total = part if total is None else total + part
    out_ref[...] = total


def restore_columns(where, parts, send, depth, width):
    return pl.pallas_call(
        restore_kernel,
        in_specs=[SCALAR, WHOLE, WHOLE],
        out_specs=blocks_of(like((depth, width)))[0],
        out_shape=like((depth, width), F32),
        compiler_params=ROOM,
    )(where, send, parts)


def piece_rows(total, count):
    tiles = total // 16
    return 16 * -(-tiles // count), lambda q: 16 * ((q * tiles) // count)


def pieces_kernel(where, w_ref, *outs):
    size, start = piece_rows(w_ref.shape[1], len(outs))
    for k, ref in enumerate(outs):
        first = pl.multiple_of(start(where[0] ^ k), 16)
        ref[...] = w_ref[:, pl.ds(first, size), :]


def proj_pieces(where, w_proj, dps):
    ratio, ff_mine, col = w_proj.shape
    size, _ = piece_rows(ff_mine, dps)
    return pl.pallas_call(
        pieces_kernel,
        in_specs=[SCALAR, WHOLE],
        out_specs=blocks_of(*[like((ratio, size, col))] * dps),
        out_shape=[like((ratio, size, col))] * dps,
        compiler_params=ROOM,
    )(where, w_proj)


def turn_kernel(where, *rest):
    ins, (out_ref, sems) = rest[:-2], rest[-2:]
    ratio = ins[0].shape[0]
    spots = [out_ref.at[pl.ds((where[0] ^ k) * ratio, ratio)] for k in range(len(ins))]
    wait_for(run_copies(list(zip(ins, spots)), sems))


def turn_pieces(where, parts):
    ratio, size, col = parts[0].shape
    return pl.pallas_call(
        turn_kernel,
        in_specs=[SCALAR] + [WHOLE] * len(parts),
        out_specs=blocks_of(like((ratio * len(parts), size, col)))[0],
        out_shape=like((ratio * len(parts), size, col)),
        scratch_shapes=[pltpu.SemaphoreType.DMA((len(parts),))],
        compiler_params=ROOM,
    )(where, *parts)


def join_kernel(in_ref, out_ref):
    width = in_ref.shape[2]
    for n in range(in_ref.shape[0]):
        out_ref[:, n * width : (n + 1) * width] = in_ref[n]


def join_columns(parts):
    seqs, size, col = parts.shape
    return pl.pallas_call(
        join_kernel,
        in_specs=[WHOLE],
        out_specs=blocks_of(like((size, col * seqs)))[0],
        out_shape=like((size, col * seqs)),
        compiler_params=ROOM,
    )(parts)


def split_kernel(*refs):
    out_ref = refs[-1]
    total = total_of([r[...] for r in refs[:-1]]).astype(BF)
    width = out_ref.shape[2]
    for n in range(out_ref.shape[0]):
        out_ref[n] = total[:, n * width : (n + 1) * width]


def split_columns(parts, seqs):
    size, model = parts[0].shape
    return pl.pallas_call(
        split_kernel,
        in_specs=[WHOLE] * len(parts),
        out_specs=blocks_of(like((seqs, size, model // seqs)))[0],
        out_shape=like((seqs, size, model // seqs)),
        compiler_params=ROOM,
    )(*parts)


def rows_kernel(where, *rest):
    ins, (out_ref, store, sems) = rest[:-3], rest[-3:]
    dps, ratio, size, _ = store.shape
    ff_mine = out_ref.shape[1] // ratio
    _, start = piece_rows(ff_mine, dps)
    wait_for(run_copies([(ref, store.at[where[0] ^ k]) for k, ref in enumerate(ins)], sems))
    for q in range(dps):
        for b in range(ratio):
            first = b * ff_mine + start(q)
            out_ref[:, first : first + size] = store[q, b].astype(F32).T


def proj_rows(where, parts, ff_mine):
    ratio, size, col = parts[0].shape
    return pl.pallas_call(
        rows_kernel,
        in_specs=[SCALAR] + [ANY] * len(parts),
        out_specs=blocks_of(like((col, ratio * ff_mine)))[0],
        out_shape=like((col, ratio * ff_mine), F32),
        scratch_shapes=[
            pltpu.VMEM((len(parts), ratio, size, col), BF),
            pltpu.SemaphoreType.DMA((len(parts),)),
        ],
        compiler_params=ROOM,
    )(where, *parts)


def head_masks(rows):
    first = lax.broadcasted_iota(jnp.int32, (rows, PAIR), 1) < HD
    causal = lax.broadcasted_iota(jnp.int32, (rows, rows), 0) >= lax.broadcasted_iota(
        jnp.int32, (rows, rows), 1
    )
    return first, causal


def masked_scores(q, keys, causal):
    rows, seen = q.shape[0], keys.shape[0]
    s = mm_nt(q, keys)
    tail = jnp.where(causal, s[:, seen - rows :], NEG_FILL)
    return tail if seen == rows else jnp.concatenate([s[:, : seen - rows], tail], axis=1)


def attend_rows(q, keys, values, first, causal):
    q = q * BF(1.0 / math.sqrt(HD))
    outs, logs = [], []
    for mine in (first, ~first):
        s = masked_scores(jnp.where(mine, q, BF(0)), keys, causal)
        top = jnp.max(s, axis=-1, keepdims=True)
        e = jnp.exp(s - top)
        total = jnp.sum(e, axis=-1, keepdims=True)
        outs.append(mm(e.astype(BF), values) / total)
        logs.append(top + jnp.log(total))
    return jnp.where(first, outs[0], outs[1]).astype(BF), jnp.where(first, logs[0], logs[1])


def attend_kernel(pairs, dps, where, x_ref, vec_ref, bias_ref, *rest):
    w_refs = rest[:dps]
    n1_ref, qkv_ref, att_ref, lse_ref, w, stage, qkv, sems = rest[dps:]
    i = pl.program_id(0)
    rows = x_ref.shape[0]
    part = rows // 2

    @pl.when(i == 0)
    def _():
        settle_rows(place_rows(where, w_refs, w, stage, sems), w, stage)

    unit, _ = normalise(x_ref[...].astype(F32))
    n1 = (unit * vec_ref[0:1, :] + vec_ref[1:2, :]).astype(BF)
    n1_ref[...] = n1
    tile = (mm(n1, w[...]) + bias_ref[...]).astype(BF)
    qkv_ref[...] = tile
    qkv[pl.ds(pl.multiple_of(i * rows, rows), rows), :] = tile
    first, causal = head_masks(rows)
    for j in range(qkv.shape[0] // rows):

        @pl.when(i == j)
        def _(j=j):
            seen = (j + 1) * rows
            for g in range(pairs):
                lanes = slice(g * PAIR, (g + 1) * PAIR)
                keys = qkv[0:seen, (pairs + g) * PAIR : (pairs + g + 1) * PAIR]
                values = qkv[0:seen, (2 * pairs + g) * PAIR : (2 * pairs + g + 1) * PAIR]
                out, log = attend_rows(qkv[j * rows : seen, lanes], keys, values, first, causal)
                for b in range(2):
                    att_ref[b, :, lanes] = out[b * part : (b + 1) * part]
                lse_ref[:, lanes] = log


def attend(where, x_all, table, bias, weights, part):
    length, model = x_all.shape
    depth, width = weights[0].shape
    dps = len(weights)
    heads = width // 3
    rows = 2 * part
    whole = lambda a: pl.BlockSpec(a.shape, lambda i: (0,) * a.ndim)
    tile = lambda cols: pl.BlockSpec((rows, cols), lambda i: (i, 0))
    return pl.pallas_call(
        functools.partial(attend_kernel, heads // PAIR, dps),
        grid=(length // rows,),
        in_specs=[SCALAR, tile(model), whole(table), whole(bias)] + [ANY] * dps,
        out_specs=[
            tile(model),
            tile(width),
            pl.BlockSpec((2, part, heads), lambda i: (i, 0, 0)),
            tile(heads),
            pl.BlockSpec((model, width), lambda i: (0, 0)),
        ],
        out_shape=[
            like((length, model)),
            like((length, width)),
            like((length // part, part, heads)),
            like((length, heads), F32),
            like((model, width)),
        ],
        scratch_shapes=[
            pltpu.VMEM(stage_shape(dps, depth, width), BF),
            pltpu.VMEM((length, width), BF),
            pltpu.SemaphoreType.DMA((dps,)),
        ],
        compiler_params=ROOM,
    )(where, x_all, table, bias, *weights)


def attend_back_kernel(pairs, qkv_ref, ga_ref, lse_ref, gqkv_ref, sums_ref, ak, av):
    length = qkv_ref.shape[0]
    part = ga_ref.shape[1]
    rows = 2 * part
    first, causal = head_masks(rows)
    for g in range(pairs):
        lanes = slice(g * PAIR, (g + 1) * PAIR)
        k_lanes = slice((pairs + g) * PAIR, (pairs + g + 1) * PAIR)
        v_lanes = slice((2 * pairs + g) * PAIR, (2 * pairs + g + 1) * PAIR)
        ak[...] = jnp.zeros_like(ak)
        av[...] = jnp.zeros_like(av)
        for i in range(length // rows):
            here = slice(i * rows, (i + 1) * rows)
            seen = (i + 1) * rows
            q = qkv_ref[here, lanes] * BF(1.0 / math.sqrt(HD))
            ga = jnp.concatenate([ga_ref[b, :, lanes] for b in (2 * i, 2 * i + 1)], axis=0)
            keys = qkv_ref[0:seen, k_lanes]
            values = qkv_ref[0:seen, v_lanes]
            grads = []
            for h, mine in enumerate((first, ~first)):
                q_h = jnp.where(mine, q, BF(0))
                ga_h = jnp.where(mine, ga, BF(0))
                s = masked_scores(q_h, keys, causal)
                lane = g * PAIR + h * HD
                p = jnp.exp(s - lse_ref[here, lane : lane + 1])
                gp = mm_nt(ga_h, values)
                centre = jnp.sum(p * gp, axis=-1, keepdims=True)
                gs = (p * (gp - centre)).astype(BF)
                av[0:seen, :] += mm_tn(p.astype(BF), ga_h)
                ak[0:seen, :] += mm_tn(gs, q_h)
                grads.append(mm(gs, keys))
            gqkv_ref[here, lanes] = (
                jnp.where(first, grads[0], grads[1]) * (1.0 / math.sqrt(HD))
            ).astype(BF)
        gqkv_ref[:, k_lanes] = ak[...].astype(BF)
        gqkv_ref[:, v_lanes] = av[...].astype(BF)
    sums_ref[...] = jnp.sum(gqkv_ref[...].astype(F32), axis=0, keepdims=True)


def attend_back(qkv, grad, lse):
    length, width = qkv.shape
    return pl.pallas_call(
        functools.partial(attend_back_kernel, grad.shape[2] // PAIR),
        in_specs=[WHOLE] * 3,
        out_specs=[WHOLE, WHOLE],
        out_shape=[like((length, width)), like((1, width), F32)],
        scratch_shapes=[pltpu.VMEM((length, PAIR), F32), pltpu.VMEM((length, PAIR), F32)],
        compiler_params=ROOM,
    )(qkv, grad, lse)


def grad_blocks_kernel(where, a_ref, g_ref, *rest):
    outs, (store, stage, sems) = rest[:-3], rest[-3:]
    g = g_ref[...]
    model = a_ref.shape[1]
    for a in range(0, model, 256):
        b = min(model, a + 256)
        store[a:b, :] = mm_tn(a_ref[:, a:b], g).astype(BF)
    wait_for(place_rows(where, outs, store, stage, sems, True))


def chunk_shapes(count, rows, cols):
    shapes = [like((rows, cols))] * count
    if can_halve(count, rows):
        shapes[3:] = [like((cut(rows), cols)), like((rows - cut(rows), cols))]
    return shapes


def grad_blocks(where, a, g, dps):
    model, width = a.shape[1], g.shape[1]
    depth = model // dps
    shapes = chunk_shapes(dps, depth, width)
    return pl.pallas_call(
        grad_blocks_kernel,
        in_specs=[SCALAR, WHOLE, WHOLE],
        out_specs=[ANY] * len(shapes),
        out_shape=shapes,
        scratch_shapes=[
            pltpu.VMEM((model, width), BF),
            pltpu.VMEM(stage_shape(dps, depth, width), BF),
            pltpu.SemaphoreType.DMA((len(shapes),)),
        ],
        compiler_params=ROOM,
    )(where, a, g)


def grad_rows_kernel(g_ref, n1_ref, w_ref, out_ref, sums_ref):
    @pl.when(pl.program_id(0) == 0)
    def _():
        sums_ref[...] = jnp.zeros_like(sums_ref)

    grad = mm_nt(g_ref[...], w_ref[...])
    sums_ref[0:1, :] += jnp.sum(grad * n1_ref[...].astype(F32), axis=0, keepdims=True)
    sums_ref[1:2, :] += jnp.sum(grad, axis=0, keepdims=True)
    out_ref[...] = grad.astype(BF)


def grad_rows(gqkv, weights, n1, rows):
    length, model = n1.shape
    width = weights.shape[1]
    tile = lambda cols: pl.BlockSpec((rows, cols), lambda i: (i, 0))
    return pl.pallas_call(
        grad_rows_kernel,
        grid=(length // rows,),
        in_specs=[tile(width), tile(model), WHOLE],
        out_specs=[tile(model), pl.BlockSpec((2, model), lambda i: (0, 0))],
        out_shape=[like((length, model)), like((2, model), F32)],
        compiler_params=ROOM,
    )(gqkv, n1, weights)


def place_pieces(where, refs, store, sems):
    size, start = piece_rows(store.shape[0], len(refs))
    starts = [start(q) for q in range(len(refs))] + [store.shape[0]]
    least = min(b - a for a, b in zip(starts, starts[1:]))
    count = len(refs)
    copies, more = [], []
    for k, ref in enumerate(refs):
        first = start(where[0] ^ k)
        spot = pl.ds(pl.multiple_of(first, 16), least)
        copies.append(
            pltpu.make_async_copy(ref.at[pl.ds(0, least), :], store.at[spot, :], sems.at[k])
        )
        if size > least:
            spot = pl.ds(pl.multiple_of(first + least, 16), size - least)
            rest = ref.at[pl.ds(least, size - least), :]
            more.append(
                (
                    start((where[0] ^ k) + 1) - first > least,
                    pltpu.make_async_copy(rest, store.at[spot, :], sems.at[count + k]),
                )
            )
    for c in copies:
        c.start()
    for needed, c in more:
        pl.when(needed)(c.start)
    wait_for(copies)
    for needed, c in more:
        pl.when(needed)(c.wait)


def gather_fc_kernel(where, *rest):
    f_refs, (wf, stage, sems) = rest[:-3], rest[-3:]
    settle_rows(place_rows(where, f_refs, wf, stage, sems), wf, stage)


def gather_fc(where, fc):
    dps = len(fc)
    depth, width = fc[0].shape
    return pl.pallas_call(
        gather_fc_kernel,
        in_specs=[SCALAR] + [ANY] * dps,
        out_specs=WHOLE,
        out_shape=like((depth * dps, width)),
        scratch_shapes=[
            pltpu.VMEM(stage_shape(dps, depth, width), BF),
            pltpu.SemaphoreType.DMA((dps,)),
        ],
        compiler_params=ROOM,
    )(where, *fc)


def gather_proj_kernel(where, *rest):
    p_refs, (wp, sems) = rest[:-2], rest[-2:]
    place_pieces(where, p_refs, wp, sems)


def gather_proj(where, proj, ff_mine):
    dps = len(proj)
    return pl.pallas_call(
        gather_proj_kernel,
        in_specs=[SCALAR] + [ANY] * dps,
        out_specs=WHOLE,
        out_shape=like((ff_mine, proj[0].shape[1])),
        scratch_shapes=[pltpu.SemaphoreType.DMA((2 * dps,))],
        compiler_params=ROOM,
    )(where, *proj)


def feed_kernel(n2_ref, gm_ref, bias_ref, wf, wp, e_ref, gu_ref, gn2_ref, sum_ref):
    @pl.when(pl.program_id(0) == 0)
    def _():
        sum_ref[...] = jnp.zeros_like(sum_ref)

    u = mm(n2_ref[...], wf[...]) + bias_ref[...]
    ge = mm_nt(gm_ref[...], wp[...])
    value, slope = gelu_parts(u)
    e_ref[...] = value.astype(BF)
    gu = (ge * slope).astype(BF)
    gu_ref[...] = gu
    sum_ref[...] += jnp.sum(gu.astype(F32), axis=0, keepdims=True)
    gn2_ref[...] = mm_nt(gu, wf[...]).astype(BF)


def feed(n2, gm, bias, fc, proj, rows):
    length, model = n2.shape
    width = fc.shape[1]
    whole = lambda shape: pl.BlockSpec(shape, lambda i: (0,) * len(shape))
    tile = lambda cols: pl.BlockSpec((rows, cols), lambda i: (i, 0))
    return pl.pallas_call(
        feed_kernel,
        grid=(length // rows,),
        in_specs=[tile(model), tile(model), whole(bias.shape), WHOLE, WHOLE],
        out_specs=[tile(width), tile(width), tile(model), whole((1, width))],
        out_shape=[
            like((length, width)),
            like((length, width)),
            like((length, model)),
            like((1, width), F32),
        ],
        compiler_params=ROOM,
    )(n2, gm, bias, fc, proj)


def grad_proj_kernel(dps, where, gm_ref, e_ref, *rest):
    outs, (store, sems) = rest[:-2], rest[-2:]
    width = store.shape[0]
    for a in range(0, width, 256):
        b = min(width, a + 256)
        store[a:b, :] = mm_tn(e_ref[:, a:b], gm_ref[...]).astype(BF)
    _, start = piece_rows(width, dps)
    pairs = []
    for i, ref in enumerate(outs):
        first = start(where[0] ^ min(i, dps - 1))
        if i == dps:
            first = first + outs[i - 1].shape[0]
        pairs.append((store.at[pl.ds(pl.multiple_of(first, 16), ref.shape[0]), :], ref))
    wait_for(run_copies(pairs, sems))


def grad_proj(where, gm, e, dps):
    model, width = gm.shape[1], e.shape[1]
    size, _ = piece_rows(width, dps)
    shapes = chunk_shapes(dps, size, model)
    return pl.pallas_call(
        functools.partial(grad_proj_kernel, dps),
        in_specs=[SCALAR, WHOLE, WHOLE],
        out_specs=[ANY] * len(shapes),
        out_shape=shapes,
        scratch_shapes=[
            pltpu.VMEM((width, model), BF),
            pltpu.SemaphoreType.DMA((len(shapes),)),
        ],
        compiler_params=ROOM,
    )(where, gm, e)


def feed_out_kernel(e_ref, wp, out_ref):
    out_ref[...] = mm(e_ref[...], wp[...]).astype(BF)


def feed_out(e, proj, rows):
    length, width = e.shape
    model = proj.shape[1]
    return pl.pallas_call(
        feed_out_kernel,
        grid=(length // rows,),
        in_specs=[pl.BlockSpec((rows, width), lambda i: (i, 0)), WHOLE],
        out_specs=pl.BlockSpec((rows, model), lambda i: (i, 0)),
        out_shape=like((length, model)),
        compiler_params=ROOM,
    )(e, proj)


def last_kernel(gn1_ref, gr_ref, vec_ref, x_hbm, out_ref, x_ref, sem):
    copy = pltpu.make_async_copy(x_hbm, x_ref, sem)
    copy.start()
    copy.wait()
    unit, inverse = normalise(x_ref[...].astype(F32))
    grad = norm_back(gn1_ref[...].astype(F32), unit, inverse, vec_ref[0:1, :])
    out_ref[...] = (gr_ref[...] + grad).T.astype(BF)


def last_norm(gn1, x, gr, table):
    shape = like(x.shape[::-1])
    return pl.pallas_call(
        last_kernel,
        in_specs=[WHOLE] * 3 + [ANY],
        out_specs=blocks_of(shape)[0],
        out_shape=shape,
        scratch_shapes=[pltpu.VMEM(x.shape, BF), pltpu.SemaphoreType.DMA],
        compiler_params=ROOM,
    )(gn1, gr, table, x)


def output_kernel(r_ref, mlp_ref, vec_ref, out_ref):
    out = r_ref[...] + (mlp_ref[...].astype(F32) + vec_ref[7:8, :])
    out_ref[...] = out.T.astype(BF)


def output_rows(r, mlp, table):
    shape = like(r.shape[::-1])
    return pl.pallas_call(
        output_kernel,
        in_specs=[WHOLE] * 3,
        out_specs=blocks_of(shape)[0],
        out_shape=shape,
        compiler_params=ROOM,
    )(r, mlp, table)


def line_blocks(block):
    seqs = lax.axis_size("seq")
    return jnp.stack(
        [block]
        + [lax.ppermute(block, "seq", xor_perm(seqs, 2 * dz)) for dz in range(1, seqs // 2)]
    )


def block_pairs(where, flat, store):
    return [
        (ref.at[dz], store.at[where[0] ^ (i // 2), where[1] ^ (2 * dz + i % 2)])
        for i, ref in enumerate(flat)
        for dz in range(ref.shape[0])
    ]


def head_columns(att_ref, owner):
    count = int(owner.max()) + 1
    parts = []
    for h in range(count):
        dev, slot = [int(i[0]) for i in np.where(owner == h)]
        parts.append(att_ref[dev, :, slot * HD : (slot + 1) * HD])
    return jnp.concatenate(parts, axis=1)


def block_scratch(flat):
    line, depth, width = flat[0].shape
    dps = len(flat) // 2
    return [
        pltpu.VMEM((dps, 2 * line, depth, width), BF),
        pltpu.SemaphoreType.DMA((dps * 2 * line + 1,)),
    ]


def out_kernel(owner, where, att_ref, vec_ref, x_hbm, *rest):
    flat, (r_ref, n2_ref, store, sems, x_ref) = rest[:-5], rest[-5:]
    copies = run_copies(block_pairs(where, flat, store) + [(x_hbm, x_ref)], sems)
    att = head_columns(att_ref, owner)
    dps, seqs, depth, width = store.shape
    wait_for(copies)
    for n in range(seqs):
        here = slice(n * width, (n + 1) * width)
        total = x_ref[:, here].astype(F32) + vec_ref[4:5, here]
        for p in range(dps):
            total = total + mm(att[:, p * depth : (p + 1) * depth], store[p, n])
        r_ref[:, here] = total
    unit, _ = normalise(r_ref[...])
    n2_ref[...] = (unit * vec_ref[5:6, :] + vec_ref[6:7, :]).astype(BF)


def out_project(where, att, x, table, flat, owner):
    return pl.pallas_call(
        functools.partial(out_kernel, owner),
        in_specs=[SCALAR, WHOLE, WHOLE, ANY] + [ANY] * len(flat),
        out_specs=blocks_of(x, x),
        out_shape=[like(x.shape, F32), like(x.shape)],
        scratch_shapes=block_scratch(flat) + [pltpu.VMEM(x.shape, BF)],
        compiler_params=ROOM,
    )(where, att, table, x, *flat)


def back_kernel(owner, where, gn2_ref, r_ref, vec_ref, g_hbm, *rest):
    flat = rest[:-7]
    gr_ref, go_ref, ga_ref, sums_ref, store, sems, g_ref = rest[-7:]
    copies = run_copies([(g_hbm, g_ref)] + block_pairs(where, flat, store), sems)
    copies[0].wait()
    dps, seqs, depth, width = store.shape
    gn2 = gn2_ref[...].astype(F32)
    unit, inverse = normalise(r_ref[...])
    gr = g_ref[...].astype(F32) + norm_back(gn2, unit, inverse, vec_ref[5:6, :])
    go = gr.astype(BF)
    gr_ref[...] = gr
    go_ref[...] = go
    sums_ref[0:1, :] = jnp.sum(go.astype(F32), axis=0, keepdims=True)
    sums_ref[1:2, :] = jnp.sum(gn2 * unit, axis=0, keepdims=True)
    sums_ref[2:3, :] = jnp.sum(gn2, axis=0, keepdims=True)
    sums_ref[3:4, :] = jnp.sum(g_ref[...].astype(F32), axis=0, keepdims=True)
    wait_for(copies[1:])
    found = []
    for p in range(dps):
        total = mm_nt(go[:, 0:width], store[p, 0])
        for n in range(1, seqs):
            total = total + mm_nt(go[:, n * width : (n + 1) * width], store[p, n])
        found.append(total)
    ga = jnp.concatenate(found, axis=1).astype(BF)
    ga_ref[...] = jnp.zeros_like(ga_ref)
    for h in range(int(owner.max()) + 1):
        dev, slot = [int(i[0]) for i in np.where(owner == h)]
        ga_ref[dev, :, slot * HD : (slot + 1) * HD] = ga[:, h * HD : (h + 1) * HD]


def out_back(where, gn2, r, g, table, flat, owner):
    shapes = [
        like(r.shape, F32),
        like(r.shape),
        like((owner.shape[0], r.shape[0], owner.shape[1] * HD)),
        like((4, r.shape[1]), F32),
    ]
    return pl.pallas_call(
        functools.partial(back_kernel, owner),
        in_specs=[SCALAR, WHOLE, WHOLE, WHOLE, ANY] + [ANY] * len(flat),
        out_specs=blocks_of(*shapes),
        out_shape=shapes,
        scratch_shapes=block_scratch(flat) + [pltpu.VMEM(g.shape, BF)],
        compiler_params=ROOM,
    )(where, gn2, r, table, g, *flat)


def grad_out_kernel(owner, where, att_ref, far_att_ref, go_ref, far_go_ref, *rest):
    outs, (store, sems) = rest[:-2], rest[-2:]
    att = jnp.concatenate([head_columns(r, owner) for r in (att_ref, far_att_ref)], axis=0)
    go = jnp.concatenate([go_ref[...], far_go_ref[...]], axis=0)
    dps, line, depth, width = store.shape
    even = where[1] % 2 == 0
    for z in range(line):
        a, b = 2 * z * width, (2 * z + 1) * width
        cols = jnp.where(even, go[:, a : a + width], go[:, b : b + width])
        for p in range(dps):
            store[p, z] = mm_tn(att[:, p * depth : (p + 1) * depth], cols).astype(BF)
    pairs = [
        (store.at[where[0] ^ k, (where[1] // 2) ^ dz], ref.at[dz])
        for k, ref in enumerate(outs)
        for dz in range(line)
    ]
    wait_for(run_copies(pairs, sems))


def grad_out(where, att, far_att, go, far_go, dps, owner):
    seqs = att.shape[0]
    line, depth, width = seqs // 2, go.shape[1] // dps, go.shape[1] // seqs
    return pl.pallas_call(
        functools.partial(grad_out_kernel, owner),
        in_specs=[SCALAR] + [WHOLE] * 4,
        out_specs=[ANY] * dps,
        out_shape=[like((line, depth, width))] * dps,
        scratch_shapes=[
            pltpu.VMEM((dps, line, depth, width), BF),
            pltpu.SemaphoreType.DMA((dps * line,)),
        ],
        compiler_params=ROOM,
    )(where, att, far_att, go, far_go)


def body(tokens, w_qkv, w_out, vectors, w_fc, b_fc, w_proj, cotangent):
    dps = lax.axis_size("dp")
    seqs = lax.axis_size("seq")
    dp = lax.axis_index("dp")
    sq = lax.axis_index("seq")
    rows, model = tokens.shape
    head_count = model // HD
    slots, owner, wide, send, recv = head_plan(head_count, seqs, w_qkv.shape[1])
    send = jnp.asarray(send)[:, :, None, :]
    recv = jnp.asarray(recv)[:, :, None, :]
    mine = slots * HD
    ff_mine = w_fc.shape[1]
    ratio = seqs // dps
    col = w_proj.shape[1]
    where = jnp.stack([dp, sq]).astype(jnp.int32)
    per, wide_vec = vectors.shape
    own_heads = jnp.asarray(owner)[sq]
    pick = (own_heads[:, None] == jnp.arange(head_count)[None, :]).astype(F32)

    def head_rows(vector):
        return jnp.sum(pick[:, :, None] * vector.reshape(1, head_count, HD), axis=1).reshape(-1)

    def head_spread(vector):
        return jnp.sum(pick[:, :, None] * vector.reshape(slots, 1, HD), axis=0).reshape(-1)

    near, far = near_far(dps)
    copies = lambda block: {k: block for k in range(dps)}
    chunks = lambda blocks: dict(enumerate(blocks))

    lanes = send.shape[3]
    small = jnp.concatenate([vectors.reshape(-1), b_fc])
    count = small.shape[0]
    small = jnp.stack(in_order(small, send_rel(copies(small), "dp", near + far)))
    small = as_rows(small.reshape(1, -1), lanes)[0]
    parts = exchange(pack_columns(where, w_qkv, send, small))
    wf_near = send_rel(copies(w_fc), "dp", near)
    pieces = proj_pieces(where, w_proj.reshape(ratio, ff_mine, col), dps)
    pieces = in_order(pieces[0], send_rel(chunks(pieces), "dp", near + far))
    parts, wf_near, x_own, out_own, pieces, fc_own = phase(
        parts, wf_near, tokens, w_out, pieces, w_fc
    )

    x_all = lax.all_gather(x_own, "seq", axis=0, tiled=True)
    own_qkv = unpack_columns(where, parts, recv, w_qkv.shape[0], 3 * mine)
    wq = in_order(own_qkv, send_rel(copies(own_qkv), "dp", near + far))
    wf_far = send_rel(copies(fc_own), "dp", far)
    line = line_blocks(out_own)
    pieces = exchange(turn_pieces(where, pieces))
    small = parts[:, w_qkv.shape[0] :].reshape(seqs, -1)[:, : dps * count].astype(F32)
    small = jnp.take(small.reshape(seqs, dps, count), dp ^ jnp.arange(dps), axis=1)
    table = small[:, :, : per * wide_vec].reshape(seqs, dps, per, wide_vec)
    table = table.transpose(1, 2, 0, 3).reshape(dps * per, model)
    bias_fc = small[:, :, per * wide_vec :].transpose(1, 0, 2).reshape(-1)
    bias_fc = lax.dynamic_slice_in_dim(bias_fc, sq * ff_mine, ff_mine)[None]
    bias_qkv = jnp.concatenate(
        [head_rows(table[2]), jnp.zeros((mine,), F32), head_rows(table[3])]
    )[None]
    x_all, wq, wf_far, line, pieces, table, bias_qkv, cot = phase(
        x_all, wq, wf_far, line, pieces, table, bias_qkv, cotangent
    )

    gm_all = lax.all_gather(cot, "seq", axis=0, tiled=True)
    wo = {0: line, **send_rel(copies(line), "dp", near)}
    n1_all, qkv, att, lse, wq = attend(where, x_all, table, bias_qkv, wq, rows)
    att, wo, pieces = phase(att, wo, pieces)

    att = exchange(att)
    wo.update(send_rel(copies(wo[0]), "dp", far))
    wo_other = {k: swap_core(wo[k]) for k in [0] + near}
    own_proj = join_columns(pieces)
    att, wo, wo_other, own_proj = phase(att, wo, wo_other, own_proj)
    wo_other.update({k: swap_core(wo[k]) for k in far})
    wp_near = send_rel(copies(own_proj), "dp", near)
    flat = [b for k in range(dps) for b in (wo[k], wo_other[k])]
    r, n2 = out_project(where, att, x_own, table, flat, owner)
    n2, att, own_proj = phase(n2, att, own_proj)

    n2_all = lax.all_gather(n2, "seq", axis=0, tiled=True)
    wp = in_order(own_proj, wp_near, send_rel(copies(own_proj), "dp", far))
    far_att = swap_core(att)
    wf = in_order(fc_own, wf_near, wf_far)
    wf = gather_fc(where, wf)
    wf, wp = phase(wf, wp)
    wp = gather_proj(where, wp, ff_mine)
    n2_all, gm_all, wp, far_att = phase(n2_all, gm_all, wp, far_att)
    e, gu, gn2_part, sum_fc = feed(n2_all, gm_all, bias_fc, wf, wp, 2 * rows)

    gn2 = lax.psum_scatter(gn2_part, "seq", scatter_dimension=0, tiled=True)
    d_proj = grad_proj(where, gm_all, e, dps)
    proj_first = reduce_first(d_proj)
    d_fc = grad_blocks(where, n2_all, gu, dps)
    d_fc, proj_first, e_late = phase(d_fc, proj_first, e)
    proj_in = reduce_second(d_proj, proj_first)
    mlp = feed_out(e_late, wp, 2 * rows)
    gn2, d_fc, mlp, proj_in = phase(gn2, d_fc, mlp, proj_in)

    mlp = lax.psum_scatter(mlp, "seq", scatter_dimension=0, tiled=True)
    gr, go, ga, sums_two = out_back(where, gn2, r, cot, table, flat, owner)
    fc_first = reduce_first(d_fc)
    ga, go, fc_first = phase(ga, go, fc_first)

    ga = exchange(ga)
    d_out = split_far(grad_out(where, att, far_att, go, swap_core(go), dps, owner))
    g_proj = split_columns(proj_in, seqs)
    fc_in = reduce_second(d_fc, fc_first)
    ga, d_out, fc_in, g_proj = phase(ga, d_out, fc_in, g_proj)

    out_first = reduce_first(d_out)
    g_proj = exchange(g_proj)
    gqkv, gqkv_sums = attend_back(qkv, ga, lse)
    gqkv, out_first = phase(gqkv, out_first)
    gn1_part, norm_sums = grad_rows(gqkv, wq, n1_all, 2 * rows)
    gn1_part, gqkv, mlp, g_proj, d_out = phase(gn1_part, gqkv, mlp, g_proj, d_out)

    gn1 = lax.psum_scatter(gn1_part, "seq", scatter_dimension=0, tiled=True)
    out_in = reduce_second(d_out, out_first)
    d_qkv = grad_blocks(where, n1_all, gqkv, dps)
    d_qkv, out_in = phase(d_qkv, out_in)
    qkv_first = reduce_first(d_qkv)
    g_line = total_of(out_in).astype(BF)
    out_in = [g_line[0]] + [
        lax.ppermute(g_line[dz], "seq", xor_perm(seqs, 2 * dz)) for dz in range(1, seqs // 2)
    ]
    qkv_in = reduce_second(d_qkv, qkv_first)
    activations = output_rows(r, mlp, table)
    g_fc = total_of(fc_in)
    g_proj = {
        k: lax.dynamic_slice_in_dim(g_proj, (dp ^ k) * ratio, ratio, axis=0) for k in range(dps)
    }
    g_proj = in_order(g_proj[0], send_rel(g_proj, "dp", near + far))
    g_proj = proj_rows(where, g_proj, ff_mine)
    vector_grads = jnp.concatenate(
        [
            ((norm_sums[0] - table[1] * norm_sums[1]) / table[0])[None],
            norm_sums[1:],
            head_spread(gqkv_sums[0, :mine])[None],
            head_spread(gqkv_sums[0, 2 * mine :])[None],
            sums_two,
        ]
    )
    fc_sums = lax.dynamic_update_slice_in_dim(
        jnp.zeros((dps * seqs * b_fc.shape[0],), F32), sum_fc[0], sq * ff_mine, axis=0
    )
    sums = jnp.concatenate(
        [
            vector_grads.reshape(dps, per, seqs, wide_vec).transpose(0, 2, 1, 3).reshape(
                dps, seqs, per * wide_vec
            ),
            fc_sums.reshape(dps, seqs, -1),
        ],
        axis=2,
    )
    sums = as_rows(sums.transpose(1, 0, 2).reshape(seqs, -1).astype(BF), lanes)
    qkv_in, sums, activations, g_fc, out_in = phase(qkv_in, sums, activations, g_fc, out_in)
    g_out = total_of(out_in)

    parts = exchange(repack_columns(where, qkv_in, recv, sums))
    input_grad = last_norm(gn1, x_own, gr, table)
    parts, input_grad, g_proj, g_out = phase(parts, input_grad, g_proj, g_out)
    g_qkv = restore_columns(where, parts, send, *w_qkv.shape)
    sums = parts[:, w_qkv.shape[0] :].reshape(seqs, -1)[:, : dps * count].astype(F32)
    sums = sums.sum(axis=0).reshape(dps, count)
    sums = {k: lax.dynamic_index_in_dim(sums, dp ^ k, 0, keepdims=False) for k in range(dps)}
    sums = total_of(in_order(sums[0], send_rel(sums, "dp", near + far)))
    return (
        activations.T,
        input_grad.T,
        g_qkv,
        g_out,
        sums[: per * wide_vec].reshape(per, wide_vec),
        g_fc,
        sums[per * wide_vec :],
        g_proj.T,
    )


def solution(mesh):
    rows = P(("dp", "seq"), None)
    grid = P("dp", "seq")
    line = P(("dp", "seq"))
    return jax.shard_map(
        body,
        mesh=mesh,
        in_specs=(rows, grid, grid, grid, grid, line, grid, rows),
        out_specs=(rows, rows, grid, grid, grid, grid, line, grid),
        check_vma=False,
    )
```

```python
import functools
import math

import jax
import jax.numpy as jnp
import numpy as np
from jax import lax
from jax.experimental import pallas as pl
from jax.experimental.pallas import tpu as pltpu
from jax.sharding import PartitionSpec as P

HD = 64
PAIR = 2 * HD
EPSILON = 1e-05
GELU_C = 0.7978845608028654
NEG_FILL = -1e30
BF = jnp.bfloat16
F32 = jnp.float32


def head_plan(head_count, seq_count, width):
    slots = -(-head_count // seq_count)
    slots += slots % 2
    model = head_count * HD

    def tables(turn):
        owner = np.full((seq_count, slots), -1, np.int32)
        for head in range(head_count):
            row = head // seq_count
            owner[(head + turn * row) % seq_count, row] = head
        place = {}
        for dev in range(seq_count):
            for slot in range(slots):
                if owner[dev, slot] >= 0:
                    place[int(owner[dev, slot])] = (dev, slot)
        lists = [[[] for _ in range(seq_count)] for _ in range(seq_count)]
        for col in range(3 * model):
            kind, rest = divmod(col, model)
            head, lane = divmod(rest, HD)
            dev, slot = place[head]
            src, local = divmod(col, width)
            lists[src][dev].append((local, (kind * slots + slot) * HD + lane))
        most = max(len(cell) for row in lists for cell in row)
        return most, owner, lists

    best = min((tables(turn) for turn in range(seq_count)), key=lambda t: t[0])
    most, owner, lists = best
    wide = -(-most // 128) * 128
    send = np.full((seq_count, seq_count, wide), -1, np.int32)
    recv = np.full((seq_count, seq_count, wide), -1, np.int32)
    for src in range(seq_count):
        for dev in range(seq_count):
            for i, (local, target) in enumerate(lists[src][dev]):
                send[src, dev, i] = local
                recv[src, dev, i] = target
    return slots, owner, wide, send, recv


ANY = pl.BlockSpec(memory_space=pl.ANY)
WHOLE = pl.BlockSpec(memory_space=pltpu.VMEM)
SCALAR = pl.BlockSpec(memory_space=pltpu.SMEM)


def blocks_of(*shapes):
    return [pl.BlockSpec(s.shape, lambda n=len(s.shape): (0,) * n) for s in shapes]


ROOM = pltpu.CompilerParams(vmem_limit_bytes=56 * 1024 * 1024)


def like(shape, kind=BF):
    return jax.ShapeDtypeStruct(shape, kind)


def phase(*values):
    return lax.optimization_barrier(values)


def xor_perm(count, k):
    return [(i, i ^ k) for i in range(count)]


def near_far(count):
    every = range(1, count)
    return [k for k in every if not k & (k - 1)], [k for k in every if k & (k - 1)]


def send_rel(blocks, axis, ks):
    count = lax.axis_size(axis)
    return {k: lax.ppermute(blocks[k], axis, xor_perm(count, k)) for k in ks}


def in_order(mine, *found):
    every = {0: mine}
    for part in found:
        every.update(part)
    return [every[k] for k in range(len(every))]


def can_halve(count, rows):
    return count == 4 and rows % 16 == 0


def cut(rows):
    return 16 * (rows // 16 - rows // 32)


def split_far(chunks):
    if len(chunks) != 4:
        return chunks
    far = chunks[3]
    half = far.shape[0] // 2 if far.ndim == 3 else cut(far.shape[0])
    return list(chunks[:3]) + [far[:half], far[half:]]


def reduce_first(chunks):
    if len(chunks) == 5:
        return [
            lax.ppermute(chunks[3], "dp", xor_perm(4, 1)),
            lax.ppermute(chunks[4], "dp", xor_perm(4, 2)),
        ]
    near, far = near_far(len(chunks))
    return list(send_rel(dict(enumerate(chunks)), "dp", far).values())


def reduce_second(chunks, found):
    if len(chunks) == 5:
        first, second = merge_halves(chunks[1], chunks[2], *found)
        return [
            chunks[0],
            lax.ppermute(first, "dp", xor_perm(4, 1)),
            lax.ppermute(second, "dp", xor_perm(4, 2)),
        ]
    near, far = near_far(len(chunks))
    return [chunks[0]] + found + list(send_rel(dict(enumerate(chunks)), "dp", near).values())


def merge_kernel(one_ref, two_ref, top_ref, low_ref, first_ref, second_ref):
    half = top_ref.shape[0]
    first_ref[:half] = one_ref[:half]
    first_ref[half:] = (one_ref[half:].astype(F32) + low_ref[...].astype(F32)).astype(BF)
    second_ref[:half] = (two_ref[:half].astype(F32) + top_ref[...].astype(F32)).astype(BF)
    second_ref[half:] = two_ref[half:]


def merge_halves(one, two, top, low):
    shape = like(one.shape)
    return pl.pallas_call(
        merge_kernel,
        in_specs=[WHOLE] * 4,
        out_specs=blocks_of(shape, shape),
        out_shape=[shape, shape],
        compiler_params=ROOM,
    )(one, two, top, low)


def gather_far(found, far):
    if len(found) + len(far) != 4:
        return {(k, 0): b for k, b in send_rel({k: found[0, 0] for k in far}, "dp", far).items()}
    half = found[0, 0].shape[0] // 2
    return {
        (3, 0): lax.ppermute(found[2, 0][:half], "dp", xor_perm(4, 1)),
        (3, half): lax.ppermute(found[1, 0][half:], "dp", xor_perm(4, 2)),
    }


def swap_core(block):
    return lax.ppermute(block, "seq", xor_perm(lax.axis_size("seq"), 1))


def exchange(block):
    return lax.all_to_all(block, "seq", 0, 0, tiled=True)


def total_of(parts):
    total = parts[0].astype(F32)
    for part in parts[1:]:
        total = total + part.astype(F32)
    return total


def as_rows(values, lanes):
    size = -values.shape[1] % (16 * lanes)
    return jnp.pad(values, ((0, 0), (0, size))).reshape(values.shape[0], -1, lanes)


def normalise(rows):
    mean = jnp.mean(rows, axis=-1, keepdims=True)
    centred = rows - mean
    inverse = lax.rsqrt(jnp.mean(centred * centred, axis=-1, keepdims=True) + EPSILON)
    return centred * inverse, inverse


def norm_back(grad, unit, inverse, gain):
    scaled = grad * gain
    return (
        scaled
        - jnp.mean(scaled, axis=-1, keepdims=True)
        - unit * jnp.mean(scaled * unit, axis=-1, keepdims=True)
    ) * inverse


def gelu_parts(u):
    square = u * u
    t = jnp.tanh(u * (GELU_C + GELU_C * 0.044715 * square))
    half = 0.5 + 0.5 * t
    slope = half + u * (0.5 - 0.5 * t * t) * (GELU_C + 3 * 0.044715 * GELU_C * square)
    return u * half, slope


def mm(a, b):
    return jnp.dot(a, b, preferred_element_type=F32)


def mm_nt(a, b):
    return lax.dot_general(a, b, (((1,), (1,)), ((), ())), preferred_element_type=F32)


def mm_tn(a, b):
    return lax.dot_general(a, b, (((0,), (0,)), ((), ())), preferred_element_type=F32)


def run_copies(pairs, sems):
    found = [pltpu.make_async_copy(src, dst, sems.at[i]) for i, (src, dst) in enumerate(pairs)]
    for c in found:
        c.start()
    return found


def wait_for(copies):
    for c in copies:
        c.wait()


def stage_shape(dps, depth, width):
    return (dps, depth, width) if depth % 16 else (1, 16, 128)


def place_rows(where, refs, store, stage, sems, outward=False):
    depth = refs[0].shape[0]
    if outward and len(refs) == 5:
        pairs = []
        for k, ref in zip((0, 1, 2, 3, 3), refs):
            first = (where[0] ^ k) * depth
            if ref is refs[4]:
                first = first + refs[3].shape[0]
            pairs.append((store.at[pl.ds(pl.multiple_of(first, 16), ref.shape[0]), :], ref))
        return run_copies(pairs, sems)
    if depth % 16:
        spots = [stage.at[where[0] ^ k] for k in range(len(refs))]
    else:
        spots = [
            store.at[pl.ds(pl.multiple_of((where[0] ^ k) * depth, 16), depth), :]
            for k in range(len(refs))
        ]
    if outward:
        if depth % 16:
            for p in range(len(refs)):
                stage[p] = store[p * depth : (p + 1) * depth, :]
        return run_copies(list(zip(spots, refs)), sems)
    return run_copies(list(zip(refs, spots)), sems)


def settle_rows(copies, store, stage):
    wait_for(copies)
    depth = stage.shape[1]
    if depth % 16:
        for p in range(stage.shape[0]):
            store[p * depth : (p + 1) * depth, :] = stage[p]


def hot(row, count):
    return (
        lax.broadcasted_iota(jnp.int32, (count, row.shape[1]), 0) == row
    ).astype(BF)


def pack_kernel(where, w_ref, send_ref, more_ref, out_ref):
    depth = w_ref.shape[0]
    for n in range(out_ref.shape[0]):
        out_ref[n, 0:depth] = mm(w_ref[...], hot(send_ref[where[1], n], w_ref.shape[1])).astype(BF)
        out_ref[n, depth:] = more_ref[...]


def pack_columns(where, w_qkv, send, more):
    seqs, _, _, wide = send.shape
    shape = like((seqs, w_qkv.shape[0] + more.shape[0], wide))
    return pl.pallas_call(
        pack_kernel,
        in_specs=[SCALAR, WHOLE, WHOLE, WHOLE],
        out_specs=blocks_of(shape)[0],
        out_shape=shape,
        compiler_params=ROOM,
    )(where, w_qkv, send, more)


def unpack_kernel(where, recv_ref, in_ref, out_ref):
    total = None
    for n in range(in_ref.shape[0]):
        part = mm_nt(in_ref[n, 0 : out_ref.shape[0]], hot(recv_ref[n, where[1]], out_ref.shape[1]))
        total = part if total is None else total + part
    out_ref[...] = total.astype(BF)


def unpack_columns(where, parts, recv, depth, width):
    return pl.pallas_call(
        unpack_kernel,
        in_specs=[SCALAR, WHOLE, WHOLE],
        out_specs=blocks_of(like((depth, width)))[0],
        out_shape=like((depth, width)),
        compiler_params=ROOM,
    )(where, recv, parts)


def repack_kernel(where, recv_ref, more_ref, *rest):
    parts, out_ref = rest[:-1], rest[-1]
    grad = total_of([p[...] for p in parts]).astype(BF)
    depth = grad.shape[0]
    for n in range(out_ref.shape[0]):
        out_ref[n, 0:depth] = mm(grad, hot(recv_ref[n, where[1]], grad.shape[1])).astype(BF)
        out_ref[n, depth:] = more_ref[n]


def repack_columns(where, parts, recv, more):
    seqs, _, _, wide = recv.shape
    shape = like((seqs, parts[0].shape[0] + more.shape[1], wide))
    return pl.pallas_call(
        repack_kernel,
        in_specs=[SCALAR] + [WHOLE] * (2 + len(parts)),
        out_specs=blocks_of(shape)[0],
        out_shape=shape,
        compiler_params=ROOM,
    )(where, recv, more, *parts)


def restore_kernel(where, send_ref, in_ref, out_ref):
    depth = out_ref.shape[0]
    total = None
    for n in range(in_ref.shape[0]):
        part = mm_nt(in_ref[n, 0:depth], hot(send_ref[where[1], n], out_ref.shape[1]))
        total = part if total is None else total + part
    out_ref[...] = total


def restore_columns(where, parts, send, depth, width):
    return pl.pallas_call(
        restore_kernel,
        in_specs=[SCALAR, WHOLE, WHOLE],
        out_specs=blocks_of(like((depth, width)))[0],
        out_shape=like((depth, width), F32),
        compiler_params=ROOM,
    )(where, send, parts)


def piece_rows(total, count):
    tiles = total // 16
    return 16 * -(-tiles // count), lambda q: 16 * ((q * tiles) // count)


def pieces_kernel(where, w_ref, *outs):
    size, start = piece_rows(w_ref.shape[1], len(outs))
    for k, ref in enumerate(outs):
        first = pl.multiple_of(start(where[0] ^ k), 16)
        ref[...] = w_ref[:, pl.ds(first, size), :]


def proj_pieces(where, w_proj, dps):
    ratio, ff_mine, col = w_proj.shape
    size, _ = piece_rows(ff_mine, dps)
    return pl.pallas_call(
        pieces_kernel,
        in_specs=[SCALAR, WHOLE],
        out_specs=blocks_of(*[like((ratio, size, col))] * dps),
        out_shape=[like((ratio, size, col))] * dps,
        compiler_params=ROOM,
    )(where, w_proj)


def turn_kernel(where, *rest):
    ins, (out_ref, sems) = rest[:-2], rest[-2:]
    ratio = ins[0].shape[0]
    spots = [out_ref.at[pl.ds((where[0] ^ k) * ratio, ratio)] for k in range(len(ins))]
    wait_for(run_copies(list(zip(ins, spots)), sems))


def turn_pieces(where, parts):
    ratio, size, col = parts[0].shape
    return pl.pallas_call(
        turn_kernel,
        in_specs=[SCALAR] + [WHOLE] * len(parts),
        out_specs=blocks_of(like((ratio * len(parts), size, col)))[0],
        out_shape=like((ratio * len(parts), size, col)),
        scratch_shapes=[pltpu.SemaphoreType.DMA((len(parts),))],
        compiler_params=ROOM,
    )(where, *parts)


def join_kernel(in_ref, out_ref):
    width = in_ref.shape[2]
    for n in range(in_ref.shape[0]):
        out_ref[:, n * width : (n + 1) * width] = in_ref[n]


def join_columns(parts):
    seqs, size, col = parts.shape
    return pl.pallas_call(
        join_kernel,
        in_specs=[WHOLE],
        out_specs=blocks_of(like((size, col * seqs)))[0],
        out_shape=like((size, col * seqs)),
        compiler_params=ROOM,
    )(parts)


def split_kernel(*refs):
    out_ref = refs[-1]
    total = total_of([r[...] for r in refs[:-1]]).astype(BF)
    width = out_ref.shape[2]
    for n in range(out_ref.shape[0]):
        out_ref[n] = total[:, n * width : (n + 1) * width]


def split_columns(parts, seqs):
    size, model = parts[0].shape
    return pl.pallas_call(
        split_kernel,
        in_specs=[WHOLE] * len(parts),
        out_specs=blocks_of(like((seqs, size, model // seqs)))[0],
        out_shape=like((seqs, size, model // seqs)),
        compiler_params=ROOM,
    )(*parts)


def rows_kernel(where, *rest):
    ins, (out_ref, store, sems) = rest[:-3], rest[-3:]
    dps, ratio, size, _ = store.shape
    ff_mine = out_ref.shape[1] // ratio
    _, start = piece_rows(ff_mine, dps)
    wait_for(run_copies([(ref, store.at[where[0] ^ k]) for k, ref in enumerate(ins)], sems))
    for q in range(dps):
        for b in range(ratio):
            first = b * ff_mine + start(q)
            out_ref[:, first : first + size] = store[q, b].astype(F32).T


def proj_rows(where, parts, ff_mine):
    ratio, size, col = parts[0].shape
    return pl.pallas_call(
        rows_kernel,
        in_specs=[SCALAR] + [ANY] * len(parts),
        out_specs=blocks_of(like((col, ratio * ff_mine)))[0],
        out_shape=like((col, ratio * ff_mine), F32),
        scratch_shapes=[
            pltpu.VMEM((len(parts), ratio, size, col), BF),
            pltpu.SemaphoreType.DMA((len(parts),)),
        ],
        compiler_params=ROOM,
    )(where, *parts)


def head_masks(rows):
    first = lax.broadcasted_iota(jnp.int32, (rows, PAIR), 1) < HD
    causal = lax.broadcasted_iota(jnp.int32, (rows, rows), 0) >= lax.broadcasted_iota(
        jnp.int32, (rows, rows), 1
    )
    return first, causal


def masked_scores(q, keys, causal):
    rows, seen = q.shape[0], keys.shape[0]
    s = mm_nt(q, keys)
    tail = jnp.where(causal, s[:, seen - rows :], NEG_FILL)
    return tail if seen == rows else jnp.concatenate([s[:, : seen - rows], tail], axis=1)


def attend_rows(q, keys, values, first, causal):
    q = q * BF(1.0 / math.sqrt(HD))
    outs, logs = [], []
    for mine in (first, ~first):
        s = masked_scores(jnp.where(mine, q, BF(0)), keys, causal)
        top = jnp.max(s, axis=-1, keepdims=True)
        e = jnp.exp(s - top)
        total = jnp.sum(e, axis=-1, keepdims=True)
        outs.append(mm(e.astype(BF), values) / total)
        logs.append(top + jnp.log(total))
    return jnp.where(first, outs[0], outs[1]).astype(BF), jnp.where(first, logs[0], logs[1])


def attend_kernel(pairs, dps, where, x_ref, vec_ref, bias_ref, *rest):
    w_refs = rest[:dps]
    n1_ref, qkv_ref, att_ref, lse_ref, w, stage, qkv, sems = rest[dps:]
    i = pl.program_id(0)
    rows = x_ref.shape[0]
    part = rows // 2

    @pl.when(i == 0)
    def _():
        settle_rows(place_rows(where, w_refs, w, stage, sems), w, stage)

    unit, _ = normalise(x_ref[...].astype(F32))
    n1 = (unit * vec_ref[0:1, :] + vec_ref[1:2, :]).astype(BF)
    n1_ref[...] = n1
    tile = (mm(n1, w[...]) + bias_ref[...]).astype(BF)
    qkv_ref[...] = tile
    qkv[pl.ds(pl.multiple_of(i * rows, rows), rows), :] = tile
    first, causal = head_masks(rows)
    for j in range(qkv.shape[0] // rows):

        @pl.when(i == j)
        def _(j=j):
            seen = (j + 1) * rows
            for g in range(pairs):
                lanes = slice(g * PAIR, (g + 1) * PAIR)
                keys = qkv[0:seen, (pairs + g) * PAIR : (pairs + g + 1) * PAIR]
                values = qkv[0:seen, (2 * pairs + g) * PAIR : (2 * pairs + g + 1) * PAIR]
                out, log = attend_rows(qkv[j * rows : seen, lanes], keys, values, first, causal)
                for b in range(2):
                    att_ref[b, :, lanes] = out[b * part : (b + 1) * part]
                lse_ref[:, lanes] = log


def attend(where, x_all, table, bias, weights, part):
    length, model = x_all.shape
    depth, width = weights[0].shape
    dps = len(weights)
    heads = width // 3
    rows = 2 * part
    whole = lambda a: pl.BlockSpec(a.shape, lambda i: (0,) * a.ndim)
    tile = lambda cols: pl.BlockSpec((rows, cols), lambda i: (i, 0))
    return pl.pallas_call(
        functools.partial(attend_kernel, heads // PAIR, dps),
        grid=(length // rows,),
        in_specs=[SCALAR, tile(model), whole(table), whole(bias)] + [ANY] * dps,
        out_specs=[
            tile(model),
            tile(width),
            pl.BlockSpec((2, part, heads), lambda i: (i, 0, 0)),
            tile(heads),
            pl.BlockSpec((model, width), lambda i: (0, 0)),
        ],
        out_shape=[
            like((length, model)),
            like((length, width)),
            like((length // part, part, heads)),
            like((length, heads), F32),
            like((model, width)),
        ],
        scratch_shapes=[
            pltpu.VMEM(stage_shape(dps, depth, width), BF),
            pltpu.VMEM((length, width), BF),
            pltpu.SemaphoreType.DMA((dps,)),
        ],
        compiler_params=ROOM,
    )(where, x_all, table, bias, *weights)


def attend_back_kernel(pairs, qkv_ref, ga_ref, lse_ref, gqkv_ref, sums_ref, ak, av):
    length = qkv_ref.shape[0]
    part = ga_ref.shape[1]
    rows = 2 * part
    first, causal = head_masks(rows)
    for g in range(pairs):
        lanes = slice(g * PAIR, (g + 1) * PAIR)
        k_lanes = slice((pairs + g) * PAIR, (pairs + g + 1) * PAIR)
        v_lanes = slice((2 * pairs + g) * PAIR, (2 * pairs + g + 1) * PAIR)
        ak[...] = jnp.zeros_like(ak)
        av[...] = jnp.zeros_like(av)
        for i in range(length // rows):
            here = slice(i * rows, (i + 1) * rows)
            seen = (i + 1) * rows
            q = qkv_ref[here, lanes] * BF(1.0 / math.sqrt(HD))
            ga = jnp.concatenate([ga_ref[b, :, lanes] for b in (2 * i, 2 * i + 1)], axis=0)
            keys = qkv_ref[0:seen, k_lanes]
            values = qkv_ref[0:seen, v_lanes]
            grads = []
            for h, mine in enumerate((first, ~first)):
                q_h = jnp.where(mine, q, BF(0))
                ga_h = jnp.where(mine, ga, BF(0))
                s = masked_scores(q_h, keys, causal)
                lane = g * PAIR + h * HD
                p = jnp.exp(s - lse_ref[here, lane : lane + 1])
                gp = mm_nt(ga_h, values)
                centre = jnp.sum(p * gp, axis=-1, keepdims=True)
                gs = (p * (gp - centre)).astype(BF)
                av[0:seen, :] += mm_tn(p.astype(BF), ga_h)
                ak[0:seen, :] += mm_tn(gs, q_h)
                grads.append(mm(gs, keys))
            gqkv_ref[here, lanes] = (
                jnp.where(first, grads[0], grads[1]) * (1.0 / math.sqrt(HD))
            ).astype(BF)
        gqkv_ref[:, k_lanes] = ak[...].astype(BF)
        gqkv_ref[:, v_lanes] = av[...].astype(BF)
    sums_ref[...] = jnp.sum(gqkv_ref[...].astype(F32), axis=0, keepdims=True)


def attend_back(qkv, grad, lse):
    length, width = qkv.shape
    return pl.pallas_call(
        functools.partial(attend_back_kernel, grad.shape[2] // PAIR),
        in_specs=[WHOLE] * 3,
        out_specs=[WHOLE, WHOLE],
        out_shape=[like((length, width)), like((1, width), F32)],
        scratch_shapes=[pltpu.VMEM((length, PAIR), F32), pltpu.VMEM((length, PAIR), F32)],
        compiler_params=ROOM,
    )(qkv, grad, lse)


def grad_blocks_kernel(where, a_ref, g_ref, *rest):
    outs, (store, stage, sems) = rest[:-3], rest[-3:]
    g = g_ref[...]
    model = a_ref.shape[1]
    for a in range(0, model, 256):
        b = min(model, a + 256)
        store[a:b, :] = mm_tn(a_ref[:, a:b], g).astype(BF)
    wait_for(place_rows(where, outs, store, stage, sems, True))


def chunk_shapes(count, rows, cols):
    shapes = [like((rows, cols))] * count
    if can_halve(count, rows):
        shapes[3:] = [like((cut(rows), cols)), like((rows - cut(rows), cols))]
    return shapes


def grad_blocks(where, a, g, dps):
    model, width = a.shape[1], g.shape[1]
    depth = model // dps
    shapes = chunk_shapes(dps, depth, width)
    return pl.pallas_call(
        grad_blocks_kernel,
        in_specs=[SCALAR, WHOLE, WHOLE],
        out_specs=[ANY] * len(shapes),
        out_shape=shapes,
        scratch_shapes=[
            pltpu.VMEM((model, width), BF),
            pltpu.VMEM(stage_shape(dps, depth, width), BF),
            pltpu.SemaphoreType.DMA((len(shapes),)),
        ],
        compiler_params=ROOM,
    )(where, a, g)


def grad_rows_kernel(g_ref, n1_ref, w_ref, out_ref, sums_ref):
    @pl.when(pl.program_id(0) == 0)
    def _():
        sums_ref[...] = jnp.zeros_like(sums_ref)

    grad = mm_nt(g_ref[...], w_ref[...])
    sums_ref[0:1, :] += jnp.sum(grad * n1_ref[...].astype(F32), axis=0, keepdims=True)
    sums_ref[1:2, :] += jnp.sum(grad, axis=0, keepdims=True)
    out_ref[...] = grad.astype(BF)


def grad_rows(gqkv, weights, n1, rows):
    length, model = n1.shape
    width = weights.shape[1]
    tile = lambda cols: pl.BlockSpec((rows, cols), lambda i: (i, 0))
    return pl.pallas_call(
        grad_rows_kernel,
        grid=(length // rows,),
        in_specs=[tile(width), tile(model), WHOLE],
        out_specs=[tile(model), pl.BlockSpec((2, model), lambda i: (0, 0))],
        out_shape=[like((length, model)), like((2, model), F32)],
        compiler_params=ROOM,
    )(gqkv, n1, weights)


def place_pieces(where, refs, store, sems):
    size, start = piece_rows(store.shape[0], len(refs))
    starts = [start(q) for q in range(len(refs))] + [store.shape[0]]
    least = min(b - a for a, b in zip(starts, starts[1:]))
    count = len(refs)
    copies, more = [], []
    for k, ref in enumerate(refs):
        first = start(where[0] ^ k)
        spot = pl.ds(pl.multiple_of(first, 16), least)
        copies.append(
            pltpu.make_async_copy(ref.at[pl.ds(0, least), :], store.at[spot, :], sems.at[k])
        )
        if size > least:
            spot = pl.ds(pl.multiple_of(first + least, 16), size - least)
            rest = ref.at[pl.ds(least, size - least), :]
            more.append(
                (
                    start((where[0] ^ k) + 1) - first > least,
                    pltpu.make_async_copy(rest, store.at[spot, :], sems.at[count + k]),
                )
            )
    for c in copies:
        c.start()
    for needed, c in more:
        pl.when(needed)(c.start)
    wait_for(copies)
    for needed, c in more:
        pl.when(needed)(c.wait)


def gather_fc_kernel(where, *rest):
    f_refs, (wf, stage, sems) = rest[:-3], rest[-3:]
    settle_rows(place_rows(where, f_refs, wf, stage, sems), wf, stage)


def gather_fc(where, fc):
    dps = len(fc)
    depth, width = fc[0].shape
    return pl.pallas_call(
        gather_fc_kernel,
        in_specs=[SCALAR] + [ANY] * dps,
        out_specs=WHOLE,
        out_shape=like((depth * dps, width)),
        scratch_shapes=[
            pltpu.VMEM(stage_shape(dps, depth, width), BF),
            pltpu.SemaphoreType.DMA((dps,)),
        ],
        compiler_params=ROOM,
    )(where, *fc)


def gather_proj_kernel(where, *rest):
    p_refs, (wp, sems) = rest[:-2], rest[-2:]
    place_pieces(where, p_refs, wp, sems)


def gather_proj(where, proj, ff_mine):
    dps = len(proj)
    return pl.pallas_call(
        gather_proj_kernel,
        in_specs=[SCALAR] + [ANY] * dps,
        out_specs=WHOLE,
        out_shape=like((ff_mine, proj[0].shape[1])),
        scratch_shapes=[pltpu.SemaphoreType.DMA((2 * dps,))],
        compiler_params=ROOM,
    )(where, *proj)


def feed_kernel(n2_ref, gm_ref, bias_ref, wf, wp, e_ref, gu_ref, gn2_ref, sum_ref):
    @pl.when(pl.program_id(0) == 0)
    def _():
        sum_ref[...] = jnp.zeros_like(sum_ref)

    u = mm(n2_ref[...], wf[...]) + bias_ref[...]
    ge = mm_nt(gm_ref[...], wp[...])
    value, slope = gelu_parts(u)
    e_ref[...] = value.astype(BF)
    gu = (ge * slope).astype(BF)
    gu_ref[...] = gu
    sum_ref[...] += jnp.sum(gu.astype(F32), axis=0, keepdims=True)
    gn2_ref[...] = mm_nt(gu, wf[...]).astype(BF)


def feed(n2, gm, bias, fc, proj, rows):
    length, model = n2.shape
    width = fc.shape[1]
    whole = lambda shape: pl.BlockSpec(shape, lambda i: (0,) * len(shape))
    tile = lambda cols: pl.BlockSpec((rows, cols), lambda i: (i, 0))
    return pl.pallas_call(
        feed_kernel,
        grid=(length // rows,),
        in_specs=[tile(model), tile(model), whole(bias.shape), WHOLE, WHOLE],
        out_specs=[tile(width), tile(width), tile(model), whole((1, width))],
        out_shape=[
            like((length, width)),
            like((length, width)),
            like((length, model)),
            like((1, width), F32),
        ],
        compiler_params=ROOM,
    )(n2, gm, bias, fc, proj)


def grad_proj_kernel(dps, where, gm_ref, e_ref, *rest):
    outs, (store, sems) = rest[:-2], rest[-2:]
    width = store.shape[0]
    for a in range(0, width, 256):
        b = min(width, a + 256)
        store[a:b, :] = mm_tn(e_ref[:, a:b], gm_ref[...]).astype(BF)
    _, start = piece_rows(width, dps)
    pairs = []
    for i, ref in enumerate(outs):
        first = start(where[0] ^ min(i, dps - 1))
        if i == dps:
            first = first + outs[i - 1].shape[0]
        pairs.append((store.at[pl.ds(pl.multiple_of(first, 16), ref.shape[0]), :], ref))
    wait_for(run_copies(pairs, sems))


def grad_proj(where, gm, e, dps):
    model, width = gm.shape[1], e.shape[1]
    size, _ = piece_rows(width, dps)
    shapes = chunk_shapes(dps, size, model)
    return pl.pallas_call(
        functools.partial(grad_proj_kernel, dps),
        in_specs=[SCALAR, WHOLE, WHOLE],
        out_specs=[ANY] * len(shapes),
        out_shape=shapes,
        scratch_shapes=[
            pltpu.VMEM((width, model), BF),
            pltpu.SemaphoreType.DMA((len(shapes),)),
        ],
        compiler_params=ROOM,
    )(where, gm, e)


def feed_out_kernel(e_ref, wp, out_ref):
    out_ref[...] = mm(e_ref[...], wp[...]).astype(BF)


def feed_out(e, proj, rows):
    length, width = e.shape
    model = proj.shape[1]
    return pl.pallas_call(
        feed_out_kernel,
        grid=(length // rows,),
        in_specs=[pl.BlockSpec((rows, width), lambda i: (i, 0)), WHOLE],
        out_specs=pl.BlockSpec((rows, model), lambda i: (i, 0)),
        out_shape=like((length, model)),
        compiler_params=ROOM,
    )(e, proj)


def last_kernel(gn1_ref, gr_ref, vec_ref, x_hbm, out_ref, x_ref, sem):
    copy = pltpu.make_async_copy(x_hbm, x_ref, sem)
    copy.start()
    copy.wait()
    unit, inverse = normalise(x_ref[...].astype(F32))
    grad = norm_back(gn1_ref[...].astype(F32), unit, inverse, vec_ref[0:1, :])
    out_ref[...] = (gr_ref[...] + grad).T.astype(BF)


def last_norm(gn1, x, gr, table):
    shape = like(x.shape[::-1])
    return pl.pallas_call(
        last_kernel,
        in_specs=[WHOLE] * 3 + [ANY],
        out_specs=blocks_of(shape)[0],
        out_shape=shape,
        scratch_shapes=[pltpu.VMEM(x.shape, BF), pltpu.SemaphoreType.DMA],
        compiler_params=ROOM,
    )(gn1, gr, table, x)


def output_kernel(r_ref, mlp_ref, vec_ref, out_ref):
    out = r_ref[...] + (mlp_ref[...].astype(F32) + vec_ref[7:8, :])
    out_ref[...] = out.T.astype(BF)


def output_rows(r, mlp, table):
    shape = like(r.shape[::-1])
    return pl.pallas_call(
        output_kernel,
        in_specs=[WHOLE] * 3,
        out_specs=blocks_of(shape)[0],
        out_shape=shape,
        compiler_params=ROOM,
    )(r, mlp, table)


def line_blocks(block):
    seqs = lax.axis_size("seq")
    return jnp.stack(
        [block]
        + [lax.ppermute(block, "seq", xor_perm(seqs, 2 * dz)) for dz in range(1, seqs // 2)]
    )


def block_pairs(where, places, flat, store):
    return [
        (
            ref.at[j],
            store.at[where[0] ^ places[i // 2][0], where[1] ^ (2 * (places[i // 2][1] + j) + i % 2)],
        )
        for i, ref in enumerate(flat)
        for j in range(ref.shape[0])
    ]


def head_columns(att_ref, owner):
    count = int(owner.max()) + 1
    parts = []
    for h in range(count):
        dev, slot = [int(i[0]) for i in np.where(owner == h)]
        parts.append(att_ref[dev, :, slot * HD : (slot + 1) * HD])
    return jnp.concatenate(parts, axis=1)


def block_scratch(dps, flat):
    line, depth, width = flat[0].shape
    return [
        pltpu.VMEM((dps, 2 * line, depth, width), BF),
        pltpu.SemaphoreType.DMA((dps * 2 * line + 1,)),
    ]


def out_kernel(owner, places, where, att_ref, vec_ref, x_hbm, *rest):
    flat, (r_ref, n2_ref, store, sems, x_ref) = rest[:-5], rest[-5:]
    copies = run_copies(block_pairs(where, places, flat, store) + [(x_hbm, x_ref)], sems)
    att = head_columns(att_ref, owner)
    dps, seqs, depth, width = store.shape
    wait_for(copies)
    for n in range(seqs):
        here = slice(n * width, (n + 1) * width)
        total = x_ref[:, here].astype(F32) + vec_ref[4:5, here]
        for p in range(dps):
            total = total + mm(att[:, p * depth : (p + 1) * depth], store[p, n])
        r_ref[:, here] = total
    unit, _ = normalise(r_ref[...])
    n2_ref[...] = (unit * vec_ref[5:6, :] + vec_ref[6:7, :]).astype(BF)


def out_project(where, att, x, table, places, flat, owner):
    dps = max(k for k, _ in places) + 1
    return pl.pallas_call(
        functools.partial(out_kernel, owner, places),
        in_specs=[SCALAR, WHOLE, WHOLE, ANY] + [ANY] * len(flat),
        out_specs=blocks_of(x, x),
        out_shape=[like(x.shape, F32), like(x.shape)],
        scratch_shapes=block_scratch(dps, flat) + [pltpu.VMEM(x.shape, BF)],
        compiler_params=ROOM,
    )(where, att, table, x, *flat)


def back_kernel(owner, places, where, gn2_ref, r_ref, vec_ref, g_hbm, *rest):
    flat = rest[:-7]
    gr_ref, go_ref, ga_ref, sums_ref, store, sems, g_ref = rest[-7:]
    copies = run_copies([(g_hbm, g_ref)] + block_pairs(where, places, flat, store), sems)
    copies[0].wait()
    dps, seqs, depth, width = store.shape
    gn2 = gn2_ref[...].astype(F32)
    unit, inverse = normalise(r_ref[...])
    gr = g_ref[...].astype(F32) + norm_back(gn2, unit, inverse, vec_ref[5:6, :])
    go = gr.astype(BF)
    gr_ref[...] = gr
    go_ref[...] = go
    sums_ref[0:1, :] = jnp.sum(go.astype(F32), axis=0, keepdims=True)
    sums_ref[1:2, :] = jnp.sum(gn2 * unit, axis=0, keepdims=True)
    sums_ref[2:3, :] = jnp.sum(gn2, axis=0, keepdims=True)
    sums_ref[3:4, :] = jnp.sum(g_ref[...].astype(F32), axis=0, keepdims=True)
    wait_for(copies[1:])
    found = []
    for p in range(dps):
        total = mm_nt(go[:, 0:width], store[p, 0])
        for n in range(1, seqs):
            total = total + mm_nt(go[:, n * width : (n + 1) * width], store[p, n])
        found.append(total)
    ga = jnp.concatenate(found, axis=1).astype(BF)
    ga_ref[...] = jnp.zeros_like(ga_ref)
    for h in range(int(owner.max()) + 1):
        dev, slot = [int(i[0]) for i in np.where(owner == h)]
        ga_ref[dev, :, slot * HD : (slot + 1) * HD] = ga[:, h * HD : (h + 1) * HD]


def out_back(where, gn2, r, g, table, places, flat, owner):
    dps = max(k for k, _ in places) + 1
    shapes = [
        like(r.shape, F32),
        like(r.shape),
        like((owner.shape[0], r.shape[0], owner.shape[1] * HD)),
        like((4, r.shape[1]), F32),
    ]
    return pl.pallas_call(
        functools.partial(back_kernel, owner, places),
        in_specs=[SCALAR, WHOLE, WHOLE, WHOLE, ANY] + [ANY] * len(flat),
        out_specs=blocks_of(*shapes),
        out_shape=shapes,
        scratch_shapes=block_scratch(dps, flat) + [pltpu.VMEM(g.shape, BF)],
        compiler_params=ROOM,
    )(where, gn2, r, table, g, *flat)


def grad_out_kernel(owner, where, att_ref, far_att_ref, go_ref, far_go_ref, *rest):
    outs, (store, sems) = rest[:-2], rest[-2:]
    att = jnp.concatenate([head_columns(r, owner) for r in (att_ref, far_att_ref)], axis=0)
    go = jnp.concatenate([go_ref[...], far_go_ref[...]], axis=0)
    dps, line, depth, width = store.shape
    even = where[1] % 2 == 0
    for z in range(line):
        a, b = 2 * z * width, (2 * z + 1) * width
        cols = jnp.where(even, go[:, a : a + width], go[:, b : b + width])
        for p in range(dps):
            store[p, z] = mm_tn(att[:, p * depth : (p + 1) * depth], cols).astype(BF)
    pairs = [
        (store.at[where[0] ^ k, (where[1] // 2) ^ dz], ref.at[dz])
        for k, ref in enumerate(outs)
        for dz in range(line)
    ]
    wait_for(run_copies(pairs, sems))


def grad_out(where, att, far_att, go, far_go, dps, owner):
    seqs = att.shape[0]
    line, depth, width = seqs // 2, go.shape[1] // dps, go.shape[1] // seqs
    return pl.pallas_call(
        functools.partial(grad_out_kernel, owner),
        in_specs=[SCALAR] + [WHOLE] * 4,
        out_specs=[ANY] * dps,
        out_shape=[like((line, depth, width))] * dps,
        scratch_shapes=[
            pltpu.VMEM((dps, line, depth, width), BF),
            pltpu.SemaphoreType.DMA((dps * line,)),
        ],
        compiler_params=ROOM,
    )(where, att, far_att, go, far_go)


def body(tokens, w_qkv, w_out, vectors, w_fc, b_fc, w_proj, cotangent):
    dps = lax.axis_size("dp")
    seqs = lax.axis_size("seq")
    dp = lax.axis_index("dp")
    sq = lax.axis_index("seq")
    rows, model = tokens.shape
    head_count = model // HD
    slots, owner, wide, send, recv = head_plan(head_count, seqs, w_qkv.shape[1])
    send = jnp.asarray(send)[:, :, None, :]
    recv = jnp.asarray(recv)[:, :, None, :]
    mine = slots * HD
    ff_mine = w_fc.shape[1]
    ratio = seqs // dps
    col = w_proj.shape[1]
    where = jnp.stack([dp, sq]).astype(jnp.int32)
    per, wide_vec = vectors.shape
    own_heads = jnp.asarray(owner)[sq]
    pick = (own_heads[:, None] == jnp.arange(head_count)[None, :]).astype(F32)

    def head_rows(vector):
        return jnp.sum(pick[:, :, None] * vector.reshape(1, head_count, HD), axis=1).reshape(-1)

    def head_spread(vector):
        return jnp.sum(pick[:, :, None] * vector.reshape(slots, 1, HD), axis=0).reshape(-1)

    near, far = near_far(dps)
    copies = lambda block: {k: block for k in range(dps)}
    chunks = lambda blocks: dict(enumerate(blocks))

    lanes = send.shape[3]
    gm_all = lax.all_gather(cotangent, "seq", axis=0, tiled=True)
    small = jnp.concatenate([vectors.reshape(-1), b_fc])
    count = small.shape[0]
    small = jnp.stack(in_order(small, send_rel(copies(small), "dp", near + far)))
    small = as_rows(small.reshape(1, -1), lanes)[0]
    parts = exchange(pack_columns(where, w_qkv, send, small))
    wf_near = send_rel(copies(w_fc), "dp", near)
    pieces = proj_pieces(where, w_proj.reshape(ratio, ff_mine, col), dps)
    pieces = in_order(pieces[0], send_rel(chunks(pieces), "dp", near + far))
    parts, wf_near, x_own, out_own, pieces, fc_own, gm_all = phase(
        parts, wf_near, tokens, w_out, pieces, w_fc, gm_all
    )

    x_all = lax.all_gather(x_own, "seq", axis=0, tiled=True)
    own_qkv = unpack_columns(where, parts, recv, w_qkv.shape[0], 3 * mine)
    wq = in_order(own_qkv, send_rel(copies(own_qkv), "dp", near + far))
    wf_far = send_rel(copies(fc_own), "dp", far)
    line = line_blocks(out_own)
    pieces = turn_pieces(where, pieces)
    small = parts[:, w_qkv.shape[0] :].reshape(seqs, -1)[:, : dps * count].astype(F32)
    small = jnp.take(small.reshape(seqs, dps, count), dp ^ jnp.arange(dps), axis=1)
    table = small[:, :, : per * wide_vec].reshape(seqs, dps, per, wide_vec)
    table = table.transpose(1, 2, 0, 3).reshape(dps * per, model)
    bias_fc = small[:, :, per * wide_vec :].transpose(1, 0, 2).reshape(-1)
    bias_fc = lax.dynamic_slice_in_dim(bias_fc, sq * ff_mine, ff_mine)[None]
    bias_qkv = jnp.concatenate(
        [head_rows(table[2]), jnp.zeros((mine,), F32), head_rows(table[3])]
    )[None]
    x_all, wq, wf_far, line, pieces, table, bias_qkv = phase(
        x_all, wq, wf_far, line, pieces, table, bias_qkv
    )

    pieces = exchange(pieces)
    wo = {(0, 0): line}
    wo.update({(k, 0): b for k, b in send_rel(copies(line), "dp", near).items()})
    n1_all, qkv, att, lse, wq = attend(where, x_all, table, bias_qkv, wq, rows)
    att, wo, pieces = phase(att, wo, pieces)

    att = exchange(att)
    wo_other = {place: swap_core(b) for place, b in wo.items()}
    found = gather_far(wo, far)
    wo.update(found)
    own_proj = join_columns(pieces)
    att, wo, wo_other, own_proj = phase(att, wo, wo_other, own_proj)
    wo_other.update({place: swap_core(wo[place]) for place in found})
    wp_near = send_rel(copies(own_proj), "dp", near)
    places = sorted(wo)
    flat = [b for place in places for b in (wo[place], wo_other[place])]
    r, n2 = out_project(where, att, x_own, table, places, flat, owner)
    n2, att, own_proj = phase(n2, att, own_proj)

    n2_all = lax.all_gather(n2, "seq", axis=0, tiled=True)
    wp = in_order(own_proj, wp_near, send_rel(copies(own_proj), "dp", far))
    far_att = swap_core(att)
    wf = in_order(fc_own, wf_near, wf_far)
    wf = gather_fc(where, wf)
    wf, wp = phase(wf, wp)
    wp = gather_proj(where, wp, ff_mine)
    n2_all, wp, far_att = phase(n2_all, wp, far_att)
    e, gu, gn2_part, sum_fc = feed(n2_all, gm_all, bias_fc, wf, wp, 2 * rows)

    gn2 = lax.psum_scatter(gn2_part, "seq", scatter_dimension=0, tiled=True)
    d_proj = grad_proj(where, gm_all, e, dps)
    proj_first = reduce_first(d_proj)
    d_fc = grad_blocks(where, n2_all, gu, dps)
    d_fc, proj_first, e_late = phase(d_fc, proj_first, e)
    proj_in = reduce_second(d_proj, proj_first)
    mlp = feed_out(e_late, wp, 2 * rows)
    gn2, d_fc, mlp, proj_in = phase(gn2, d_fc, mlp, proj_in)

    mlp = lax.psum_scatter(mlp, "seq", scatter_dimension=0, tiled=True)
    gr, go, ga, sums_two = out_back(where, gn2, r, cotangent, table, places, flat, owner)
    fc_first = reduce_first(d_fc)
    ga, go, fc_first = phase(ga, go, fc_first)

    ga = exchange(ga)
    d_out = split_far(grad_out(where, att, far_att, go, swap_core(go), dps, owner))
    g_proj = split_columns(proj_in, seqs)
    fc_in = reduce_second(d_fc, fc_first)
    ga, d_out, fc_in, g_proj = phase(ga, d_out, fc_in, g_proj)

    out_first = reduce_first(d_out)
    g_proj = exchange(g_proj)
    gqkv, gqkv_sums = attend_back(qkv, ga, lse)
    gqkv, out_first = phase(gqkv, out_first)
    gn1_part, norm_sums = grad_rows(gqkv, wq, n1_all, 2 * rows)
    gn1_part, gqkv, mlp, g_proj, d_out = phase(gn1_part, gqkv, mlp, g_proj, d_out)

    gn1 = lax.psum_scatter(gn1_part, "seq", scatter_dimension=0, tiled=True)
    out_in = reduce_second(d_out, out_first)
    d_qkv = grad_blocks(where, n1_all, gqkv, dps)
    d_qkv, out_in = phase(d_qkv, out_in)
    qkv_first = reduce_first(d_qkv)
    g_line = total_of(out_in).astype(BF)
    out_in = [g_line[0]] + [
        lax.ppermute(g_line[dz], "seq", xor_perm(seqs, 2 * dz)) for dz in range(1, seqs // 2)
    ]
    qkv_in = reduce_second(d_qkv, qkv_first)
    activations = output_rows(r, mlp, table)
    g_fc = total_of(fc_in)
    g_proj = {
        k: lax.dynamic_slice_in_dim(g_proj, (dp ^ k) * ratio, ratio, axis=0) for k in range(dps)
    }
    g_proj = in_order(g_proj[0], send_rel(g_proj, "dp", near + far))
    g_proj = proj_rows(where, g_proj, ff_mine)
    vector_grads = jnp.concatenate(
        [
            ((norm_sums[0] - table[1] * norm_sums[1]) / table[0])[None],
            norm_sums[1:],
            head_spread(gqkv_sums[0, :mine])[None],
            head_spread(gqkv_sums[0, 2 * mine :])[None],
            sums_two,
        ]
    )
    fc_sums = lax.dynamic_update_slice_in_dim(
        jnp.zeros((dps * seqs * b_fc.shape[0],), F32), sum_fc[0], sq * ff_mine, axis=0
    )
    sums = jnp.concatenate(
        [
            vector_grads.reshape(dps, per, seqs, wide_vec).transpose(0, 2, 1, 3).reshape(
                dps, seqs, per * wide_vec
            ),
            fc_sums.reshape(dps, seqs, -1),
        ],
        axis=2,
    )
    sums = as_rows(sums.transpose(1, 0, 2).reshape(seqs, -1).astype(BF), lanes)
    qkv_in, sums, activations, g_fc, out_in = phase(qkv_in, sums, activations, g_fc, out_in)
    g_out = total_of(out_in)

    parts = exchange(repack_columns(where, qkv_in, recv, sums))
    input_grad = last_norm(gn1, x_own, gr, table)
    parts, input_grad, g_proj, g_out = phase(parts, input_grad, g_proj, g_out)
    g_qkv = restore_columns(where, parts, send, *w_qkv.shape)
    sums = parts[:, w_qkv.shape[0] :].reshape(seqs, -1)[:, : dps * count].astype(F32)
    sums = sums.sum(axis=0).reshape(dps, count)
    sums = {k: lax.dynamic_index_in_dim(sums, dp ^ k, 0, keepdims=False) for k in range(dps)}
    sums = total_of(in_order(sums[0], send_rel(sums, "dp", near + far)))
    return (
        activations.T,
        input_grad.T,
        g_qkv,
        g_out,
        sums[: per * wide_vec].reshape(per, wide_vec),
        g_fc,
        sums[per * wide_vec :],
        g_proj.T,
    )


def solution(mesh):
    rows = P(("dp", "seq"), None)
    grid = P("dp", "seq")
    line = P(("dp", "seq"))
    return jax.shard_map(
        body,
        mesh=mesh,
        in_specs=(rows, grid, grid, grid, grid, line, grid, rows),
        out_specs=(rows, rows, grid, grid, grid, grid, line, grid),
        check_vma=False,
    )
```

```python
import functools
import math

import jax
import jax.numpy as jnp
import numpy as np
from jax import lax
from jax.experimental import pallas as pl
from jax.experimental.pallas import tpu as pltpu
from jax.sharding import PartitionSpec as P

HD = 64
PAIR = 2 * HD
EPSILON = 1e-05
GELU_C = 0.7978845608028654
NEG_FILL = -1e30
BF = jnp.bfloat16
F32 = jnp.float32


def head_plan(head_count, seq_count, width):
    slots = -(-head_count // seq_count)
    slots += slots % 2
    model = head_count * HD

    def tables(turn):
        owner = np.full((seq_count, slots), -1, np.int32)
        for head in range(head_count):
            row = head // seq_count
            owner[(head + turn * row) % seq_count, row] = head
        place = {}
        for dev in range(seq_count):
            for slot in range(slots):
                if owner[dev, slot] >= 0:
                    place[int(owner[dev, slot])] = (dev, slot)
        lists = [[[] for _ in range(seq_count)] for _ in range(seq_count)]
        for col in range(3 * model):
            kind, rest = divmod(col, model)
            head, lane = divmod(rest, HD)
            dev, slot = place[head]
            src, local = divmod(col, width)
            lists[src][dev].append((local, (kind * slots + slot) * HD + lane))
        most = max(len(cell) for row in lists for cell in row)
        return most, owner, lists

    best = min((tables(turn) for turn in range(seq_count)), key=lambda t: t[0])
    most, owner, lists = best
    wide = -(-most // 128) * 128
    send = np.full((seq_count, seq_count, wide), -1, np.int32)
    recv = np.full((seq_count, seq_count, wide), -1, np.int32)
    for src in range(seq_count):
        for dev in range(seq_count):
            for i, (local, target) in enumerate(lists[src][dev]):
                send[src, dev, i] = local
                recv[src, dev, i] = target
    return slots, owner, wide, send, recv


ANY = pl.BlockSpec(memory_space=pl.ANY)
WHOLE = pl.BlockSpec(memory_space=pltpu.VMEM)
SCALAR = pl.BlockSpec(memory_space=pltpu.SMEM)


def blocks_of(*shapes):
    return [pl.BlockSpec(s.shape, lambda n=len(s.shape): (0,) * n) for s in shapes]


ROOM = pltpu.CompilerParams(vmem_limit_bytes=56 * 1024 * 1024)


def like(shape, kind=BF):
    return jax.ShapeDtypeStruct(shape, kind)


def phase(*values):
    return lax.optimization_barrier(values)


def xor_perm(count, k):
    return [(i, i ^ k) for i in range(count)]


def near_far(count):
    every = range(1, count)
    return [k for k in every if not k & (k - 1)], [k for k in every if k & (k - 1)]


def send_rel(blocks, axis, ks):
    count = lax.axis_size(axis)
    return {k: lax.ppermute(blocks[k], axis, xor_perm(count, k)) for k in ks}


def in_order(mine, *found):
    every = {0: mine}
    for part in found:
        every.update(part)
    return [every[k] for k in range(len(every))]


def can_halve(count, rows):
    return count == 4 and rows % 16 == 0


def cut(rows):
    return 16 * (rows // 16 - rows // 32)


def split_far(chunks):
    if len(chunks) != 4:
        return chunks
    far = chunks[3]
    half = far.shape[0] // 2 if far.ndim == 3 else cut(far.shape[0])
    return list(chunks[:3]) + [far[:half], far[half:]]


def reduce_first(chunks):
    if len(chunks) == 5:
        return [
            lax.ppermute(chunks[3], "dp", xor_perm(4, 1)),
            lax.ppermute(chunks[4], "dp", xor_perm(4, 2)),
        ]
    near, far = near_far(len(chunks))
    return list(send_rel(dict(enumerate(chunks)), "dp", far).values())


def reduce_second(chunks, found):
    if len(chunks) == 5:
        first, second = merge_halves(chunks[1], chunks[2], *found)
        return [
            chunks[0],
            lax.ppermute(first, "dp", xor_perm(4, 1)),
            lax.ppermute(second, "dp", xor_perm(4, 2)),
        ]
    near, far = near_far(len(chunks))
    return [chunks[0]] + found + list(send_rel(dict(enumerate(chunks)), "dp", near).values())


def merge_kernel(one_ref, two_ref, top_ref, low_ref, first_ref, second_ref):
    half = top_ref.shape[0]
    first_ref[:half] = one_ref[:half]
    first_ref[half:] = (one_ref[half:].astype(F32) + low_ref[...].astype(F32)).astype(BF)
    second_ref[:half] = (two_ref[:half].astype(F32) + top_ref[...].astype(F32)).astype(BF)
    second_ref[half:] = two_ref[half:]


def merge_halves(one, two, top, low):
    shape = like(one.shape)
    return pl.pallas_call(
        merge_kernel,
        in_specs=[WHOLE] * 4,
        out_specs=blocks_of(shape, shape),
        out_shape=[shape, shape],
        compiler_params=ROOM,
    )(one, two, top, low)


def gather_far(found, far):
    if len(found) + len(far) != 4:
        return {(k, 0): b for k, b in send_rel({k: found[0, 0] for k in far}, "dp", far).items()}
    half = found[0, 0].shape[0] // 2
    return {
        (3, 0): lax.ppermute(found[2, 0][:half], "dp", xor_perm(4, 1)),
        (3, half): lax.ppermute(found[1, 0][half:], "dp", xor_perm(4, 2)),
    }


def swap_core(block):
    return lax.ppermute(block, "seq", xor_perm(lax.axis_size("seq"), 1))


def exchange(block):
    return lax.all_to_all(block, "seq", 0, 0, tiled=True)


def chip_permute(block, pairs):
    return lax.ppermute(
        block, "seq", [(2 * a + core, 2 * b + core) for a, b in pairs for core in range(2)]
    )


def chips():
    return lax.axis_size("seq") // 2


def gather_first(block):
    count = chips()
    fetch = lambda off: chip_permute(block, [((z + off) % count, z) for z in range(count)])
    if count != 4:
        return [block] + [fetch(off) for off in range(1, count)]
    return [block, fetch(1), None, fetch(3)]


def gather_second(found):
    if len(found) != 4:
        return found
    above = chip_permute(found[3], [(1, 2), (2, 3)])
    below = chip_permute(found[1], [(2, 1), (1, 0)])
    far = jnp.where(lax.axis_index("seq") >= 4, above, below)
    return [found[0], found[1], far, found[3]]


def scatter_first(chunks):
    count = chips()
    if count != 4:
        return [
            chip_permute(chunks[off], [(z, (z + off) % count) for z in range(count)])
            for off in range(1, count)
        ]
    above = chip_permute(chunks[2], [(0, 1), (1, 2)])
    below = chip_permute(chunks[2], [(3, 2), (2, 1)])
    return [above, below]


def scatter_second(chunks, found):
    count = chips()
    if count != 4:
        return [chunks[0]] + found
    up = total_of([chunks[1], found[0]]).astype(BF)
    down = total_of([chunks[3], found[1]]).astype(BF)
    up = chip_permute(up, [(z, (z + 1) % 4) for z in range(4)])
    down = chip_permute(down, [(z, (z - 1) % 4) for z in range(4)])
    return [chunks[0], up, down]


def total_of(parts):
    total = parts[0].astype(F32)
    for part in parts[1:]:
        total = total + part.astype(F32)
    return total


def as_rows(values, lanes):
    size = -values.shape[1] % (16 * lanes)
    return jnp.pad(values, ((0, 0), (0, size))).reshape(values.shape[0], -1, lanes)


def normalise(rows):
    mean = jnp.mean(rows, axis=-1, keepdims=True)
    centred = rows - mean
    inverse = lax.rsqrt(jnp.mean(centred * centred, axis=-1, keepdims=True) + EPSILON)
    return centred * inverse, inverse


def norm_back(grad, unit, inverse, gain):
    scaled = grad * gain
    return (
        scaled
        - jnp.mean(scaled, axis=-1, keepdims=True)
        - unit * jnp.mean(scaled * unit, axis=-1, keepdims=True)
    ) * inverse


def gelu_parts(u):
    square = u * u
    t = jnp.tanh(u * (GELU_C + GELU_C * 0.044715 * square))
    half = 0.5 + 0.5 * t
    slope = half + u * (0.5 - 0.5 * t * t) * (GELU_C + 3 * 0.044715 * GELU_C * square)
    return u * half, slope


def mm(a, b):
    return jnp.dot(a, b, preferred_element_type=F32)


def mm_nt(a, b):
    return lax.dot_general(a, b, (((1,), (1,)), ((), ())), preferred_element_type=F32)


def mm_tn(a, b):
    return lax.dot_general(a, b, (((0,), (0,)), ((), ())), preferred_element_type=F32)


def run_copies(pairs, sems):
    found = [pltpu.make_async_copy(src, dst, sems.at[i]) for i, (src, dst) in enumerate(pairs)]
    for c in found:
        c.start()
    return found


def wait_for(copies):
    for c in copies:
        c.wait()


def stage_shape(dps, depth, width):
    return (dps, depth, width) if depth % 16 else (1, 16, 128)


def place_rows(where, refs, store, stage, sems, outward=False):
    depth = refs[0].shape[0]
    if outward and len(refs) == 5:
        pairs = []
        for k, ref in zip((0, 1, 2, 3, 3), refs):
            first = (where[0] ^ k) * depth
            if ref is refs[4]:
                first = first + refs[3].shape[0]
            pairs.append((store.at[pl.ds(pl.multiple_of(first, 16), ref.shape[0]), :], ref))
        return run_copies(pairs, sems)
    if depth % 16:
        spots = [stage.at[where[0] ^ k] for k in range(len(refs))]
    else:
        spots = [
            store.at[pl.ds(pl.multiple_of((where[0] ^ k) * depth, 16), depth), :]
            for k in range(len(refs))
        ]
    if outward:
        if depth % 16:
            for p in range(len(refs)):
                stage[p] = store[p * depth : (p + 1) * depth, :]
        return run_copies(list(zip(spots, refs)), sems)
    return run_copies(list(zip(refs, spots)), sems)


def settle_rows(copies, store, stage):
    wait_for(copies)
    depth = stage.shape[1]
    if depth % 16:
        for p in range(stage.shape[0]):
            store[p * depth : (p + 1) * depth, :] = stage[p]


def hot(row, count):
    return (
        lax.broadcasted_iota(jnp.int32, (count, row.shape[1]), 0) == row
    ).astype(BF)


def pack_kernel(where, w_ref, send_ref, more_ref, out_ref):
    depth = w_ref.shape[0]
    for n in range(out_ref.shape[0]):
        out_ref[n, 0:depth] = mm(w_ref[...], hot(send_ref[where[1], n], w_ref.shape[1])).astype(BF)
        out_ref[n, depth:] = more_ref[...]


def pack_columns(where, w_qkv, send, more):
    seqs, _, _, wide = send.shape
    shape = like((seqs, w_qkv.shape[0] + more.shape[0], wide))
    return pl.pallas_call(
        pack_kernel,
        in_specs=[SCALAR, WHOLE, WHOLE, WHOLE],
        out_specs=blocks_of(shape)[0],
        out_shape=shape,
        compiler_params=ROOM,
    )(where, w_qkv, send, more)


def unpack_kernel(where, recv_ref, in_ref, out_ref):
    total = None
    for n in range(in_ref.shape[0]):
        part = mm_nt(in_ref[n, 0 : out_ref.shape[0]], hot(recv_ref[n, where[1]], out_ref.shape[1]))
        total = part if total is None else total + part
    out_ref[...] = total.astype(BF)


def unpack_columns(where, parts, recv, depth, width):
    return pl.pallas_call(
        unpack_kernel,
        in_specs=[SCALAR, WHOLE, WHOLE],
        out_specs=blocks_of(like((depth, width)))[0],
        out_shape=like((depth, width)),
        compiler_params=ROOM,
    )(where, recv, parts)


def repack_kernel(where, recv_ref, more_ref, *rest):
    parts, out_ref = rest[:-1], rest[-1]
    grad = total_of([p[...] for p in parts]).astype(BF)
    depth = grad.shape[0]
    for n in range(out_ref.shape[0]):
        out_ref[n, 0:depth] = mm(grad, hot(recv_ref[n, where[1]], grad.shape[1])).astype(BF)
        out_ref[n, depth:] = more_ref[n]


def repack_columns(where, parts, recv, more):
    seqs, _, _, wide = recv.shape
    shape = like((seqs, parts[0].shape[0] + more.shape[1], wide))
    return pl.pallas_call(
        repack_kernel,
        in_specs=[SCALAR] + [WHOLE] * (2 + len(parts)),
        out_specs=blocks_of(shape)[0],
        out_shape=shape,
        compiler_params=ROOM,
    )(where, recv, more, *parts)


def restore_kernel(where, send_ref, in_ref, out_ref):
    depth = out_ref.shape[0]
    total = None
    for n in range(in_ref.shape[0]):
        part = mm_nt(in_ref[n, 0:depth], hot(send_ref[where[1], n], out_ref.shape[1]))
        total = part if total is None else total + part
    out_ref[...] = total


def restore_columns(where, parts, send, depth, width):
    return pl.pallas_call(
        restore_kernel,
        in_specs=[SCALAR, WHOLE, WHOLE],
        out_specs=blocks_of(like((depth, width)))[0],
        out_shape=like((depth, width), F32),
        compiler_params=ROOM,
    )(where, send, parts)


def piece_rows(total, count):
    tiles = total // 16
    return 16 * -(-tiles // count), lambda q: 16 * ((q * tiles) // count)


def pieces_kernel(where, w_ref, *outs):
    size, start = piece_rows(w_ref.shape[1], len(outs))
    for k, ref in enumerate(outs):
        first = pl.multiple_of(start(where[0] ^ k), 16)
        ref[...] = w_ref[:, pl.ds(first, size), :]


def proj_pieces(where, w_proj, dps):
    ratio, ff_mine, col = w_proj.shape
    size, _ = piece_rows(ff_mine, dps)
    return pl.pallas_call(
        pieces_kernel,
        in_specs=[SCALAR, WHOLE],
        out_specs=blocks_of(*[like((ratio, size, col))] * dps),
        out_shape=[like((ratio, size, col))] * dps,
        compiler_params=ROOM,
    )(where, w_proj)


def turn_kernel(where, *rest):
    ins, (out_ref, sems) = rest[:-2], rest[-2:]
    ratio = ins[0].shape[0]
    spots = [out_ref.at[pl.ds((where[0] ^ k) * ratio, ratio)] for k in range(len(ins))]
    wait_for(run_copies(list(zip(ins, spots)), sems))


def turn_pieces(where, parts):
    ratio, size, col = parts[0].shape
    return pl.pallas_call(
        turn_kernel,
        in_specs=[SCALAR] + [WHOLE] * len(parts),
        out_specs=blocks_of(like((ratio * len(parts), size, col)))[0],
        out_shape=like((ratio * len(parts), size, col)),
        scratch_shapes=[pltpu.SemaphoreType.DMA((len(parts),))],
        compiler_params=ROOM,
    )(where, *parts)


def join_kernel(in_ref, out_ref):
    width = in_ref.shape[2]
    for n in range(in_ref.shape[0]):
        out_ref[:, n * width : (n + 1) * width] = in_ref[n]


def join_columns(parts):
    seqs, size, col = parts.shape
    return pl.pallas_call(
        join_kernel,
        in_specs=[WHOLE],
        out_specs=blocks_of(like((size, col * seqs)))[0],
        out_shape=like((size, col * seqs)),
        compiler_params=ROOM,
    )(parts)


def split_kernel(*refs):
    out_ref = refs[-1]
    total = total_of([r[...] for r in refs[:-1]]).astype(BF)
    width = out_ref.shape[2]
    for n in range(out_ref.shape[0]):
        out_ref[n] = total[:, n * width : (n + 1) * width]


def split_columns(parts, seqs):
    size, model = parts[0].shape
    return pl.pallas_call(
        split_kernel,
        in_specs=[WHOLE] * len(parts),
        out_specs=blocks_of(like((seqs, size, model // seqs)))[0],
        out_shape=like((seqs, size, model // seqs)),
        compiler_params=ROOM,
    )(*parts)


def rows_kernel(where, *rest):
    ins, (out_ref, store, sems) = rest[:-3], rest[-3:]
    dps, ratio, size, _ = store.shape
    ff_mine = out_ref.shape[1] // ratio
    _, start = piece_rows(ff_mine, dps)
    wait_for(run_copies([(ref, store.at[where[0] ^ k]) for k, ref in enumerate(ins)], sems))
    for q in range(dps):
        for b in range(ratio):
            first = b * ff_mine + start(q)
            out_ref[:, first : first + size] = store[q, b].astype(F32).T


def proj_rows(where, parts, ff_mine):
    ratio, size, col = parts[0].shape
    return pl.pallas_call(
        rows_kernel,
        in_specs=[SCALAR] + [ANY] * len(parts),
        out_specs=blocks_of(like((col, ratio * ff_mine)))[0],
        out_shape=like((col, ratio * ff_mine), F32),
        scratch_shapes=[
            pltpu.VMEM((len(parts), ratio, size, col), BF),
            pltpu.SemaphoreType.DMA((len(parts),)),
        ],
        compiler_params=ROOM,
    )(where, *parts)


def head_masks(rows):
    first = lax.broadcasted_iota(jnp.int32, (rows, PAIR), 1) < HD
    causal = lax.broadcasted_iota(jnp.int32, (rows, rows), 0) >= lax.broadcasted_iota(
        jnp.int32, (rows, rows), 1
    )
    return first, causal


def masked_scores(q, keys, causal):
    rows, seen = q.shape[0], keys.shape[0]
    s = mm_nt(q, keys)
    tail = jnp.where(causal, s[:, seen - rows :], NEG_FILL)
    return tail if seen == rows else jnp.concatenate([s[:, : seen - rows], tail], axis=1)


def attend_rows(q, keys, values, first, causal):
    q = q * BF(1.0 / math.sqrt(HD))
    outs, logs = [], []
    for mine in (first, ~first):
        s = masked_scores(jnp.where(mine, q, BF(0)), keys, causal)
        top = jnp.max(s, axis=-1, keepdims=True)
        e = jnp.exp(s - top)
        total = jnp.sum(e, axis=-1, keepdims=True)
        outs.append(mm(e.astype(BF), values) / total)
        logs.append(top + jnp.log(total))
    return jnp.where(first, outs[0], outs[1]).astype(BF), jnp.where(first, logs[0], logs[1])


def attend_kernel(pairs, dps, where, x_ref, vec_ref, bias_ref, *rest):
    w_refs = rest[:dps]
    n1_ref, qkv_ref, att_ref, lse_ref, w, stage, qkv, sems = rest[dps:]
    i = pl.program_id(0)
    rows = x_ref.shape[0]
    part = rows // 2

    @pl.when(i == 0)
    def _():
        settle_rows(place_rows(where, w_refs, w, stage, sems), w, stage)

    unit, _ = normalise(x_ref[...].astype(F32))
    n1 = (unit * vec_ref[0:1, :] + vec_ref[1:2, :]).astype(BF)
    n1_ref[...] = n1
    tile = (mm(n1, w[...]) + bias_ref[...]).astype(BF)
    qkv_ref[...] = tile
    qkv[pl.ds(pl.multiple_of(i * rows, rows), rows), :] = tile
    first, causal = head_masks(rows)
    for j in range(qkv.shape[0] // rows):

        @pl.when(i == j)
        def _(j=j):
            seen = (j + 1) * rows
            for g in range(pairs):
                lanes = slice(g * PAIR, (g + 1) * PAIR)
                keys = qkv[0:seen, (pairs + g) * PAIR : (pairs + g + 1) * PAIR]
                values = qkv[0:seen, (2 * pairs + g) * PAIR : (2 * pairs + g + 1) * PAIR]
                out, log = attend_rows(qkv[j * rows : seen, lanes], keys, values, first, causal)
                for b in range(2):
                    att_ref[b, :, lanes] = out[b * part : (b + 1) * part]
                lse_ref[:, lanes] = log


def attend(where, x_all, table, bias, weights, part):
    length, model = x_all.shape
    depth, width = weights[0].shape
    dps = len(weights)
    heads = width // 3
    rows = 2 * part
    whole = lambda a: pl.BlockSpec(a.shape, lambda i: (0,) * a.ndim)
    tile = lambda cols: pl.BlockSpec((rows, cols), lambda i: (i, 0))
    return pl.pallas_call(
        functools.partial(attend_kernel, heads // PAIR, dps),
        grid=(length // rows,),
        in_specs=[SCALAR, tile(model), whole(table), whole(bias)] + [ANY] * dps,
        out_specs=[
            tile(model),
            tile(width),
            pl.BlockSpec((2, part, heads), lambda i: (i, 0, 0)),
            tile(heads),
            pl.BlockSpec((model, width), lambda i: (0, 0)),
        ],
        out_shape=[
            like((length, model)),
            like((length, width)),
            like((length // part, part, heads)),
            like((length, heads), F32),
            like((model, width)),
        ],
        scratch_shapes=[
            pltpu.VMEM(stage_shape(dps, depth, width), BF),
            pltpu.VMEM((length, width), BF),
            pltpu.SemaphoreType.DMA((dps,)),
        ],
        compiler_params=ROOM,
    )(where, x_all, table, bias, *weights)


def attend_back_kernel(pairs, qkv_ref, ga_ref, lse_ref, gqkv_ref, sums_ref, ak, av):
    length = qkv_ref.shape[0]
    part = ga_ref.shape[1]
    rows = 2 * part
    first, causal = head_masks(rows)
    for g in range(pairs):
        lanes = slice(g * PAIR, (g + 1) * PAIR)
        k_lanes = slice((pairs + g) * PAIR, (pairs + g + 1) * PAIR)
        v_lanes = slice((2 * pairs + g) * PAIR, (2 * pairs + g + 1) * PAIR)
        ak[...] = jnp.zeros_like(ak)
        av[...] = jnp.zeros_like(av)
        for i in range(length // rows):
            here = slice(i * rows, (i + 1) * rows)
            seen = (i + 1) * rows
            q = qkv_ref[here, lanes] * BF(1.0 / math.sqrt(HD))
            ga = jnp.concatenate([ga_ref[b, :, lanes] for b in (2 * i, 2 * i + 1)], axis=0)
            keys = qkv_ref[0:seen, k_lanes]
            values = qkv_ref[0:seen, v_lanes]
            grads = []
            for h, mine in enumerate((first, ~first)):
                q_h = jnp.where(mine, q, BF(0))
                ga_h = jnp.where(mine, ga, BF(0))
                s = masked_scores(q_h, keys, causal)
                lane = g * PAIR + h * HD
                p = jnp.exp(s - lse_ref[here, lane : lane + 1])
                gp = mm_nt(ga_h, values)
                centre = jnp.sum(p * gp, axis=-1, keepdims=True)
                gs = (p * (gp - centre)).astype(BF)
                av[0:seen, :] += mm_tn(p.astype(BF), ga_h)
                ak[0:seen, :] += mm_tn(gs, q_h)
                grads.append(mm(gs, keys))
            gqkv_ref[here, lanes] = (
                jnp.where(first, grads[0], grads[1]) * (1.0 / math.sqrt(HD))
            ).astype(BF)
        gqkv_ref[:, k_lanes] = ak[...].astype(BF)
        gqkv_ref[:, v_lanes] = av[...].astype(BF)
    sums_ref[...] = jnp.sum(gqkv_ref[...].astype(F32), axis=0, keepdims=True)


def attend_back(qkv, grad, lse):
    length, width = qkv.shape
    return pl.pallas_call(
        functools.partial(attend_back_kernel, grad.shape[2] // PAIR),
        in_specs=[WHOLE] * 3,
        out_specs=[WHOLE, WHOLE],
        out_shape=[like((length, width)), like((1, width), F32)],
        scratch_shapes=[pltpu.VMEM((length, PAIR), F32), pltpu.VMEM((length, PAIR), F32)],
        compiler_params=ROOM,
    )(qkv, grad, lse)


def grad_blocks_kernel(where, a_ref, g_ref, *rest):
    outs, (store, stage, sems) = rest[:-3], rest[-3:]
    g = g_ref[...]
    model = a_ref.shape[1]
    for a in range(0, model, 256):
        b = min(model, a + 256)
        store[a:b, :] = mm_tn(a_ref[:, a:b], g).astype(BF)
    wait_for(place_rows(where, outs, store, stage, sems, True))


def chunk_shapes(count, rows, cols):
    shapes = [like((rows, cols))] * count
    if can_halve(count, rows):
        shapes[3:] = [like((cut(rows), cols)), like((rows - cut(rows), cols))]
    return shapes


def grad_blocks(where, a, g, dps):
    model, width = a.shape[1], g.shape[1]
    depth = model // dps
    shapes = chunk_shapes(dps, depth, width)
    return pl.pallas_call(
        grad_blocks_kernel,
        in_specs=[SCALAR, WHOLE, WHOLE],
        out_specs=[ANY] * len(shapes),
        out_shape=shapes,
        scratch_shapes=[
            pltpu.VMEM((model, width), BF),
            pltpu.VMEM(stage_shape(dps, depth, width), BF),
            pltpu.SemaphoreType.DMA((len(shapes),)),
        ],
        compiler_params=ROOM,
    )(where, a, g)


def grad_rows_kernel(g_ref, n1_ref, w_ref, out_ref, sums_ref):
    @pl.when(pl.program_id(0) == 0)
    def _():
        sums_ref[...] = jnp.zeros_like(sums_ref)

    grad = mm_nt(g_ref[...], w_ref[...])
    sums_ref[0:1, :] += jnp.sum(grad * n1_ref[...].astype(F32), axis=0, keepdims=True)
    sums_ref[1:2, :] += jnp.sum(grad, axis=0, keepdims=True)
    out_ref[...] = grad.astype(BF)


def grad_rows(gqkv, weights, n1, rows):
    length, model = n1.shape
    width = weights.shape[1]
    tile = lambda cols: pl.BlockSpec((rows, cols), lambda i: (i, 0))
    return pl.pallas_call(
        grad_rows_kernel,
        grid=(length // rows,),
        in_specs=[tile(width), tile(model), WHOLE],
        out_specs=[tile(model), pl.BlockSpec((2, model), lambda i: (0, 0))],
        out_shape=[like((length, model)), like((2, model), F32)],
        compiler_params=ROOM,
    )(gqkv, n1, weights)


def place_pieces(where, refs, store, sems):
    size, start = piece_rows(store.shape[0], len(refs))
    starts = [start(q) for q in range(len(refs))] + [store.shape[0]]
    least = min(b - a for a, b in zip(starts, starts[1:]))
    count = len(refs)
    copies, more = [], []
    for k, ref in enumerate(refs):
        first = start(where[0] ^ k)
        spot = pl.ds(pl.multiple_of(first, 16), least)
        copies.append(
            pltpu.make_async_copy(ref.at[pl.ds(0, least), :], store.at[spot, :], sems.at[k])
        )
        if size > least:
            spot = pl.ds(pl.multiple_of(first + least, 16), size - least)
            rest = ref.at[pl.ds(least, size - least), :]
            more.append(
                (
                    start((where[0] ^ k) + 1) - first > least,
                    pltpu.make_async_copy(rest, store.at[spot, :], sems.at[count + k]),
                )
            )
    for c in copies:
        c.start()
    for needed, c in more:
        pl.when(needed)(c.start)
    wait_for(copies)
    for needed, c in more:
        pl.when(needed)(c.wait)


def gather_fc_kernel(where, *rest):
    f_refs, (wf, stage, sems) = rest[:-3], rest[-3:]
    settle_rows(place_rows(where, f_refs, wf, stage, sems), wf, stage)


def gather_fc(where, fc):
    dps = len(fc)
    depth, width = fc[0].shape
    return pl.pallas_call(
        gather_fc_kernel,
        in_specs=[SCALAR] + [ANY] * dps,
        out_specs=WHOLE,
        out_shape=like((depth * dps, width)),
        scratch_shapes=[
            pltpu.VMEM(stage_shape(dps, depth, width), BF),
            pltpu.SemaphoreType.DMA((dps,)),
        ],
        compiler_params=ROOM,
    )(where, *fc)


def gather_proj_kernel(where, *rest):
    p_refs, (wp, sems) = rest[:-2], rest[-2:]
    place_pieces(where, p_refs, wp, sems)


def gather_proj(where, proj, ff_mine):
    dps = len(proj)
    return pl.pallas_call(
        gather_proj_kernel,
        in_specs=[SCALAR] + [ANY] * dps,
        out_specs=WHOLE,
        out_shape=like((ff_mine, proj[0].shape[1])),
        scratch_shapes=[pltpu.SemaphoreType.DMA((2 * dps,))],
        compiler_params=ROOM,
    )(where, *proj)


def feed_kernel(n2_ref, gm_ref, bias_ref, wf, wp, e_ref, gu_ref, gn2_ref, sum_ref):
    @pl.when(pl.program_id(0) == 0)
    def _():
        sum_ref[...] = jnp.zeros_like(sum_ref)

    u = mm(n2_ref[...], wf[...]) + bias_ref[...]
    ge = mm_nt(gm_ref[...], wp[...])
    value, slope = gelu_parts(u)
    e_ref[...] = value.astype(BF)
    gu = (ge * slope).astype(BF)
    gu_ref[...] = gu
    sum_ref[...] += jnp.sum(gu.astype(F32), axis=0, keepdims=True)
    gn2_ref[...] = mm_nt(gu, wf[...]).astype(BF)


def feed(n2, gm, bias, fc, proj, rows):
    length, model = n2.shape
    width = fc.shape[1]
    whole = lambda shape: pl.BlockSpec(shape, lambda i: (0,) * len(shape))
    tile = lambda cols: pl.BlockSpec((rows, cols), lambda i: (i, 0))
    return pl.pallas_call(
        feed_kernel,
        grid=(length // rows,),
        in_specs=[tile(model), tile(model), whole(bias.shape), WHOLE, WHOLE],
        out_specs=[tile(width), tile(width), tile(model), whole((1, width))],
        out_shape=[
            like((length, width)),
            like((length, width)),
            like((length, model)),
            like((1, width), F32),
        ],
        compiler_params=ROOM,
    )(n2, gm, bias, fc, proj)


def grad_proj_kernel(dps, where, gm_ref, e_ref, *rest):
    outs, (store, sems) = rest[:-2], rest[-2:]
    width = store.shape[0]
    for a in range(0, width, 256):
        b = min(width, a + 256)
        store[a:b, :] = mm_tn(e_ref[:, a:b], gm_ref[...]).astype(BF)
    _, start = piece_rows(width, dps)
    pairs = []
    for i, ref in enumerate(outs):
        first = start(where[0] ^ min(i, dps - 1))
        if i == dps:
            first = first + outs[i - 1].shape[0]
        pairs.append((store.at[pl.ds(pl.multiple_of(first, 16), ref.shape[0]), :], ref))
    wait_for(run_copies(pairs, sems))


def grad_proj(where, gm, e, dps):
    model, width = gm.shape[1], e.shape[1]
    size, _ = piece_rows(width, dps)
    shapes = chunk_shapes(dps, size, model)
    return pl.pallas_call(
        functools.partial(grad_proj_kernel, dps),
        in_specs=[SCALAR, WHOLE, WHOLE],
        out_specs=[ANY] * len(shapes),
        out_shape=shapes,
        scratch_shapes=[
            pltpu.VMEM((width, model), BF),
            pltpu.SemaphoreType.DMA((len(shapes),)),
        ],
        compiler_params=ROOM,
    )(where, gm, e)


def feed_out_kernel(e_ref, wp, out_ref):
    out_ref[...] = mm(e_ref[...], wp[...]).astype(BF)


def feed_out(e, proj, rows):
    length, width = e.shape
    model = proj.shape[1]
    return pl.pallas_call(
        feed_out_kernel,
        grid=(length // rows,),
        in_specs=[pl.BlockSpec((rows, width), lambda i: (i, 0)), WHOLE],
        out_specs=pl.BlockSpec((rows, model), lambda i: (i, 0)),
        out_shape=like((length, model)),
        compiler_params=ROOM,
    )(e, proj)


def last_kernel(gn1_ref, gr_ref, vec_ref, x_hbm, out_ref, x_ref, sem):
    copy = pltpu.make_async_copy(x_hbm, x_ref, sem)
    copy.start()
    copy.wait()
    unit, inverse = normalise(x_ref[...].astype(F32))
    grad = norm_back(gn1_ref[...].astype(F32), unit, inverse, vec_ref[0:1, :])
    out_ref[...] = (gr_ref[...] + grad).T.astype(BF)


def last_norm(gn1, x, gr, table):
    shape = like(x.shape[::-1])
    return pl.pallas_call(
        last_kernel,
        in_specs=[WHOLE] * 3 + [ANY],
        out_specs=blocks_of(shape)[0],
        out_shape=shape,
        scratch_shapes=[pltpu.VMEM(x.shape, BF), pltpu.SemaphoreType.DMA],
        compiler_params=ROOM,
    )(gn1, gr, table, x)


def output_kernel(r_ref, mlp_ref, vec_ref, out_ref):
    out = r_ref[...] + (mlp_ref[...].astype(F32) + vec_ref[7:8, :])
    out_ref[...] = out.T.astype(BF)


def output_rows(r, mlp, table):
    shape = like(r.shape[::-1])
    return pl.pallas_call(
        output_kernel,
        in_specs=[WHOLE] * 3,
        out_specs=blocks_of(shape)[0],
        out_shape=shape,
        compiler_params=ROOM,
    )(r, mlp, table)


def line_blocks(block):
    seqs = lax.axis_size("seq")
    if seqs != 8:
        others = [lax.ppermute(block, "seq", xor_perm(seqs, 2 * dz)) for dz in range(1, seqs // 2)]
        return jnp.stack([block] + others)
    _, above, far, below = gather_second(gather_first(block))
    even = (lax.axis_index("seq") // 2) % 2 == 0
    return jnp.stack([block, jnp.where(even, above, below), far, jnp.where(even, below, above)])


def block_pairs(where, places, flat, store):
    return [
        (
            ref.at[j],
            store.at[where[0] ^ places[i // 2][0], where[1] ^ (2 * (places[i // 2][1] + j) + i % 2)],
        )
        for i, ref in enumerate(flat)
        for j in range(ref.shape[0])
    ]


def head_columns(att_ref, owner):
    count = int(owner.max()) + 1
    parts = []
    for h in range(count):
        dev, slot = [int(i[0]) for i in np.where(owner == h)]
        parts.append(att_ref[dev, :, slot * HD : (slot + 1) * HD])
    return jnp.concatenate(parts, axis=1)


def block_scratch(dps, flat):
    line, depth, width = flat[0].shape
    return [
        pltpu.VMEM((dps, 2 * line, depth, width), BF),
        pltpu.SemaphoreType.DMA((dps * 2 * line + 1,)),
    ]


def out_kernel(owner, places, where, att_ref, vec_ref, x_hbm, *rest):
    flat, (r_ref, n2_ref, store, sems, x_ref) = rest[:-5], rest[-5:]
    copies = run_copies(block_pairs(where, places, flat, store) + [(x_hbm, x_ref)], sems)
    att = head_columns(att_ref, owner)
    dps, seqs, depth, width = store.shape
    wait_for(copies)
    for n in range(seqs):
        here = slice(n * width, (n + 1) * width)
        total = x_ref[:, here].astype(F32) + vec_ref[4:5, here]
        for p in range(dps):
            total = total + mm(att[:, p * depth : (p + 1) * depth], store[p, n])
        r_ref[:, here] = total
    unit, _ = normalise(r_ref[...])
    n2_ref[...] = (unit * vec_ref[5:6, :] + vec_ref[6:7, :]).astype(BF)


def out_project(where, att, x, table, places, flat, owner):
    dps = max(k for k, _ in places) + 1
    return pl.pallas_call(
        functools.partial(out_kernel, owner, places),
        in_specs=[SCALAR, WHOLE, WHOLE, ANY] + [ANY] * len(flat),
        out_specs=blocks_of(x, x),
        out_shape=[like(x.shape, F32), like(x.shape)],
        scratch_shapes=block_scratch(dps, flat) + [pltpu.VMEM(x.shape, BF)],
        compiler_params=ROOM,
    )(where, att, table, x, *flat)


def back_kernel(owner, places, where, gn2_ref, r_ref, vec_ref, g_hbm, *rest):
    flat = rest[:-7]
    gr_ref, go_ref, ga_ref, sums_ref, store, sems, g_ref = rest[-7:]
    copies = run_copies([(g_hbm, g_ref)] + block_pairs(where, places, flat, store), sems)
    copies[0].wait()
    dps, seqs, depth, width = store.shape
    gn2 = gn2_ref[...].astype(F32)
    unit, inverse = normalise(r_ref[...])
    gr = g_ref[...].astype(F32) + norm_back(gn2, unit, inverse, vec_ref[5:6, :])
    go = gr.astype(BF)
    gr_ref[...] = gr
    go_ref[...] = go
    sums_ref[0:1, :] = jnp.sum(go.astype(F32), axis=0, keepdims=True)
    sums_ref[1:2, :] = jnp.sum(gn2 * unit, axis=0, keepdims=True)
    sums_ref[2:3, :] = jnp.sum(gn2, axis=0, keepdims=True)
    sums_ref[3:4, :] = jnp.sum(g_ref[...].astype(F32), axis=0, keepdims=True)
    wait_for(copies[1:])
    found = []
    for p in range(dps):
        total = mm_nt(go[:, 0:width], store[p, 0])
        for n in range(1, seqs):
            total = total + mm_nt(go[:, n * width : (n + 1) * width], store[p, n])
        found.append(total)
    ga = jnp.concatenate(found, axis=1).astype(BF)
    ga_ref[...] = jnp.zeros_like(ga_ref)
    for h in range(int(owner.max()) + 1):
        dev, slot = [int(i[0]) for i in np.where(owner == h)]
        ga_ref[dev, :, slot * HD : (slot + 1) * HD] = ga[:, h * HD : (h + 1) * HD]


def out_back(where, gn2, r, g, table, places, flat, owner):
    dps = max(k for k, _ in places) + 1
    shapes = [
        like(r.shape, F32),
        like(r.shape),
        like((owner.shape[0], r.shape[0], owner.shape[1] * HD)),
        like((4, r.shape[1]), F32),
    ]
    return pl.pallas_call(
        functools.partial(back_kernel, owner, places),
        in_specs=[SCALAR, WHOLE, WHOLE, WHOLE, ANY] + [ANY] * len(flat),
        out_specs=blocks_of(*shapes),
        out_shape=shapes,
        scratch_shapes=block_scratch(dps, flat) + [pltpu.VMEM(g.shape, BF)],
        compiler_params=ROOM,
    )(where, gn2, r, table, g, *flat)


def grad_out_kernel(owner, where, att_ref, far_att_ref, go_ref, far_go_ref, *rest):
    outs, (store, sems) = rest[:-2], rest[-2:]
    att = jnp.concatenate([head_columns(r, owner) for r in (att_ref, far_att_ref)], axis=0)
    go = jnp.concatenate([go_ref[...], far_go_ref[...]], axis=0)
    dps, line, depth, width = store.shape
    even = where[1] % 2 == 0
    for z in range(line):
        a, b = 2 * z * width, (2 * z + 1) * width
        cols = jnp.where(even, go[:, a : a + width], go[:, b : b + width])
        for p in range(dps):
            store[p, z] = mm_tn(att[:, p * depth : (p + 1) * depth], cols).astype(BF)
    pairs = [
        (store.at[where[0] ^ k, (where[1] // 2) ^ dz], ref.at[dz])
        for k, ref in enumerate(outs)
        for dz in range(line)
    ]
    wait_for(run_copies(pairs, sems))


def grad_out(where, att, far_att, go, far_go, dps, owner):
    seqs = att.shape[0]
    line, depth, width = seqs // 2, go.shape[1] // dps, go.shape[1] // seqs
    return pl.pallas_call(
        functools.partial(grad_out_kernel, owner),
        in_specs=[SCALAR] + [WHOLE] * 4,
        out_specs=[ANY] * dps,
        out_shape=[like((line, depth, width))] * dps,
        scratch_shapes=[
            pltpu.VMEM((dps, line, depth, width), BF),
            pltpu.SemaphoreType.DMA((dps * line,)),
        ],
        compiler_params=ROOM,
    )(where, att, far_att, go, far_go)


def body(tokens, w_qkv, w_out, vectors, w_fc, b_fc, w_proj, cotangent):
    dps = lax.axis_size("dp")
    seqs = lax.axis_size("seq")
    dp = lax.axis_index("dp")
    sq = lax.axis_index("seq")
    rows, model = tokens.shape
    head_count = model // HD
    slots, owner, wide, send, recv = head_plan(head_count, seqs, w_qkv.shape[1])
    send = jnp.asarray(send)[:, :, None, :]
    recv = jnp.asarray(recv)[:, :, None, :]
    mine = slots * HD
    ff_mine = w_fc.shape[1]
    ratio = seqs // dps
    col = w_proj.shape[1]
    where = jnp.stack([dp, sq]).astype(jnp.int32)
    per, wide_vec = vectors.shape
    own_heads = jnp.asarray(owner)[sq]
    pick = (own_heads[:, None] == jnp.arange(head_count)[None, :]).astype(F32)

    def head_rows(vector):
        return jnp.sum(pick[:, :, None] * vector.reshape(1, head_count, HD), axis=1).reshape(-1)

    def head_spread(vector):
        return jnp.sum(pick[:, :, None] * vector.reshape(slots, 1, HD), axis=0).reshape(-1)

    near, far = near_far(dps)
    copies = lambda block: {k: block for k in range(dps)}
    chunks = lambda blocks: dict(enumerate(blocks))

    lanes = send.shape[3]
    gm_all = lax.all_gather(cotangent, "seq", axis=0, tiled=True)
    small = jnp.concatenate([vectors.reshape(-1), b_fc])
    count = small.shape[0]
    small = jnp.stack(in_order(small, send_rel(copies(small), "dp", near + far)))
    small = as_rows(small.reshape(1, -1), lanes)[0]
    parts = exchange(pack_columns(where, w_qkv, send, small))
    wf = in_order(w_fc, send_rel(copies(w_fc), "dp", near + far))
    pieces = proj_pieces(where, w_proj.reshape(ratio, ff_mine, col), dps)
    parts, wf, x_own, out_own, pieces, gm_all = phase(
        parts, wf, tokens, w_out, pieces, gm_all
    )

    x_all = lax.all_gather(x_own, "seq", axis=0, tiled=True)
    own_qkv = unpack_columns(where, parts, recv, w_qkv.shape[0], 3 * mine)
    wq = in_order(own_qkv, send_rel(copies(own_qkv), "dp", near + far))
    line = line_blocks(out_own)
    pieces = in_order(pieces[0], send_rel(chunks(pieces), "dp", near + far))
    pieces = turn_pieces(where, pieces)
    small = parts[:, w_qkv.shape[0] :].reshape(seqs, -1)[:, : dps * count].astype(F32)
    small = jnp.take(small.reshape(seqs, dps, count), dp ^ jnp.arange(dps), axis=1)
    table = small[:, :, : per * wide_vec].reshape(seqs, dps, per, wide_vec)
    table = table.transpose(1, 2, 0, 3).reshape(dps * per, model)
    bias_fc = small[:, :, per * wide_vec :].transpose(1, 0, 2).reshape(-1)
    bias_fc = lax.dynamic_slice_in_dim(bias_fc, sq * ff_mine, ff_mine)[None]
    bias_qkv = jnp.concatenate(
        [head_rows(table[2]), jnp.zeros((mine,), F32), head_rows(table[3])]
    )[None]
    x_all, wq, line, pieces, table, bias_qkv = phase(x_all, wq, line, pieces, table, bias_qkv)

    pieces = exchange(pieces)
    wo = {(0, 0): line}
    wo.update({(k, 0): b for k, b in send_rel(copies(line), "dp", near).items()})
    n1_all, qkv, att, lse, wq = attend(where, x_all, table, bias_qkv, wq, rows)
    att, wo, pieces = phase(att, wo, pieces)

    att = exchange(att)
    wo_other = {place: swap_core(b) for place, b in wo.items()}
    found = gather_far(wo, far)
    wo.update(found)
    own_proj = join_columns(pieces)
    att, wo, wo_other, own_proj = phase(att, wo, wo_other, own_proj)
    wo_other.update({place: swap_core(wo[place]) for place in found})
    wp_near = send_rel(copies(own_proj), "dp", near)
    places = sorted(wo)
    flat = [b for place in places for b in (wo[place], wo_other[place])]
    r, n2 = out_project(where, att, x_own, table, places, flat, owner)
    n2, att, own_proj = phase(n2, att, own_proj)

    n2_all = lax.all_gather(n2, "seq", axis=0, tiled=True)
    wp = in_order(own_proj, wp_near, send_rel(copies(own_proj), "dp", far))
    far_att = swap_core(att)
    wf = gather_fc(where, wf)
    wf, wp = phase(wf, wp)
    wp = gather_proj(where, wp, ff_mine)
    n2_all, wp, far_att = phase(n2_all, wp, far_att)
    e, gu, gn2_part, sum_fc = feed(n2_all, gm_all, bias_fc, wf, wp, 2 * rows)

    gn2 = lax.psum_scatter(gn2_part, "seq", scatter_dimension=0, tiled=True)
    d_proj = grad_proj(where, gm_all, e, dps)
    proj_first = reduce_first(d_proj)
    d_fc = grad_blocks(where, n2_all, gu, dps)
    d_fc, proj_first, e_late = phase(d_fc, proj_first, e)
    proj_in = reduce_second(d_proj, proj_first)
    mlp = feed_out(e_late, wp, 2 * rows)
    gn2, d_fc, mlp, proj_in = phase(gn2, d_fc, mlp, proj_in)

    mlp = lax.psum_scatter(mlp, "seq", scatter_dimension=0, tiled=True)
    gr, go, ga, sums_two = out_back(where, gn2, r, cotangent, table, places, flat, owner)
    fc_first = reduce_first(d_fc)
    ga, go, fc_first = phase(ga, go, fc_first)

    ga = exchange(ga)
    d_out = split_far(grad_out(where, att, far_att, go, swap_core(go), dps, owner))
    g_proj = split_columns(proj_in, seqs)
    fc_in = reduce_second(d_fc, fc_first)
    ga, d_out, fc_in, g_proj = phase(ga, d_out, fc_in, g_proj)

    out_first = reduce_first(d_out)
    g_proj = exchange(g_proj)
    gqkv, gqkv_sums = attend_back(qkv, ga, lse)
    gqkv, out_first = phase(gqkv, out_first)
    gn1_part, norm_sums = grad_rows(gqkv, wq, n1_all, 2 * rows)
    gn1_part, gqkv, mlp, g_proj, d_out = phase(gn1_part, gqkv, mlp, g_proj, d_out)

    gn1 = lax.psum_scatter(gn1_part, "seq", scatter_dimension=0, tiled=True)
    out_in = reduce_second(d_out, out_first)
    d_qkv = grad_blocks(where, n1_all, gqkv, dps)
    d_qkv, out_in = phase(d_qkv, out_in)
    qkv_first = reduce_first(d_qkv)
    g_line = total_of(out_in).astype(BF)
    if seqs == 8:
        even = (sq // 2) % 2 == 0
        above = jnp.where(even, g_line[1], g_line[3])
        below = jnp.where(even, g_line[3], g_line[1])
        line_out = [g_line[0], above, g_line[2], below]
    else:
        line_out = [
            lax.dynamic_index_in_dim(
                g_line, ((sq // 2 + off) % (seqs // 2)) ^ (sq // 2), 0, keepdims=False
            )
            for off in range(seqs // 2)
        ]
    out_in = scatter_second(line_out, scatter_first(line_out))
    qkv_in = reduce_second(d_qkv, qkv_first)
    activations = output_rows(r, mlp, table)
    g_fc = total_of(fc_in)
    g_proj = {
        k: lax.dynamic_slice_in_dim(g_proj, (dp ^ k) * ratio, ratio, axis=0) for k in range(dps)
    }
    g_proj = in_order(g_proj[0], send_rel(g_proj, "dp", near + far))
    g_proj = proj_rows(where, g_proj, ff_mine)
    vector_grads = jnp.concatenate(
        [
            ((norm_sums[0] - table[1] * norm_sums[1]) / table[0])[None],
            norm_sums[1:],
            head_spread(gqkv_sums[0, :mine])[None],
            head_spread(gqkv_sums[0, 2 * mine :])[None],
            sums_two,
        ]
    )
    fc_sums = lax.dynamic_update_slice_in_dim(
        jnp.zeros((dps * seqs * b_fc.shape[0],), F32), sum_fc[0], sq * ff_mine, axis=0
    )
    sums = jnp.concatenate(
        [
            vector_grads.reshape(dps, per, seqs, wide_vec).transpose(0, 2, 1, 3).reshape(
                dps, seqs, per * wide_vec
            ),
            fc_sums.reshape(dps, seqs, -1),
        ],
        axis=2,
    )
    sums = as_rows(sums.transpose(1, 0, 2).reshape(seqs, -1).astype(BF), lanes)
    qkv_in, sums, activations, g_fc, out_in = phase(qkv_in, sums, activations, g_fc, out_in)
    g_out = total_of(out_in)

    parts = exchange(repack_columns(where, qkv_in, recv, sums))
    input_grad = last_norm(gn1, x_own, gr, table)
    parts, input_grad, g_proj, g_out = phase(parts, input_grad, g_proj, g_out)
    g_qkv = restore_columns(where, parts, send, *w_qkv.shape)
    sums = parts[:, w_qkv.shape[0] :].reshape(seqs, -1)[:, : dps * count].astype(F32)
    sums = sums.sum(axis=0).reshape(dps, count)
    sums = {k: lax.dynamic_index_in_dim(sums, dp ^ k, 0, keepdims=False) for k in range(dps)}
    sums = total_of(in_order(sums[0], send_rel(sums, "dp", near + far)))
    return (
        activations.T,
        input_grad.T,
        g_qkv,
        g_out,
        sums[: per * wide_vec].reshape(per, wide_vec),
        g_fc,
        sums[per * wide_vec :],
        g_proj.T,
    )


def solution(mesh):
    rows = P(("dp", "seq"), None)
    grid = P("dp", "seq")
    line = P(("dp", "seq"))
    return jax.shard_map(
        body,
        mesh=mesh,
        in_specs=(rows, grid, grid, grid, grid, line, grid, rows),
        out_specs=(rows, rows, grid, grid, grid, grid, line, grid),
        check_vma=False,
    )
```

```python
import functools
import math

import jax
import jax.numpy as jnp
import numpy as np
from jax import lax
from jax.experimental import pallas as pl
from jax.experimental.pallas import tpu as pltpu
from jax.sharding import PartitionSpec as P

HD = 64
PAIR = 2 * HD
EPSILON = 1e-05
GELU_C = 0.7978845608028654
NEG_FILL = -1e30
BF = jnp.bfloat16
F32 = jnp.float32


def head_plan(head_count, seq_count, width):
    slots = -(-head_count // seq_count)
    slots += slots % 2
    model = head_count * HD

    def tables(turn):
        owner = np.full((seq_count, slots), -1, np.int32)
        for head in range(head_count):
            row = head // seq_count
            owner[(head + turn * row) % seq_count, row] = head
        place = {}
        for dev in range(seq_count):
            for slot in range(slots):
                if owner[dev, slot] >= 0:
                    place[int(owner[dev, slot])] = (dev, slot)
        lists = [[[] for _ in range(seq_count)] for _ in range(seq_count)]
        for col in range(3 * model):
            kind, rest = divmod(col, model)
            head, lane = divmod(rest, HD)
            dev, slot = place[head]
            src, local = divmod(col, width)
            lists[src][dev].append((local, (kind * slots + slot) * HD + lane))
        most = max(len(cell) for row in lists for cell in row)
        return most, owner, lists

    best = min((tables(turn) for turn in range(seq_count)), key=lambda t: t[0])
    most, owner, lists = best
    wide = -(-most // 128) * 128
    send = np.full((seq_count, seq_count, wide), -1, np.int32)
    recv = np.full((seq_count, seq_count, wide), -1, np.int32)
    for src in range(seq_count):
        for dev in range(seq_count):
            for i, (local, target) in enumerate(lists[src][dev]):
                send[src, dev, i] = local
                recv[src, dev, i] = target
    return slots, owner, wide, send, recv


ANY = pl.BlockSpec(memory_space=pl.ANY)
WHOLE = pl.BlockSpec(memory_space=pltpu.VMEM)
SCALAR = pl.BlockSpec(memory_space=pltpu.SMEM)


def blocks_of(*shapes):
    return [pl.BlockSpec(s.shape, lambda n=len(s.shape): (0,) * n) for s in shapes]


ROOM = pltpu.CompilerParams(vmem_limit_bytes=56 * 1024 * 1024)


def like(shape, kind=BF):
    return jax.ShapeDtypeStruct(shape, kind)


def phase(*values):
    return lax.optimization_barrier(values)


def xor_perm(count, k):
    return [(i, i ^ k) for i in range(count)]


def near_far(count):
    every = range(1, count)
    return [k for k in every if not k & (k - 1)], [k for k in every if k & (k - 1)]


def send_rel(blocks, axis, ks):
    count = lax.axis_size(axis)
    return {k: lax.ppermute(blocks[k], axis, xor_perm(count, k)) for k in ks}


def in_order(mine, *found):
    every = {0: mine}
    for part in found:
        every.update(part)
    return [every[k] for k in range(len(every))]


def can_halve(count, rows):
    return count == 4 and rows % 16 == 0


def cut(rows):
    return 16 * (rows // 16 - rows // 32)


def split_far(chunks):
    if len(chunks) != 4:
        return chunks
    far = chunks[3]
    half = far.shape[0] // 2 if far.ndim == 3 else cut(far.shape[0])
    return list(chunks[:3]) + [far[:half], far[half:]]


def reduce_first(chunks):
    if len(chunks) == 5:
        return [
            lax.ppermute(chunks[3], "dp", xor_perm(4, 1)),
            lax.ppermute(chunks[4], "dp", xor_perm(4, 2)),
        ]
    near, far = near_far(len(chunks))
    return list(send_rel(dict(enumerate(chunks)), "dp", far).values())


def reduce_second(chunks, found):
    if len(chunks) == 5:
        first, second = merge_halves(chunks[1], chunks[2], *found)
        return [
            chunks[0],
            lax.ppermute(first, "dp", xor_perm(4, 1)),
            lax.ppermute(second, "dp", xor_perm(4, 2)),
        ]
    near, far = near_far(len(chunks))
    return [chunks[0]] + found + list(send_rel(dict(enumerate(chunks)), "dp", near).values())


def merge_kernel(one_ref, two_ref, top_ref, low_ref, first_ref, second_ref):
    half = top_ref.shape[0]
    first_ref[:half] = one_ref[:half]
    first_ref[half:] = (one_ref[half:].astype(F32) + low_ref[...].astype(F32)).astype(BF)
    second_ref[:half] = (two_ref[:half].astype(F32) + top_ref[...].astype(F32)).astype(BF)
    second_ref[half:] = two_ref[half:]


def merge_halves(one, two, top, low):
    shape = like(one.shape)
    return pl.pallas_call(
        merge_kernel,
        in_specs=[WHOLE] * 4,
        out_specs=blocks_of(shape, shape),
        out_shape=[shape, shape],
        compiler_params=ROOM,
    )(one, two, top, low)


def gather_far(found, far):
    if len(found) + len(far) != 4:
        return {(k, 0): b for k, b in send_rel({k: found[0, 0] for k in far}, "dp", far).items()}
    half = found[0, 0].shape[0] // 2
    return {
        (3, 0): lax.ppermute(found[2, 0][:half], "dp", xor_perm(4, 1)),
        (3, half): lax.ppermute(found[1, 0][half:], "dp", xor_perm(4, 2)),
    }


def swap_core(block):
    return lax.ppermute(block, "seq", xor_perm(lax.axis_size("seq"), 1))


def exchange(block):
    return lax.all_to_all(block, "seq", 0, 0, tiled=True)


def chip_permute(block, pairs):
    return lax.ppermute(
        block, "seq", [(2 * a + core, 2 * b + core) for a, b in pairs for core in range(2)]
    )


def chips():
    return lax.axis_size("seq") // 2


def gather_first(block):
    count = chips()
    fetch = lambda off: chip_permute(block, [((z + off) % count, z) for z in range(count)])
    if count != 4:
        return [block] + [fetch(off) for off in range(1, count)]
    return [block, fetch(1), None, fetch(3)]


def gather_second(found):
    if len(found) != 4:
        return found
    above = chip_permute(found[3], [(1, 2), (2, 3)])
    below = chip_permute(found[1], [(2, 1), (1, 0)])
    far = jnp.where(lax.axis_index("seq") >= 4, above, below)
    return [found[0], found[1], far, found[3]]


def scatter_first(chunks):
    count = chips()
    if count != 4:
        return [
            chip_permute(chunks[off], [(z, (z + off) % count) for z in range(count)])
            for off in range(1, count)
        ]
    above = chip_permute(chunks[2], [(0, 1), (1, 2)])
    below = chip_permute(chunks[2], [(3, 2), (2, 1)])
    return [above, below]


def scatter_second(chunks, found):
    count = chips()
    if count != 4:
        return [chunks[0]] + found
    up = total_of([chunks[1], found[0]]).astype(BF)
    down = total_of([chunks[3], found[1]]).astype(BF)
    up = chip_permute(up, [(z, (z + 1) % 4) for z in range(4)])
    down = chip_permute(down, [(z, (z - 1) % 4) for z in range(4)])
    return [chunks[0], up, down]


def total_of(parts):
    total = parts[0].astype(F32)
    for part in parts[1:]:
        total = total + part.astype(F32)
    return total


def as_rows(values, lanes):
    size = -values.shape[1] % (16 * lanes)
    return jnp.pad(values, ((0, 0), (0, size))).reshape(values.shape[0], -1, lanes)


def normalise(rows):
    mean = jnp.mean(rows, axis=-1, keepdims=True)
    centred = rows - mean
    inverse = lax.rsqrt(jnp.mean(centred * centred, axis=-1, keepdims=True) + EPSILON)
    return centred * inverse, inverse


def norm_back(grad, unit, inverse, gain):
    scaled = grad * gain
    return (
        scaled
        - jnp.mean(scaled, axis=-1, keepdims=True)
        - unit * jnp.mean(scaled * unit, axis=-1, keepdims=True)
    ) * inverse


def gelu_parts(u):
    square = u * u
    t = jnp.tanh(u * (GELU_C + GELU_C * 0.044715 * square))
    half = 0.5 + 0.5 * t
    slope = half + u * (0.5 - 0.5 * t * t) * (GELU_C + 3 * 0.044715 * GELU_C * square)
    return u * half, slope


def mm(a, b):
    return jnp.dot(a, b, preferred_element_type=F32)


def mm_nt(a, b):
    return lax.dot_general(a, b, (((1,), (1,)), ((), ())), preferred_element_type=F32)


def mm_tn(a, b):
    return lax.dot_general(a, b, (((0,), (0,)), ((), ())), preferred_element_type=F32)


def run_copies(pairs, sems):
    found = [pltpu.make_async_copy(src, dst, sems.at[i]) for i, (src, dst) in enumerate(pairs)]
    for c in found:
        c.start()
    return found


def wait_for(copies):
    for c in copies:
        c.wait()


def stage_shape(dps, depth, width):
    return (dps, depth, width) if depth % 16 else (1, 16, 128)


def place_rows(where, refs, store, stage, sems, outward=False):
    depth = refs[0].shape[0]
    if outward and len(refs) == 5:
        pairs = []
        for k, ref in zip((0, 1, 2, 3, 3), refs):
            first = (where[0] ^ k) * depth
            if ref is refs[4]:
                first = first + refs[3].shape[0]
            pairs.append((store.at[pl.ds(pl.multiple_of(first, 16), ref.shape[0]), :], ref))
        return run_copies(pairs, sems)
    if depth % 16:
        spots = [stage.at[where[0] ^ k] for k in range(len(refs))]
    else:
        spots = [
            store.at[pl.ds(pl.multiple_of((where[0] ^ k) * depth, 16), depth), :]
            for k in range(len(refs))
        ]
    if outward:
        if depth % 16:
            for p in range(len(refs)):
                stage[p] = store[p * depth : (p + 1) * depth, :]
        return run_copies(list(zip(spots, refs)), sems)
    return run_copies(list(zip(refs, spots)), sems)


def settle_rows(copies, store, stage):
    wait_for(copies)
    depth = stage.shape[1]
    if depth % 16:
        for p in range(stage.shape[0]):
            store[p * depth : (p + 1) * depth, :] = stage[p]


def hot(row, count):
    return (
        lax.broadcasted_iota(jnp.int32, (count, row.shape[1]), 0) == row
    ).astype(BF)


def pack_kernel(where, w_ref, send_ref, more_ref, out_ref):
    depth = w_ref.shape[0]
    for n in range(out_ref.shape[0]):
        out_ref[n, 0:depth] = mm(w_ref[...], hot(send_ref[where[1], n], w_ref.shape[1])).astype(BF)
        out_ref[n, depth:] = more_ref[...]


def pack_columns(where, w_qkv, send, more):
    seqs, _, _, wide = send.shape
    shape = like((seqs, w_qkv.shape[0] + more.shape[0], wide))
    return pl.pallas_call(
        pack_kernel,
        in_specs=[SCALAR, WHOLE, WHOLE, WHOLE],
        out_specs=blocks_of(shape)[0],
        out_shape=shape,
        compiler_params=ROOM,
    )(where, w_qkv, send, more)


def unpack_kernel(where, recv_ref, in_ref, out_ref):
    total = None
    for n in range(in_ref.shape[0]):
        part = mm_nt(in_ref[n, 0 : out_ref.shape[0]], hot(recv_ref[n, where[1]], out_ref.shape[1]))
        total = part if total is None else total + part
    out_ref[...] = total.astype(BF)


def unpack_columns(where, parts, recv, depth, width):
    return pl.pallas_call(
        unpack_kernel,
        in_specs=[SCALAR, WHOLE, WHOLE],
        out_specs=blocks_of(like((depth, width)))[0],
        out_shape=like((depth, width)),
        compiler_params=ROOM,
    )(where, recv, parts)


def repack_kernel(where, recv_ref, more_ref, *rest):
    parts, out_ref = rest[:-1], rest[-1]
    grad = total_of([p[...] for p in parts]).astype(BF)
    depth = grad.shape[0]
    for n in range(out_ref.shape[0]):
        out_ref[n, 0:depth] = mm(grad, hot(recv_ref[n, where[1]], grad.shape[1])).astype(BF)
        out_ref[n, depth:] = more_ref[n]


def repack_columns(where, parts, recv, more):
    seqs, _, _, wide = recv.shape
    shape = like((seqs, parts[0].shape[0] + more.shape[1], wide))
    return pl.pallas_call(
        repack_kernel,
        in_specs=[SCALAR] + [WHOLE] * (2 + len(parts)),
        out_specs=blocks_of(shape)[0],
        out_shape=shape,
        compiler_params=ROOM,
    )(where, recv, more, *parts)


def restore_kernel(where, send_ref, in_ref, out_ref):
    depth = out_ref.shape[0]
    total = None
    for n in range(in_ref.shape[0]):
        part = mm_nt(in_ref[n, 0:depth], hot(send_ref[where[1], n], out_ref.shape[1]))
        total = part if total is None else total + part
    out_ref[...] = total


def restore_columns(where, parts, send, depth, width):
    return pl.pallas_call(
        restore_kernel,
        in_specs=[SCALAR, WHOLE, WHOLE],
        out_specs=blocks_of(like((depth, width)))[0],
        out_shape=like((depth, width), F32),
        compiler_params=ROOM,
    )(where, send, parts)


def piece_rows(total, count):
    tiles = total // 16
    return 16 * -(-tiles // count), lambda q: 16 * ((q * tiles) // count)


def pieces_kernel(where, w_ref, *outs):
    size, start = piece_rows(w_ref.shape[1], len(outs))
    for k, ref in enumerate(outs):
        first = pl.multiple_of(start(where[0] ^ k), 16)
        ref[...] = w_ref[:, pl.ds(first, size), :]


def proj_pieces(where, w_proj, dps):
    ratio, ff_mine, col = w_proj.shape
    size, _ = piece_rows(ff_mine, dps)
    return pl.pallas_call(
        pieces_kernel,
        in_specs=[SCALAR, WHOLE],
        out_specs=blocks_of(*[like((ratio, size, col))] * dps),
        out_shape=[like((ratio, size, col))] * dps,
        compiler_params=ROOM,
    )(where, w_proj)


def turn_kernel(where, *rest):
    ins, (out_ref, sems) = rest[:-2], rest[-2:]
    ratio = ins[0].shape[0]
    spots = [out_ref.at[pl.ds((where[0] ^ k) * ratio, ratio)] for k in range(len(ins))]
    wait_for(run_copies(list(zip(ins, spots)), sems))


def turn_pieces(where, parts):
    ratio, size, col = parts[0].shape
    return pl.pallas_call(
        turn_kernel,
        in_specs=[SCALAR] + [WHOLE] * len(parts),
        out_specs=blocks_of(like((ratio * len(parts), size, col)))[0],
        out_shape=like((ratio * len(parts), size, col)),
        scratch_shapes=[pltpu.SemaphoreType.DMA((len(parts),))],
        compiler_params=ROOM,
    )(where, *parts)


def join_kernel(in_ref, out_ref):
    width = in_ref.shape[2]
    for n in range(in_ref.shape[0]):
        out_ref[:, n * width : (n + 1) * width] = in_ref[n]


def join_columns(parts):
    seqs, size, col = parts.shape
    return pl.pallas_call(
        join_kernel,
        in_specs=[WHOLE],
        out_specs=blocks_of(like((size, col * seqs)))[0],
        out_shape=like((size, col * seqs)),
        compiler_params=ROOM,
    )(parts)


def split_kernel(*refs):
    out_ref = refs[-1]
    total = total_of([r[...] for r in refs[:-1]]).astype(BF)
    width = out_ref.shape[2]
    for n in range(out_ref.shape[0]):
        out_ref[n] = total[:, n * width : (n + 1) * width]


def split_columns(parts, seqs):
    size, model = parts[0].shape
    return pl.pallas_call(
        split_kernel,
        in_specs=[WHOLE] * len(parts),
        out_specs=blocks_of(like((seqs, size, model // seqs)))[0],
        out_shape=like((seqs, size, model // seqs)),
        compiler_params=ROOM,
    )(*parts)


def rows_kernel(where, *rest):
    ins, (out_ref, store, sems) = rest[:-3], rest[-3:]
    dps, ratio, size, _ = store.shape
    ff_mine = out_ref.shape[1] // ratio
    _, start = piece_rows(ff_mine, dps)
    wait_for(run_copies([(ref, store.at[where[0] ^ k]) for k, ref in enumerate(ins)], sems))
    for q in range(dps):
        for b in range(ratio):
            first = b * ff_mine + start(q)
            out_ref[:, first : first + size] = store[q, b].astype(F32).T


def proj_rows(where, parts, ff_mine):
    ratio, size, col = parts[0].shape
    return pl.pallas_call(
        rows_kernel,
        in_specs=[SCALAR] + [ANY] * len(parts),
        out_specs=blocks_of(like((col, ratio * ff_mine)))[0],
        out_shape=like((col, ratio * ff_mine), F32),
        scratch_shapes=[
            pltpu.VMEM((len(parts), ratio, size, col), BF),
            pltpu.SemaphoreType.DMA((len(parts),)),
        ],
        compiler_params=ROOM,
    )(where, *parts)


def head_masks(rows):
    first = lax.broadcasted_iota(jnp.int32, (rows, PAIR), 1) < HD
    causal = lax.broadcasted_iota(jnp.int32, (rows, rows), 0) <= lax.broadcasted_iota(
        jnp.int32, (rows, rows), 1
    )
    return first, causal


def masked_scores(keys, q, causal):
    rows, seen = q.shape[0], keys.shape[0]
    s = mm_nt(keys, q)
    tail = jnp.where(causal, s[seen - rows :], NEG_FILL)
    return tail if seen == rows else jnp.concatenate([s[: seen - rows], tail], axis=0)


def attend_rows(q, keys, values, first, causal):
    q = q * BF(1.0 / math.sqrt(HD))
    values = jnp.concatenate([values, jnp.ones_like(values)], axis=1)
    outs, logs = [], []
    for mine in (first, ~first):
        s = masked_scores(keys, jnp.where(mine, q, BF(0)), causal)
        top = jnp.max(s, axis=0, keepdims=True)
        e = jnp.exp(s - top)
        logs.append(top + jnp.log(jnp.sum(e, axis=0, keepdims=True)))
        both = mm_tn(e.astype(BF), values)
        outs.append(both[:, :PAIR] / both[:, PAIR:])
    return jnp.where(first, outs[0], outs[1]).astype(BF), logs


def attend_kernel(pairs, dps, where, x_ref, vec_ref, bias_ref, *rest):
    w_refs = rest[:dps]
    n1_ref, qkv_ref, att_ref, lse_ref, w, stage, qkv, sems = rest[dps:]
    i = pl.program_id(0)
    rows = x_ref.shape[0]
    part = rows // 2

    @pl.when(i == 0)
    def _():
        settle_rows(place_rows(where, w_refs, w, stage, sems), w, stage)

    unit, _ = normalise(x_ref[...].astype(F32))
    n1 = (unit * vec_ref[0:1, :] + vec_ref[1:2, :]).astype(BF)
    n1_ref[...] = n1
    tile = (mm(n1, w[...]) + bias_ref[...]).astype(BF)
    qkv_ref[...] = tile
    qkv[pl.ds(pl.multiple_of(i * rows, rows), rows), :] = tile
    first, causal = head_masks(rows)
    for j in range(qkv.shape[0] // rows):

        @pl.when(i == j)
        def _(j=j):
            seen = (j + 1) * rows
            for g in range(pairs):
                lanes = slice(g * PAIR, (g + 1) * PAIR)
                keys = qkv[0:seen, (pairs + g) * PAIR : (pairs + g + 1) * PAIR]
                values = qkv[0:seen, (2 * pairs + g) * PAIR : (2 * pairs + g + 1) * PAIR]
                out, logs = attend_rows(qkv[j * rows : seen, lanes], keys, values, first, causal)
                for b in range(2):
                    att_ref[b, :, lanes] = out[b * part : (b + 1) * part]
                for h in range(2):
                    lse_ref[2 * g + h : 2 * g + h + 1, :] = logs[h]


def attend(where, x_all, table, bias, weights, part):
    length, model = x_all.shape
    depth, width = weights[0].shape
    dps = len(weights)
    heads = width // 3
    rows = 2 * part
    whole = lambda a: pl.BlockSpec(a.shape, lambda i: (0,) * a.ndim)
    tile = lambda cols: pl.BlockSpec((rows, cols), lambda i: (i, 0))
    return pl.pallas_call(
        functools.partial(attend_kernel, heads // PAIR, dps),
        grid=(length // rows,),
        in_specs=[SCALAR, tile(model), whole(table), whole(bias)] + [ANY] * dps,
        out_specs=[
            tile(model),
            tile(width),
            pl.BlockSpec((2, part, heads), lambda i: (i, 0, 0)),
            pl.BlockSpec((heads // HD, rows), lambda i: (0, i)),
        ],
        out_shape=[
            like((length, model)),
            like((length, width)),
            like((length // part, part, heads)),
            like((heads // HD, length), F32),
        ],
        scratch_shapes=[
            pltpu.VMEM((model, width), BF),
            pltpu.VMEM(stage_shape(dps, depth, width), BF),
            pltpu.VMEM((length, width), BF),
            pltpu.SemaphoreType.DMA((dps,)),
        ],
        compiler_params=ROOM,
    )(where, x_all, table, bias, *weights)


def attend_back_kernel(pairs, dps, where, qkv_ref, ga_ref, lse_ref, n1_hbm, *rest):
    w_refs, rest = rest[:dps], rest[dps:]
    gqkv_ref, gn1_hbm, sums_ref, norm_ref, ak, av, w, stage, n1, gn1, sems, sems2 = rest
    length = qkv_ref.shape[0]
    part = ga_ref.shape[1]
    rows = 2 * part
    copies = place_rows(where, w_refs, w, stage, sems)
    late = run_copies([(n1_hbm, n1)], sems2)
    first, causal = head_masks(rows)
    for g in range(pairs):
        lanes = slice(g * PAIR, (g + 1) * PAIR)
        k_lanes = slice((pairs + g) * PAIR, (pairs + g + 1) * PAIR)
        v_lanes = slice((2 * pairs + g) * PAIR, (2 * pairs + g + 1) * PAIR)
        ak[...] = jnp.zeros_like(ak)
        av[...] = jnp.zeros_like(av)
        for i in range(length // rows):
            here = slice(i * rows, (i + 1) * rows)
            seen = (i + 1) * rows
            q = qkv_ref[here, lanes] * BF(1.0 / math.sqrt(HD))
            ga = jnp.concatenate([ga_ref[b, :, lanes] for b in (2 * i, 2 * i + 1)], axis=0)
            keys = qkv_ref[0:seen, k_lanes]
            values = qkv_ref[0:seen, v_lanes]
            grads = []
            for h, mine in enumerate((first, ~first)):
                q_h = jnp.where(mine, q, BF(0))
                ga_h = jnp.where(mine, ga, BF(0))
                s = masked_scores(keys, q_h, causal)
                p = jnp.exp(s - lse_ref[2 * g + h : 2 * g + h + 1, here])
                gp = mm_nt(values, ga_h)
                centre = jnp.sum(p * gp, axis=0, keepdims=True)
                gs = (p * (gp - centre)).astype(BF)
                av[0:seen, :] += mm(p.astype(BF), ga_h)
                ak[0:seen, :] += mm(gs, q_h)
                grads.append(mm_tn(gs, keys))
            gqkv_ref[here, lanes] = (
                jnp.where(first, grads[0], grads[1]) * (1.0 / math.sqrt(HD))
            ).astype(BF)
        gqkv_ref[:, k_lanes] = ak[...].astype(BF)
        gqkv_ref[:, v_lanes] = av[...].astype(BF)
    settle_rows(copies, w, stage)
    wait_for(late)
    out = []
    norm_ref[...] = jnp.zeros_like(norm_ref)
    sums_ref[...] = jnp.zeros_like(sums_ref)
    for i in range(length // rows):
        here = slice(i * rows, (i + 1) * rows)
        grad = mm_nt(gqkv_ref[here, :], w[...])
        gn1[here, :] = grad.astype(BF)
        out.append(pltpu.make_async_copy(gn1.at[here, :], gn1_hbm.at[here, :], sems2.at[i]))
        out[-1].start()
        norm_ref[0:1, :] += jnp.sum(grad * n1[here, :].astype(F32), axis=0, keepdims=True)
        norm_ref[1:2, :] += jnp.sum(grad, axis=0, keepdims=True)
        sums_ref[...] += jnp.sum(gqkv_ref[here, :].astype(F32), axis=0, keepdims=True)
    wait_for(out)


def attend_back(where, qkv, grad, lse, n1, weights):
    length, width = qkv.shape
    model = n1.shape[1]
    dps = len(weights)
    depth = weights[0].shape[0]
    return pl.pallas_call(
        functools.partial(attend_back_kernel, grad.shape[2] // PAIR, dps),
        in_specs=[SCALAR, WHOLE, WHOLE, WHOLE] + [ANY] * (1 + dps),
        out_specs=[WHOLE, ANY, WHOLE, WHOLE],
        out_shape=[
            like((length, width)),
            like((length, model)),
            like((1, width), F32),
            like((2, model), F32),
        ],
        scratch_shapes=[
            pltpu.VMEM((length, PAIR), F32),
            pltpu.VMEM((length, PAIR), F32),
            pltpu.VMEM((model, width), BF),
            pltpu.VMEM(stage_shape(dps, depth, width), BF),
            pltpu.VMEM((length, model), BF),
            pltpu.VMEM((length, model), BF),
            pltpu.SemaphoreType.DMA((dps,)),
            pltpu.SemaphoreType.DMA((length // (2 * grad.shape[1]),)),
        ],
        compiler_params=ROOM,
    )(where, qkv, grad, lse, n1, *weights)


def grad_blocks_kernel(where, a_ref, g_ref, *rest):
    outs, (store, stage, sems) = rest[:-3], rest[-3:]
    g = g_ref[...]
    model = a_ref.shape[1]
    for a in range(0, model, 256):
        b = min(model, a + 256)
        store[a:b, :] = mm_tn(a_ref[:, a:b], g).astype(BF)
    wait_for(place_rows(where, outs, store, stage, sems, True))


def chunk_shapes(count, rows, cols):
    shapes = [like((rows, cols))] * count
    if can_halve(count, rows):
        shapes[3:] = [like((cut(rows), cols)), like((rows - cut(rows), cols))]
    return shapes


def grad_blocks(where, a, g, dps):
    model, width = a.shape[1], g.shape[1]
    depth = model // dps
    shapes = chunk_shapes(dps, depth, width)
    return pl.pallas_call(
        grad_blocks_kernel,
        in_specs=[SCALAR, WHOLE, WHOLE],
        out_specs=[ANY] * len(shapes),
        out_shape=shapes,
        scratch_shapes=[
            pltpu.VMEM((model, width), BF),
            pltpu.VMEM(stage_shape(dps, depth, width), BF),
            pltpu.SemaphoreType.DMA((len(shapes),)),
        ],
        compiler_params=ROOM,
    )(where, a, g)


def place_pieces(where, refs, store, sems):
    size, start = piece_rows(store.shape[0], len(refs))
    starts = [start(q) for q in range(len(refs))] + [store.shape[0]]
    least = min(b - a for a, b in zip(starts, starts[1:]))
    count = len(refs)
    copies, more = [], []
    for k, ref in enumerate(refs):
        first = start(where[0] ^ k)
        spot = pl.ds(pl.multiple_of(first, 16), least)
        copies.append(
            pltpu.make_async_copy(ref.at[pl.ds(0, least), :], store.at[spot, :], sems.at[k])
        )
        if size > least:
            spot = pl.ds(pl.multiple_of(first + least, 16), size - least)
            rest = ref.at[pl.ds(least, size - least), :]
            more.append(
                (
                    start((where[0] ^ k) + 1) - first > least,
                    pltpu.make_async_copy(rest, store.at[spot, :], sems.at[count + k]),
                )
            )
    for c in copies:
        c.start()
    for needed, c in more:
        pl.when(needed)(c.start)
    wait_for(copies)
    for needed, c in more:
        pl.when(needed)(c.wait)


def gather_fc_kernel(where, *rest):
    f_refs, (wf, stage, sems) = rest[:-3], rest[-3:]
    settle_rows(place_rows(where, f_refs, wf, stage, sems), wf, stage)


def gather_fc(where, fc):
    dps = len(fc)
    depth, width = fc[0].shape
    return pl.pallas_call(
        gather_fc_kernel,
        in_specs=[SCALAR] + [ANY] * dps,
        out_specs=WHOLE,
        out_shape=like((depth * dps, width)),
        scratch_shapes=[
            pltpu.VMEM(stage_shape(dps, depth, width), BF),
            pltpu.SemaphoreType.DMA((dps,)),
        ],
        compiler_params=ROOM,
    )(where, *fc)


def gather_proj_kernel(where, *rest):
    p_refs, (wp, sems) = rest[:-2], rest[-2:]
    place_pieces(where, p_refs, wp, sems)


def gather_proj(where, proj, ff_mine):
    dps = len(proj)
    return pl.pallas_call(
        gather_proj_kernel,
        in_specs=[SCALAR] + [ANY] * dps,
        out_specs=WHOLE,
        out_shape=like((ff_mine, proj[0].shape[1])),
        scratch_shapes=[pltpu.SemaphoreType.DMA((2 * dps,))],
        compiler_params=ROOM,
    )(where, *proj)


def feed_kernel(n2_ref, gm_ref, bias_ref, wf, wp, e_ref, gu_ref, gn2_ref, sum_ref):
    @pl.when(pl.program_id(0) == 0)
    def _():
        sum_ref[...] = jnp.zeros_like(sum_ref)

    u = mm(n2_ref[...], wf[...]) + bias_ref[...]
    ge = mm_nt(gm_ref[...], wp[...])
    value, slope = gelu_parts(u)
    e_ref[...] = value.astype(BF)
    gu = (ge * slope).astype(BF)
    gu_ref[...] = gu
    sum_ref[...] += jnp.sum(gu.astype(F32), axis=0, keepdims=True)
    gn2_ref[...] = mm_nt(gu, wf[...]).astype(BF)


def feed(n2, gm, bias, fc, proj, rows):
    length, model = n2.shape
    width = fc.shape[1]
    whole = lambda shape: pl.BlockSpec(shape, lambda i: (0,) * len(shape))
    tile = lambda cols: pl.BlockSpec((rows, cols), lambda i: (i, 0))
    return pl.pallas_call(
        feed_kernel,
        grid=(length // rows,),
        in_specs=[tile(model), tile(model), whole(bias.shape), WHOLE, WHOLE],
        out_specs=[tile(width), tile(width), tile(model), whole((1, width))],
        out_shape=[
            like((length, width)),
            like((length, width)),
            like((length, model)),
            like((1, width), F32),
        ],
        compiler_params=ROOM,
    )(n2, gm, bias, fc, proj)


def grad_proj_kernel(dps, where, gm_ref, e_ref, *rest):
    outs, (store, sems) = rest[:-2], rest[-2:]
    width = store.shape[0]
    for a in range(0, width, 256):
        b = min(width, a + 256)
        store[a:b, :] = mm_tn(e_ref[:, a:b], gm_ref[...]).astype(BF)
    _, start = piece_rows(width, dps)
    pairs = []
    for i, ref in enumerate(outs):
        first = start(where[0] ^ min(i, dps - 1))
        if i == dps:
            first = first + outs[i - 1].shape[0]
        pairs.append((store.at[pl.ds(pl.multiple_of(first, 16), ref.shape[0]), :], ref))
    wait_for(run_copies(pairs, sems))


def grad_proj(where, gm, e, dps):
    model, width = gm.shape[1], e.shape[1]
    size, _ = piece_rows(width, dps)
    shapes = chunk_shapes(dps, size, model)
    return pl.pallas_call(
        functools.partial(grad_proj_kernel, dps),
        in_specs=[SCALAR, WHOLE, WHOLE],
        out_specs=[ANY] * len(shapes),
        out_shape=shapes,
        scratch_shapes=[
            pltpu.VMEM((width, model), BF),
            pltpu.SemaphoreType.DMA((len(shapes),)),
        ],
        compiler_params=ROOM,
    )(where, gm, e)


def feed_out_kernel(e_ref, wp, out_ref):
    out_ref[...] = mm(e_ref[...], wp[...]).astype(BF)


def feed_out(e, proj, rows):
    length, width = e.shape
    model = proj.shape[1]
    return pl.pallas_call(
        feed_out_kernel,
        grid=(length // rows,),
        in_specs=[pl.BlockSpec((rows, width), lambda i: (i, 0)), WHOLE],
        out_specs=pl.BlockSpec((rows, model), lambda i: (i, 0)),
        out_shape=like((length, model)),
        compiler_params=ROOM,
    )(e, proj)


def last_kernel(gn1_ref, gr_ref, vec_ref, x_hbm, out_ref, x_ref, sem):
    copy = pltpu.make_async_copy(x_hbm, x_ref, sem)
    copy.start()
    copy.wait()
    unit, inverse = normalise(x_ref[...].astype(F32))
    grad = norm_back(gn1_ref[...].astype(F32), unit, inverse, vec_ref[0:1, :])
    out_ref[...] = (gr_ref[...] + grad).T.astype(BF)


def last_norm(gn1, x, gr, table):
    shape = like(x.shape[::-1])
    return pl.pallas_call(
        last_kernel,
        in_specs=[WHOLE] * 3 + [ANY],
        out_specs=blocks_of(shape)[0],
        out_shape=shape,
        scratch_shapes=[pltpu.VMEM(x.shape, BF), pltpu.SemaphoreType.DMA],
        compiler_params=ROOM,
    )(gn1, gr, table, x)


def output_kernel(r_ref, mlp_ref, vec_ref, out_ref):
    out = r_ref[...] + (mlp_ref[...].astype(F32) + vec_ref[7:8, :])
    out_ref[...] = out.T.astype(BF)


def output_rows(r, mlp, table):
    shape = like(r.shape[::-1])
    return pl.pallas_call(
        output_kernel,
        in_specs=[WHOLE] * 3,
        out_specs=blocks_of(shape)[0],
        out_shape=shape,
        compiler_params=ROOM,
    )(r, mlp, table)


def line_blocks(block):
    seqs = lax.axis_size("seq")
    if seqs != 8:
        others = [lax.ppermute(block, "seq", xor_perm(seqs, 2 * dz)) for dz in range(1, seqs // 2)]
        return jnp.stack([block] + others)
    _, above, far, below = gather_second(gather_first(block))
    even = (lax.axis_index("seq") // 2) % 2 == 0
    return jnp.stack([block, jnp.where(even, above, below), far, jnp.where(even, below, above)])


def block_pairs(where, places, flat, store):
    return [
        (
            ref.at[j],
            store.at[where[0] ^ places[i // 2][0], where[1] ^ (2 * (places[i // 2][1] + j) + i % 2)],
        )
        for i, ref in enumerate(flat)
        for j in range(ref.shape[0])
    ]


def head_columns(att_ref, owner):
    count = int(owner.max()) + 1
    parts = []
    for h in range(count):
        dev, slot = [int(i[0]) for i in np.where(owner == h)]
        parts.append(att_ref[dev, :, slot * HD : (slot + 1) * HD])
    return jnp.concatenate(parts, axis=1)


def block_scratch(dps, flat):
    line, depth, width = flat[0].shape
    return [
        pltpu.VMEM((dps, 2 * line, depth, width), BF),
        pltpu.SemaphoreType.DMA((dps * 2 * line + 1,)),
    ]


def out_kernel(owner, places, where, att_ref, vec_ref, x_hbm, *rest):
    flat, (r_ref, n2_ref, store, sems, x_ref) = rest[:-5], rest[-5:]
    copies = run_copies(block_pairs(where, places, flat, store) + [(x_hbm, x_ref)], sems)
    att = head_columns(att_ref, owner)
    dps, seqs, depth, width = store.shape
    wait_for(copies)
    for n in range(seqs):
        here = slice(n * width, (n + 1) * width)
        total = x_ref[:, here].astype(F32) + vec_ref[4:5, here]
        for p in range(dps):
            total = total + mm(att[:, p * depth : (p + 1) * depth], store[p, n])
        r_ref[:, here] = total
    unit, _ = normalise(r_ref[...])
    n2_ref[...] = (unit * vec_ref[5:6, :] + vec_ref[6:7, :]).astype(BF)


def out_project(where, att, x, table, places, flat, owner):
    dps = max(k for k, _ in places) + 1
    return pl.pallas_call(
        functools.partial(out_kernel, owner, places),
        in_specs=[SCALAR, WHOLE, WHOLE, ANY] + [ANY] * len(flat),
        out_specs=blocks_of(x, x),
        out_shape=[like(x.shape, F32), like(x.shape)],
        scratch_shapes=block_scratch(dps, flat) + [pltpu.VMEM(x.shape, BF)],
        compiler_params=ROOM,
    )(where, att, table, x, *flat)


def back_kernel(owner, places, where, gn2_ref, r_ref, vec_ref, g_hbm, *rest):
    flat = rest[:-7]
    gr_ref, go_ref, ga_ref, sums_ref, store, sems, g_ref = rest[-7:]
    copies = run_copies([(g_hbm, g_ref)] + block_pairs(where, places, flat, store), sems)
    copies[0].wait()
    dps, seqs, depth, width = store.shape
    gn2 = gn2_ref[...].astype(F32)
    unit, inverse = normalise(r_ref[...])
    gr = g_ref[...].astype(F32) + norm_back(gn2, unit, inverse, vec_ref[5:6, :])
    go = gr.astype(BF)
    gr_ref[...] = gr
    go_ref[...] = go
    sums_ref[0:1, :] = jnp.sum(go.astype(F32), axis=0, keepdims=True)
    sums_ref[1:2, :] = jnp.sum(gn2 * unit, axis=0, keepdims=True)
    sums_ref[2:3, :] = jnp.sum(gn2, axis=0, keepdims=True)
    sums_ref[3:4, :] = jnp.sum(g_ref[...].astype(F32), axis=0, keepdims=True)
    wait_for(copies[1:])
    found = []
    for p in range(dps):
        total = mm_nt(go[:, 0:width], store[p, 0])
        for n in range(1, seqs):
            total = total + mm_nt(go[:, n * width : (n + 1) * width], store[p, n])
        found.append(total)
    ga = jnp.concatenate(found, axis=1).astype(BF)
    ga_ref[...] = jnp.zeros_like(ga_ref)
    for h in range(int(owner.max()) + 1):
        dev, slot = [int(i[0]) for i in np.where(owner == h)]
        ga_ref[dev, :, slot * HD : (slot + 1) * HD] = ga[:, h * HD : (h + 1) * HD]


def out_back(where, gn2, r, g, table, places, flat, owner):
    dps = max(k for k, _ in places) + 1
    shapes = [
        like(r.shape, F32),
        like(r.shape),
        like((owner.shape[0], r.shape[0], owner.shape[1] * HD)),
        like((4, r.shape[1]), F32),
    ]
    return pl.pallas_call(
        functools.partial(back_kernel, owner, places),
        in_specs=[SCALAR, WHOLE, WHOLE, WHOLE, ANY] + [ANY] * len(flat),
        out_specs=blocks_of(*shapes),
        out_shape=shapes,
        scratch_shapes=block_scratch(dps, flat) + [pltpu.VMEM(g.shape, BF)],
        compiler_params=ROOM,
    )(where, gn2, r, table, g, *flat)


def grad_out_kernel(owner, where, att_ref, far_att_ref, go_ref, far_go_ref, *rest):
    outs, (store, sems) = rest[:-2], rest[-2:]
    att = jnp.concatenate([head_columns(r, owner) for r in (att_ref, far_att_ref)], axis=0)
    go = jnp.concatenate([go_ref[...], far_go_ref[...]], axis=0)
    dps, line, depth, width = store.shape
    even = where[1] % 2 == 0
    for z in range(line):
        a, b = 2 * z * width, (2 * z + 1) * width
        cols = jnp.where(even, go[:, a : a + width], go[:, b : b + width])
        for p in range(dps):
            store[p, z] = mm_tn(att[:, p * depth : (p + 1) * depth], cols).astype(BF)
    pairs = [
        (store.at[where[0] ^ k, (where[1] // 2) ^ dz], ref.at[dz])
        for k, ref in enumerate(outs)
        for dz in range(line)
    ]
    wait_for(run_copies(pairs, sems))


def grad_out(where, att, far_att, go, far_go, dps, owner):
    seqs = att.shape[0]
    line, depth, width = seqs // 2, go.shape[1] // dps, go.shape[1] // seqs
    return pl.pallas_call(
        functools.partial(grad_out_kernel, owner),
        in_specs=[SCALAR] + [WHOLE] * 4,
        out_specs=[ANY] * dps,
        out_shape=[like((line, depth, width))] * dps,
        scratch_shapes=[
            pltpu.VMEM((dps, line, depth, width), BF),
            pltpu.SemaphoreType.DMA((dps * line,)),
        ],
        compiler_params=ROOM,
    )(where, att, far_att, go, far_go)


def body(tokens, w_qkv, w_out, vectors, w_fc, b_fc, w_proj, cotangent):
    dps = lax.axis_size("dp")
    seqs = lax.axis_size("seq")
    dp = lax.axis_index("dp")
    sq = lax.axis_index("seq")
    rows, model = tokens.shape
    head_count = model // HD
    slots, owner, wide, send, recv = head_plan(head_count, seqs, w_qkv.shape[1])
    send = jnp.asarray(send)[:, :, None, :]
    recv = jnp.asarray(recv)[:, :, None, :]
    mine = slots * HD
    ff_mine = w_fc.shape[1]
    ratio = seqs // dps
    col = w_proj.shape[1]
    where = jnp.stack([dp, sq]).astype(jnp.int32)
    per, wide_vec = vectors.shape
    own_heads = jnp.asarray(owner)[sq]
    pick = (own_heads[:, None] == jnp.arange(head_count)[None, :]).astype(F32)

    def head_rows(vector):
        return jnp.sum(pick[:, :, None] * vector.reshape(1, head_count, HD), axis=1).reshape(-1)

    def head_spread(vector):
        return jnp.sum(pick[:, :, None] * vector.reshape(slots, 1, HD), axis=0).reshape(-1)

    near, far = near_far(dps)
    copies = lambda block: {k: block for k in range(dps)}
    chunks = lambda blocks: dict(enumerate(blocks))

    lanes = send.shape[3]
    gm_all = lax.all_gather(cotangent, "seq", axis=0, tiled=True)
    small = jnp.concatenate([vectors.reshape(-1), b_fc])
    count = small.shape[0]
    small = jnp.stack(in_order(small, send_rel(copies(small), "dp", near + far)))
    small = as_rows(small.reshape(1, -1), lanes)[0]
    parts = exchange(pack_columns(where, w_qkv, send, small))
    wf = in_order(w_fc, send_rel(copies(w_fc), "dp", near + far))
    pieces = proj_pieces(where, w_proj.reshape(ratio, ff_mine, col), dps)
    parts, wf, x_own, out_own, pieces, gm_all = phase(
        parts, wf, tokens, w_out, pieces, gm_all
    )

    x_all = lax.all_gather(x_own, "seq", axis=0, tiled=True)
    own_qkv = unpack_columns(where, parts, recv, w_qkv.shape[0], 3 * mine)
    wq = in_order(own_qkv, send_rel(copies(own_qkv), "dp", near + far))
    line = line_blocks(out_own)
    pieces = in_order(pieces[0], send_rel(chunks(pieces), "dp", near + far))
    pieces = turn_pieces(where, pieces)
    small = parts[:, w_qkv.shape[0] :].reshape(seqs, -1)[:, : dps * count].astype(F32)
    small = jnp.take(small.reshape(seqs, dps, count), dp ^ jnp.arange(dps), axis=1)
    table = small[:, :, : per * wide_vec].reshape(seqs, dps, per, wide_vec)
    table = table.transpose(1, 2, 0, 3).reshape(dps * per, model)
    bias_fc = small[:, :, per * wide_vec :].transpose(1, 0, 2).reshape(-1)
    bias_fc = lax.dynamic_slice_in_dim(bias_fc, sq * ff_mine, ff_mine)[None]
    bias_qkv = jnp.concatenate(
        [head_rows(table[2]), jnp.zeros((mine,), F32), head_rows(table[3])]
    )[None]
    x_all, wq, line, pieces, table, bias_qkv = phase(x_all, wq, line, pieces, table, bias_qkv)

    pieces = exchange(pieces)
    wo = {(0, 0): line}
    wo.update({(k, 0): b for k, b in send_rel(copies(line), "dp", near).items()})
    n1_all, qkv, att, lse = attend(where, x_all, table, bias_qkv, wq, rows)
    att, wo, pieces = phase(att, wo, pieces)

    att = exchange(att)
    wo_other = {place: swap_core(b) for place, b in wo.items()}
    found = gather_far(wo, far)
    wo.update(found)
    own_proj = join_columns(pieces)
    att, wo, wo_other, own_proj = phase(att, wo, wo_other, own_proj)
    wo_other.update({place: swap_core(wo[place]) for place in found})
    wp_near = send_rel(copies(own_proj), "dp", near)
    places = sorted(wo)
    flat = [b for place in places for b in (wo[place], wo_other[place])]
    r, n2 = out_project(where, att, x_own, table, places, flat, owner)
    n2, att, own_proj = phase(n2, att, own_proj)

    n2_all = lax.all_gather(n2, "seq", axis=0, tiled=True)
    wp = in_order(own_proj, wp_near, send_rel(copies(own_proj), "dp", far))
    far_att = swap_core(att)
    wf = gather_fc(where, wf)
    wf, wp = phase(wf, wp)
    wp = gather_proj(where, wp, ff_mine)
    n2_all, wp, far_att = phase(n2_all, wp, far_att)
    e, gu, gn2_part, sum_fc = feed(n2_all, gm_all, bias_fc, wf, wp, 2 * rows)

    gn2 = lax.psum_scatter(gn2_part, "seq", scatter_dimension=0, tiled=True)
    d_proj = grad_proj(where, gm_all, e, dps)
    proj_first = reduce_first(d_proj)
    d_fc = grad_blocks(where, n2_all, gu, dps)
    d_fc, proj_first, e_late = phase(d_fc, proj_first, e)
    proj_in = reduce_second(d_proj, proj_first)
    mlp = feed_out(e_late, wp, 2 * rows)
    gn2, d_fc, mlp, proj_in = phase(gn2, d_fc, mlp, proj_in)

    mlp = lax.psum_scatter(mlp, "seq", scatter_dimension=0, tiled=True)
    gr, go, ga, sums_two = out_back(where, gn2, r, cotangent, table, places, flat, owner)
    fc_first = reduce_first(d_fc)
    ga, go, fc_first = phase(ga, go, fc_first)

    ga = exchange(ga)
    d_out = split_far(grad_out(where, att, far_att, go, swap_core(go), dps, owner))
    g_proj = split_columns(proj_in, seqs)
    fc_in = reduce_second(d_fc, fc_first)
    ga, d_out, fc_in, g_proj = phase(ga, d_out, fc_in, g_proj)

    out_first = reduce_first(d_out)
    g_proj = exchange(g_proj)
    gqkv, gn1_part, gqkv_sums, norm_sums = attend_back(where, qkv, ga, lse, n1_all, wq)
    gn1_part, gqkv, mlp, g_proj, d_out, out_first = phase(
        gn1_part, gqkv, mlp, g_proj, d_out, out_first
    )

    gn1 = lax.psum_scatter(gn1_part, "seq", scatter_dimension=0, tiled=True)
    out_in = reduce_second(d_out, out_first)
    d_qkv = grad_blocks(where, n1_all, gqkv, dps)
    d_qkv, out_in = phase(d_qkv, out_in)
    qkv_first = reduce_first(d_qkv)
    g_line = total_of(out_in).astype(BF)
    if seqs == 8:
        even = (sq // 2) % 2 == 0
        above = jnp.where(even, g_line[1], g_line[3])
        below = jnp.where(even, g_line[3], g_line[1])
        line_out = [g_line[0], above, g_line[2], below]
    else:
        line_out = [
            lax.dynamic_index_in_dim(
                g_line, ((sq // 2 + off) % (seqs // 2)) ^ (sq // 2), 0, keepdims=False
            )
            for off in range(seqs // 2)
        ]
    out_in = scatter_second(line_out, scatter_first(line_out))
    qkv_in = reduce_second(d_qkv, qkv_first)
    activations = output_rows(r, mlp, table)
    g_fc = total_of(fc_in)
    g_proj = {
        k: lax.dynamic_slice_in_dim(g_proj, (dp ^ k) * ratio, ratio, axis=0) for k in range(dps)
    }
    g_proj = in_order(g_proj[0], send_rel(g_proj, "dp", near + far))
    g_proj = proj_rows(where, g_proj, ff_mine)
    vector_grads = jnp.concatenate(
        [
            ((norm_sums[0] - table[1] * norm_sums[1]) / table[0])[None],
            norm_sums[1:],
            head_spread(gqkv_sums[0, :mine])[None],
            head_spread(gqkv_sums[0, 2 * mine :])[None],
            sums_two,
        ]
    )
    fc_sums = lax.dynamic_update_slice_in_dim(
        jnp.zeros((dps * seqs * b_fc.shape[0],), F32), sum_fc[0], sq * ff_mine, axis=0
    )
    sums = jnp.concatenate(
        [
            vector_grads.reshape(dps, per, seqs, wide_vec).transpose(0, 2, 1, 3).reshape(
                dps, seqs, per * wide_vec
            ),
            fc_sums.reshape(dps, seqs, -1),
        ],
        axis=2,
    )
    sums = as_rows(sums.transpose(1, 0, 2).reshape(seqs, -1).astype(BF), lanes)
    qkv_in, sums, activations, g_fc, out_in = phase(qkv_in, sums, activations, g_fc, out_in)
    g_out = total_of(out_in)

    parts = exchange(repack_columns(where, qkv_in, recv, sums))
    input_grad = last_norm(gn1, x_own, gr, table)
    parts, input_grad, g_proj, g_out = phase(parts, input_grad, g_proj, g_out)
    g_qkv = restore_columns(where, parts, send, *w_qkv.shape)
    sums = parts[:, w_qkv.shape[0] :].reshape(seqs, -1)[:, : dps * count].astype(F32)
    sums = sums.sum(axis=0).reshape(dps, count)
    sums = {k: lax.dynamic_index_in_dim(sums, dp ^ k, 0, keepdims=False) for k in range(dps)}
    sums = total_of(in_order(sums[0], send_rel(sums, "dp", near + far)))
    return (
        activations.T,
        input_grad.T,
        g_qkv,
        g_out,
        sums[: per * wide_vec].reshape(per, wide_vec),
        g_fc,
        sums[per * wide_vec :],
        g_proj.T,
    )


def solution(mesh):
    rows = P(("dp", "seq"), None)
    grid = P("dp", "seq")
    line = P(("dp", "seq"))
    return jax.shard_map(
        body,
        mesh=mesh,
        in_specs=(rows, grid, grid, grid, grid, line, grid, rows),
        out_specs=(rows, rows, grid, grid, grid, grid, line, grid),
        check_vma=False,
    )
```
